32 devices in a mesh: tm: 8 (over z, y), src: 4 (over x, core).
Axes of the slice: x: 2, y: 2, z: 4, core: 2. Of those that a mesh axis runs over, the one named last changes fastest.
Arguments:
- mix_in: float32 [32768, 128], P('tm')
- skip_in: float32 [32768, 128], P('tm'), may hold values from -6 to 6
- encoded: float32 [32768, 512], P('tm'), may hold values from 0.1 to 3
- lengths: int32 [5], replicated, may hold values from 3999 to 8772, as said below
- w_in: float32 [128, 512], P(None, 'src'), may hold values from -0.5 to 0.5
- b_in: float32 [512], P('src'), may hold values from -3 to 3
- slope_in: float32 [512], P('src'), may hold values from 0.05 to 0.5
- gain_in: float32 [512], P('src'), may hold values from 0.25 to 1.75
- beta_in: float32 [512], P('src'), may hold values from -3 to 3
- w_depth: float32 [3, 512], P(None, 'src'), may hold values from -3 to 3
- b_depth: float32 [512], P('src'), may hold values from -3 to 3
- slope_mid: float32 [512], P('src'), may hold values from 0.05 to 0.5
- gain_mid: float32 [512], P('src'), may hold values from 0.25 to 1.75
- beta_mid: float32 [512], P('src'), may hold values from -3 to 3
- w_out: float32 [512, 256], P('src'), may hold values from -0.25 to 0.25
- b_out: float32 [256], replicated, may hold values from -3 to 3
- slope_skip: float32 [128], replicated, may hold values from 0.05 to 0.5
- w_mask: float32 [128, 1024], P(None, 'src'), may hold values from -0.5 to 0.5
- b_mask: float32 [1024], P('src'), may hold values from -3 to 3
- basis: float32 [512, 16], replicated, may hold values from -0.25 to 0.25
- cot_out: float32 [32768, 128], P('tm'), may hold values from -6 to 6
- cot_wave: float32 [2, 262144], P(None, 'tm'), may hold values from -6 to 6
Outputs:
- block_out: float32 [32768, 128], P('tm')
- wave: float32 [2, 262144], P(None, 'tm')
- grad_mix_in: float32 [32768, 128], P('tm')
- grad_skip_in: float32 [32768, 128], P('tm')
- grad_encoded: float32 [32768, 512], P('tm')
- grad_w_in: float32 [128, 512], P(None, 'src')
- grad_b_in: float32 [512], P('src')
- grad_slope_in: float32 [512], P('src')
- grad_gain_in: float32 [512], P('src')
- grad_beta_in: float32 [512], P('src')
- grad_w_depth: float32 [3, 512], P(None, 'src')
- grad_b_depth: float32 [512], P('src')
- grad_slope_mid: float32 [512], P('src')
- grad_gain_mid: float32 [512], P('src')
- grad_beta_mid: float32 [512], P('src')
- grad_w_out: float32 [512, 256], P('src')
- grad_b_out: float32 [256], replicated
- grad_slope_skip: float32 [128], replicated
- grad_w_mask: float32 [128, 1024], P(None, 'src')
- grad_b_mask: float32 [1024], P('src')
- grad_basis: float32 [512, 16], replicated
The draws below stay inside these ranges and needn't reach their ends.
Inputs may be any that keep to these rules, and one draw needn't show every extreme that they name: The 5 items are 2 items of 3999 frames, 2 items of 7999 frames and one item of the remaining frames, in an order drawn from the seed; the lengths sum to 32768.
All inputs are finite; a program needn't handle non-finite values.
Results may differ from the reference program's by a relative error of at most 0.0003.
Values sent between devices are 32-bit elements; how exact they have to be, the bound alone decides.
No kernel may reach another device: no remote copies, remote signals or barrier semaphores. Data moves between devices by JAX's collectives and lax.ppermute only.
A program may use at most 128 MiB of HBM per device.

```python
import math
import jax
import jax.numpy as jnp
from jax import lax

N = 512
L = 16
B = 128
HIDDEN_WIDTH = 512
SC = 128
P_SIZE = 3
DILATION_STEP = 128
SHORT_LEN = 3999
LONG_LEN = 7999
FRAMES = 32768
PAIRS = 2
ITEMS = 5


def draw_mix_in(key, part):
    frame_slots = jnp.arange(FRAMES, dtype=jnp.float32)
    rising = jnp.exp(jnp.log(3.0) * frame_slots / FRAMES)[:, None]
    return jax.random.normal(key, (FRAMES, B), jnp.float32) * rising * 0.7


def draw_lengths(key, part):
    remaining = FRAMES - PAIRS * (SHORT_LEN + LONG_LEN)
    shorts = jnp.full((PAIRS,), SHORT_LEN, jnp.int32)
    longs = jnp.full((PAIRS,), LONG_LEN, jnp.int32)
    last_item = jnp.full((1,), remaining, jnp.int32)
    pieces = jnp.concatenate([shorts, longs, last_item]).astype(jnp.int32)
    order = jax.random.permutation(jax.random.fold_in(key, 17), ITEMS)
    return pieces[order].astype(jnp.int32)


def block_levels(rng, dims, cuts, smallest, top_value):
    level, own = 1.0, jax.random.fold_in(rng, 6)
    for dim, blocks in cuts:
        draws = jnp.exp(jax.random.uniform(jax.random.fold_in(own, dim), (blocks,), jnp.float32, smallest / len(cuts), top_value / len(cuts)))
        level = level * jnp.repeat(draws, dims[dim] // blocks).reshape([-1 if axis == dim else 1 for axis in range(len(dims))])
    return level


def bell_draw(key, dims, spread, most, cuts=(), kind=jnp.bfloat16):
    values = spread * jax.random.normal(key, dims, jnp.float32)
    if cuts:
        values = values * block_levels(key, dims, cuts, -0.22, 0.18)
    return jnp.clip(values, -most, most).astype(kind)


def setup_inputs(seed: int = 0) -> dict:
    keys = jax.random.split(jax.random.key(seed), 23)
    mix_in = draw_mix_in(jax.random.fold_in(keys[22], 71), 0)
    skip_in = bell_draw(keys[1], (FRAMES, SC), 1.0, 6.0, ((0, 8),), jnp.float32)
    encoded = jnp.clip(jnp.exp(math.log(3.0) - 3.4011974 * jax.random.uniform(keys[2], (FRAMES, N), jnp.float32) ** block_levels(keys[2], (FRAMES, N), ((0, 8),), -0.2, 0.2)), 0.1, 3.0)
    lengths = draw_lengths(jax.random.fold_in(keys[22], 71), 0)
    w_in = bell_draw(keys[4], (B, HIDDEN_WIDTH), B ** -0.5, 0.5, ((1, 4),), jnp.float32)
    b_in = bell_draw(keys[5], (HIDDEN_WIDTH,), 0.3, 3.0, ((0, 4),), jnp.float32)
    slope_in = jnp.clip(0.05 + 0.45 * jax.random.uniform(keys[6], (HIDDEN_WIDTH,), jnp.float32) ** block_levels(keys[6], (HIDDEN_WIDTH,), ((0, 4),), -0.2, 0.2), 0.05, 0.5)
    gain_in = jnp.clip(1.0 + 0.15 * jax.random.normal(keys[7], (HIDDEN_WIDTH,), jnp.float32), 0.25, 1.75)
    beta_in = bell_draw(keys[8], (HIDDEN_WIDTH,), 0.3, 3.0, ((0, 4),), jnp.float32)
    w_depth = bell_draw(keys[9], (P_SIZE, HIDDEN_WIDTH), 0.6, 3.0, ((1, 4),), jnp.float32)
    b_depth = bell_draw(keys[10], (HIDDEN_WIDTH,), 0.3, 3.0, ((0, 4),), jnp.float32)
    slope_mid = jnp.clip(0.05 + 0.45 * jax.random.uniform(keys[11], (HIDDEN_WIDTH,), jnp.float32) ** block_levels(keys[11], (HIDDEN_WIDTH,), ((0, 4),), -0.2, 0.2), 0.05, 0.5)
    gain_mid = jnp.clip(1.0 + 0.15 * jax.random.normal(keys[12], (HIDDEN_WIDTH,), jnp.float32), 0.25, 1.75)
    beta_mid = bell_draw(keys[13], (HIDDEN_WIDTH,), 0.3, 3.0, ((0, 4),), jnp.float32)
    w_out = bell_draw(keys[14], (HIDDEN_WIDTH, B + SC), HIDDEN_WIDTH ** -0.5, 0.25, ((0, 4),), jnp.float32)
    b_out = bell_draw(keys[15], (B + SC,), 0.3, 3.0, (), jnp.float32)
    slope_skip = jnp.clip(jax.random.uniform(keys[16], (SC,), jnp.float32, 0.05, 0.5), 0.05, 0.5)
    w_mask = bell_draw(keys[17], (SC, 2 * N), SC ** -0.5, 0.5, ((1, 4),), jnp.float32)
    b_mask = bell_draw(keys[18], (2 * N,), 0.5, 3.0, ((0, 4),), jnp.float32)
    basis = bell_draw(keys[19], (N, L), N ** -0.5, 0.25, (), jnp.float32)
    cot_out = bell_draw(keys[20], (FRAMES, B), 1.0, 6.0, ((0, 8),), jnp.float32)
    cot_wave = bell_draw(keys[21], (2, FRAMES * (L // 2)), 1.0, 6.0, ((1, 8),), jnp.float32)
    return dict(mix_in=mix_in, skip_in=skip_in, encoded=encoded, lengths=lengths, w_in=w_in, b_in=b_in, slope_in=slope_in, gain_in=gain_in, beta_in=beta_in, w_depth=w_depth, b_depth=b_depth, slope_mid=slope_mid, gain_mid=gain_mid, beta_mid=beta_mid, w_out=w_out, b_out=b_out, slope_skip=slope_skip, w_mask=w_mask, b_mask=b_mask, basis=basis, cot_out=cot_out, cot_wave=cot_wave)


epsilon = 1e-05

@jax.custom_vjp
def low(v):
    return lax.optimization_barrier(v.astype(jnp.bfloat16)).astype(jnp.float32)

@jax.custom_vjp
def low_back(v):
    return v

def low_keep(v):
    return (low(v), None)

def low_pass(kept, grad):
    return (grad,)

def back_keep(v):
    return (v, None)

def back_low(kept, grad):
    return (low(grad),)
low.defvjp(low_keep, low_pass)
low_back.defvjp(back_keep, back_low)

def product(matrix, weights):
    return jnp.dot(matrix, weights, precision=lax.Precision.HIGHEST, preferred_element_type=jnp.float32)

def param_silu(value_entries, slopes):
    return slopes * value_entries + (1.0 - slopes) * jax.nn.silu(value_entries)

def item_lookup_tables(lengths, frame_slots, spacing):
    item_ends = jnp.cumsum(lengths, dtype=jnp.int32)
    item_starts = item_ends - lengths

    def item_of(places):
        return lax.optimization_barrier(jnp.sum((places[:, None] >= item_ends[None, :]).astype(jnp.int32), axis=1))
    item_ids = item_of(frame_slots)
    indicator_matrix = ((frame_slots[:, None] >= item_starts[None, :]) & (frame_slots[:, None] < item_ends[None, :])).astype(jnp.float32)
    lower_matches_item = ((frame_slots >= spacing) & (item_of(frame_slots - spacing) == item_ids)).astype(jnp.float32)
    upper_matches_item = (item_of(frame_slots + spacing) == item_ids).astype(jnp.float32)
    preceding_matches_item = ((frame_slots >= 1) & (item_of(frame_slots - 1) == item_ids)).astype(jnp.float32)
    following_matches_item = (item_of(frame_slots + 1) == item_ids).astype(jnp.float32)
    return (indicator_matrix, lower_matches_item, upper_matches_item, preceding_matches_item, following_matches_item)

def group_norm(value_entries, norm_gain, norm_bias, indicator_matrix, counts):
    totals = jnp.dot(lax.optimization_barrier(jnp.sum(value_entries, axis=1)), indicator_matrix, precision=lax.Precision.HIGHEST)
    means = totals / counts
    centered = value_entries - product(indicator_matrix, means[:, None])
    squares = jnp.dot(lax.optimization_barrier(jnp.sum(centered * centered, axis=1)), indicator_matrix, precision=lax.Precision.HIGHEST)
    inv_rows = product(indicator_matrix, lax.rsqrt(squares / counts + epsilon)[:, None])
    return centered * inv_rows * norm_gain + norm_bias

def reference(mix_in, skip_in, encoded, lengths, w_in, b_in, slope_in, gain_in, beta_in, w_depth, b_depth, slope_mid, gain_mid, beta_mid, w_out, b_out, slope_skip, w_mask, b_mask, basis, cot_out, cot_wave):
    frame_slots = jnp.arange(FRAMES, dtype=jnp.int32)
    indicator_matrix, lower_matches_item, upper_matches_item, preceding_matches_item, following_matches_item = item_lookup_tables(lengths, frame_slots, DILATION_STEP)
    counts = lengths.astype(jnp.float32) * HIDDEN_WIDTH
    stride = L // 2

    def forward(mix_in, skip_in, encoded, w_in, b_in, slope_in, gain_in, beta_in, w_depth, b_depth, slope_mid, gain_mid, beta_mid, w_out, b_out, slope_skip, w_mask, b_mask, basis):
        hidden_in = product(mix_in, w_in) + b_in
        input_norm = group_norm(param_silu(hidden_in, slope_in), gain_in, beta_in, indicator_matrix, counts)
        empty_rows = jnp.zeros((DILATION_STEP, HIDDEN_WIDTH), jnp.float32)
        lower_neighbor = jnp.concatenate([empty_rows, input_norm[:-DILATION_STEP]], axis=0) * lower_matches_item[:, None]
        upper_neighbor = jnp.concatenate([input_norm[DILATION_STEP:], empty_rows], axis=0) * upper_matches_item[:, None]
        depth_out = w_depth[0] * lower_neighbor + w_depth[1] * input_norm + w_depth[2] * upper_neighbor + b_depth
        norm_mid = group_norm(param_silu(depth_out, slope_mid), gain_mid, beta_mid, indicator_matrix, counts)
        branch = product(norm_mid, w_out) + b_out
        block_out = mix_in + branch[:, :B]
        skip_total = skip_in + branch[:, B:]
        mask = jax.nn.sigmoid(product(param_silu(skip_total, slope_skip), w_mask) + b_mask)
        masked = mask.reshape(FRAMES, 2, N) * encoded[:, None, :]
        decoded = jnp.einsum('fcn,nk->cfk', masked, basis, precision=lax.Precision.HIGHEST)
        tails = jnp.concatenate([jnp.zeros((2, 1, stride), jnp.float32), decoded[:, :-1, stride:]], axis=1) * preceding_matches_item[None, :, None]
        wave = (decoded[:, :, :stride] + tails).reshape(2, FRAMES * stride)
        return (block_out, wave)
    outputs, pullback = jax.vjp(forward, mix_in, skip_in, encoded, w_in, b_in, slope_in, gain_in, beta_in, w_depth, b_depth, slope_mid, gain_mid, beta_mid, w_out, b_out, slope_skip, w_mask, b_mask, basis)
    grad_mix_in, grad_skip_in, grad_encoded, grad_w_in, grad_b_in, grad_slope_in, grad_gain_in, grad_beta_in, grad_w_depth, grad_b_depth, grad_slope_mid, grad_gain_mid, grad_beta_mid, grad_w_out, grad_b_out, grad_slope_skip, grad_w_mask, grad_b_mask, grad_basis = pullback((cot_out, cot_wave))
    return (outputs[0], outputs[1], grad_mix_in, grad_skip_in, grad_encoded, grad_w_in, grad_b_in, grad_slope_in, grad_gain_in, grad_beta_in, grad_w_depth, grad_b_depth, grad_slope_mid, grad_gain_mid, grad_beta_mid, grad_w_out, grad_b_out, grad_slope_skip, grad_w_mask, grad_b_mask, grad_basis)
```

```python
import functools

import jax
import jax.numpy as jnp
from jax import lax
from jax.experimental import pallas as pl
from jax.experimental.pallas import tpu as pltpu
from jax.sharding import PartitionSpec as P

L = 16
STRIDE = L // 2
HIDDEN = 512
STEP = 128
EPS = 1e-05
T = 256
T1 = 512
LANES = 128
F32 = jnp.float32
BF16 = jnp.bfloat16
NVEC = 16
PACK_IN = 128 + NVEC


def split(x):
    hi = x.astype(BF16)
    return hi, (x - hi.astype(F32)).astype(BF16)


def mm(a, b):
    return lax.dot_general(a, b, (((1,), (0,)), ((), ())), preferred_element_type=F32)


def mm_tn(a, b):
    return lax.dot_general(a, b, (((0,), (0,)), ((), ())), preferred_element_type=F32)


def mm_nt(a, b):
    return lax.dot_general(a, b, (((1,), (1,)), ((), ())), preferred_element_type=F32)


def cat(parts, axis):
    return jnp.concatenate(parts, axis=axis)


def iota(shape, axis):
    return lax.broadcasted_iota(jnp.int32, shape, axis)


def sigmoid(x):
    return 1.0 / (1.0 + jnp.exp(-x))


def colsum(x):
    return jnp.sum(x, axis=0, keepdims=True)


def boundary(pos_ref, items, start):
    ahead = jnp.where(start - STEP >= 0, 0, -1)
    edge = jnp.int32(0)
    for k in range(items):
        end = pos_ref[3 + k]
        passed = end <= start - STEP
        ahead = ahead + passed.astype(jnp.int32)
    for k in range(items):
        edge = jnp.where(ahead == k, pos_ref[3 + k], edge)
    return edge, ahead


def item_rows(ahead, items):
    return jnp.maximum(ahead, 0), jnp.minimum(ahead + 1, items - 1)


def lane_items(ahead, items):
    lane = iota((1, LANES), 1)
    return (lane == ahead).astype(F32), (lane == ahead + 1).astype(F32)


def put_statistics(msg_ref, sums, squares, counts, onehot):
    groups = sums.shape[0]
    count = counts[:, :1]
    safe = jnp.maximum(count, 1.0)
    total = jnp.sum(sum(sums[g] for g in range(groups)), axis=1, keepdims=True)
    number = count * (groups * LANES)
    mean = total / jnp.maximum(number, 1.0)
    spread = 0.0
    for g in range(groups):
        away = sums[g] / safe - mean
        spread = spread + squares[g] + count * away * away
    spread = jnp.sum(spread, axis=1, keepdims=True)
    item_sum = colsum(onehot * total)
    item_number = colsum(onehot * number)
    item_mean = item_sum / jnp.maximum(item_number, 1.0)
    away = mean - item_mean
    item_spread = colsum(onehot * (spread + number * away * away))
    msg = cat(
        [item_sum, item_spread, item_number, item_mean, jnp.zeros((4, LANES), F32)], 0
    )
    for i in range(msg_ref.shape[0]):
        msg_ref[i] = msg


def to_rows(row, items_padded):
    wide = jnp.broadcast_to(row, (items_padded, LANES))
    own = iota((items_padded, LANES), 0) == iota((items_padded, LANES), 1)
    column = jnp.sum(jnp.where(own, wide, 0.0), axis=1, keepdims=True)
    return jnp.broadcast_to(column, (items_padded, HIDDEN))


def merge_statistics(msg_ref, table_ref):
    msg = msg_ref[...]
    item_sum = jnp.sum(msg[:, 0:1, :], axis=0)
    number = jnp.sum(msg[:, 2:3, :], axis=0)
    mean = item_sum / jnp.maximum(number, 1.0)
    away = msg[:, 3:4, :] - mean[None]
    squares = jnp.sum(msg[:, 1:2, :] + msg[:, 2:3, :] * away * away, axis=0)
    inverse = lax.rsqrt(squares / jnp.maximum(number, 1.0) + EPS)
    padded = table_ref.shape[1]
    table_ref[0] = to_rows(mean, padded)
    table_ref[1] = to_rows(inverse, padded)


def two_part_statistics(act, after, before, counts, sums_ref, squares_ref, counts_ref, onehot_ref, entry, ahead):
    n_before, n_after = counts
    groups = sums_ref.shape[0]
    sum_b = colsum(jnp.where(before, act, 0.0))
    sum_a = colsum(jnp.where(after, act, 0.0))
    mean_b = sum_b / jnp.maximum(n_before, 1.0)
    mean_a = sum_a / jnp.maximum(n_after, 1.0)
    dev = act - jnp.where(after, mean_a, mean_b)
    dev = dev * dev
    sq_b = colsum(jnp.where(before, dev, 0.0))
    sq_a = colsum(jnp.where(after, dev, 0.0))
    for g in range(groups):
        cut = slice(g * LANES, (g + 1) * LANES)
        sums_ref[g, pl.ds(2 * entry, 1), :] = sum_b[:, cut]
        sums_ref[g, pl.ds(2 * entry + 1, 1), :] = sum_a[:, cut]
        squares_ref[g, pl.ds(2 * entry, 1), :] = sq_b[:, cut]
        squares_ref[g, pl.ds(2 * entry + 1, 1), :] = sq_a[:, cut]
    counts_ref[pl.ds(2 * entry, 1), :] = jnp.full((1, LANES), n_before, F32)
    counts_ref[pl.ds(2 * entry + 1, 1), :] = jnp.full((1, LANES), n_after, F32)
    hot_b, hot_a = lane_items(ahead, 0)
    onehot_ref[pl.ds(2 * entry, 1), :] = hot_b
    onehot_ref[pl.ds(2 * entry + 1, 1), :] = hot_a


def first_kernel(items, pos_ref, mix_ref, w_ref, b_ref, slope_ref, msg_ref, sums, squares, counts, onehot):
    j = pl.program_id(0)
    start = pos_ref[0] + j * T1
    edge, ahead = boundary(pos_ref, items, start)
    m_hi, m_lo = split(mix_ref[...])
    w_hi, w_lo = split(w_ref[...])
    hidden = mm(cat([m_hi, m_lo], 1), cat([w_hi, w_hi], 0)) + mm(m_hi, w_lo) + b_ref[...]
    slope = slope_ref[...]
    act = hidden * (slope + (1.0 - slope) * sigmoid(hidden))
    offset = iota((T1, LANES), 0) + (start - edge)
    n_before = jnp.clip(edge - start, 0, T1).astype(F32)
    two_part_statistics(
        act, offset >= 0, offset < 0, (n_before, T1 - n_before), sums, squares, counts, onehot, j, ahead
    )

    @pl.when(j == pl.num_programs(0) - 1)
    def _():
        put_statistics(msg_ref, sums[...], squares[...], counts[...], onehot[...])


def depth_kernel(
    items, pos_ref, msg_in_ref, mix_ref, prev_ref, next_ref, own_ref, core_ref, x_ref, far_ref,
    hidden_ref, depth_ref, msg_ref, vec_ref, table_ref,
    gathered, sems, w_stack, w_low, ring, sums, squares, counts, onehot,
):
    m = pl.program_id(0)
    last = pl.num_programs(0) - 1
    half = pos_ref[1]
    own_rows = (last - 1) * T

    @pl.when(m == 0)
    def _():
        me = pos_ref[2]
        copies = [
            pltpu.make_async_copy(ref.at[pl.ds(0, PACK_IN)], gathered.at[me ^ k], sems.at[k])
            for k, ref in enumerate((own_ref, core_ref, x_ref, far_ref))
        ]
        for copy in copies:
            copy.start()
        merge_statistics(msg_in_ref, table_ref)
        sums[...] = jnp.zeros_like(sums)
        squares[...] = jnp.zeros_like(squares)
        counts[...] = jnp.zeros_like(counts)
        onehot[...] = jnp.zeros_like(onehot)
        for copy in copies:
            copy.wait()
        for s in range(4):
            cut = slice(s * LANES, (s + 1) * LANES)
            hi, lo = split(gathered[s, 0:128, :])
            w_stack[0:128, cut] = hi
            w_stack[128:256, cut] = hi
            w_low[:, cut] = lo
            vec_ref[:, cut] = gathered[s, 128 : 128 + NVEC, :]

    def vec(row):
        return vec_ref[row : row + 1, :]

    start = pos_ref[0] + half * own_rows + (m - 1) * T
    edge, ahead = boundary(pos_ref, items, start)
    block = half * (own_rows // T) + m - 1
    top = 2 * (own_rows // T)
    mix = jnp.where(block < 0, prev_ref[...], jnp.where(block >= top, next_ref[...], mix_ref[...]))
    m_hi, m_lo = split(mix)
    hidden = mm(cat([m_hi, m_lo], 1), w_stack[...]) + mm(m_hi, w_low[...]) + vec(0)

    @pl.when((m > 0) & (m < last))
    def _():
        hidden_ref[...] = hidden

    slope = vec(1)
    act = hidden * (slope + (1.0 - slope) * sigmoid(hidden))
    row_b, row_a = item_rows(ahead, items)
    inv_b, inv_a = table_ref[1, pl.ds(row_b, 1), :], table_ref[1, pl.ds(row_a, 1), :]
    mean_b, mean_a = table_ref[0, pl.ds(row_b, 1), :], table_ref[0, pl.ds(row_a, 1), :]
    scale_b, scale_a = inv_b * vec(2), inv_a * vec(2)
    shift_b, shift_a = vec(3) - mean_b * scale_b, vec(3) - mean_a * scale_a
    after = iota((T, HIDDEN), 0) + (start - edge) >= 0

    @pl.when(m > 0)
    def _():
        ring[0:T, :] = ring[T : 2 * T, :]

    ring[T : 2 * T, :] = act * jnp.where(after, scale_a, scale_b) + jnp.where(after, shift_a, shift_b)

    @pl.when(m > 0)
    def _():
        begin = start - STEP
        edge, ahead = boundary(pos_ref, items, begin)
        offset = iota((T, HIDDEN), 0) + (begin - edge)
        lower = jnp.where((offset >= 0) & (offset < STEP), 0.0, ring[0:T, :])
        upper = jnp.where((offset < 0) & (offset >= -STEP), 0.0, ring[T : 2 * T, :])
        depth = vec(4) * lower + vec(5) * ring[STEP : STEP + T, :] + vec(6) * upper + vec(7)
        depth_ref[...] = depth
        slope = vec(8)
        act = depth * (slope + (1.0 - slope) * sigmoid(depth))
        low = jnp.where(m == 1, STEP, 0)
        high = jnp.where(m == last, STEP, T)
        row = iota((T, HIDDEN), 0)
        own = (row >= low) & (row < high)
        n_before = jnp.clip(edge - begin, low, high) - low
        n_after = (high - low - n_before).astype(F32)
        two_part_statistics(
            act, own & (offset >= 0), own & (offset < 0), (n_before.astype(F32), n_after),
            sums, squares, counts, onehot, m - 1, ahead,
        )

    @pl.when(m == last)
    def _():
        put_statistics(msg_ref, sums[...], squares[...], counts[...], onehot[...])


def mask_kernel(
    items, pos_ref, msg_in_ref, depth_a_ref, depth_b_ref, mix_ref, skip_ref, enc_ref, cot_ref, wave_cot_ref,
    wave_next_ref, edge_next_ref, basis_ref, vec_ref, b_out_ref, slope_skip_ref, own_ref, core_ref, x_ref, far_ref,
    block_ref, grad_skip_ref, grad_enc_ref, send_ref, wave_ref, r_ref, up_ref, down_ref, keep_ref, give_ref, msg_ref,
    table_ref,
    gathered, sems, wo_hi, wo_lo, wot_hi, wot_lo, wm_stack, wm_low, wmt, basis_hi, basis_lo, basis_back, select_hi,
    select_lo, norm_hi, norm_lo, logit_hi, logit_lo, carry, acc_out, acc_mask, acc_basis, acc_vec, acc_small, entries,
    onehot,
):
    j = pl.program_id(0)
    last = pl.num_programs(0) - 1
    half = pos_ref[1]
    me = pos_ref[2]
    side = me // 2
    own_rows = (last + 1) * T

    def vec(row):
        return vec_ref[row : row + 1, :]

    @pl.when(j == 0)
    def _():
        rows = own_ref.shape[0] - PACK_IN
        copies = [
            pltpu.make_async_copy(ref.at[pl.ds(PACK_IN, rows)], gathered.at[me ^ k], sems.at[k])
            for k, ref in enumerate((own_ref, core_ref, x_ref, far_ref))
        ]
        for copy in copies:
            copy.start()
        merge_statistics(msg_in_ref, table_ref)
        acc_out[...] = jnp.zeros_like(acc_out)
        acc_mask[...] = jnp.zeros_like(acc_mask)
        acc_basis[...] = jnp.zeros_like(acc_basis)
        acc_vec[...] = jnp.zeros_like(acc_vec)
        acc_small[...] = jnp.zeros_like(acc_small)
        carry[...] = jnp.zeros_like(carry)
        b_hi, b_lo = split(basis_ref[...])
        col = iota((L, 2 * LANES), 1)
        row = iota((L, 2 * LANES), 0)
        spread = ((col & 7) == (row & 7)) & ((col >> 7) == (row >> 3))
        spread = spread.astype(F32).astype(BF16)
        basis_hi[...] = mm(b_hi, spread).astype(BF16)
        basis_lo[...] = mm(b_lo, spread).astype(BF16)
        for c in range(2):
            row = iota((LANES, L), 0) - 48 * c
            col = iota((LANES, L), 1)
            with_hi = ((row == col) | (row == col + 32)).astype(F32).astype(BF16)
            with_lo = (row == col + 16).astype(F32).astype(BF16)
            back = mm_nt(with_hi, b_hi) + mm_nt(with_lo, b_lo)
            basis_back[:, c * HIDDEN : (c + 1) * HIDDEN] = back.astype(BF16)
            row = iota((2 * LANES, LANES), 0)
            col = iota((2 * LANES, LANES), 1) - 48 * c
            place = (row & 7) + ((row >> 7) << 3)
            select_hi[c] = ((col == place) | (col == place + 16)).astype(F32).astype(BF16)
            select_lo[c] = (col == place + 32).astype(F32).astype(BF16)
        for copy in copies:
            copy.wait()
        for s in range(4):
            cut = slice(s * LANES, (s + 1) * LANES)
            for k in range(2):
                col = slice(k * LANES, (k + 1) * LANES)
                part = gathered[s, k * LANES : (k + 1) * LANES, :]
                hi, lo = split(part)
                wo_hi[cut, col] = hi
                wo_lo[cut, col] = lo
                hi, lo = split(part.T)
                wot_hi[col, cut] = hi
                wot_lo[col, cut] = lo
                part = gathered[s, (2 + k) * LANES : (3 + k) * LANES, :]
                wide = slice(s * 256 + k * LANES, s * 256 + (k + 1) * LANES)
                hi, lo = split(part)
                wm_stack[0:128, wide] = hi
                wm_stack[128:256, wide] = hi
                wm_low[:, wide] = lo
                hi, lo = split(part.T)
                wmt[wide, 0:128] = hi
                wmt[wide, 128:256] = lo

    start = pos_ref[0] + half * own_rows + j * T
    edge, ahead = boundary(pos_ref, items, start)
    row_b, row_a = item_rows(ahead, items)
    offset = iota((T, LANES), 0) + (start - edge)
    after = offset >= 0
    after4 = cat([after] * 4, 1) if False else (iota((T, HIDDEN), 0) + (start - edge) >= 0)

    depth = cat([depth_a_ref[...], depth_b_ref[...]], 0)
    slope = vec(8)
    s = sigmoid(depth)
    part = (1.0 - slope) * s
    act = depth * (slope + part)
    inv = jnp.where(after4, table_ref[1, pl.ds(row_a, 1), :], table_ref[1, pl.ds(row_b, 1), :])
    mean = jnp.where(after4, table_ref[0, pl.ds(row_a, 1), :], table_ref[0, pl.ds(row_b, 1), :])
    normed = (act - mean) * inv
    hi, lo = split(normed * vec(9) + vec(10))
    norm_hi[...] = hi
    norm_lo[...] = lo
    branch = mm(hi, wo_hi[...]) + mm(hi, wo_lo[...]) + mm(lo, wo_hi[...]) + b_out_ref[...]
    block = mix_ref[...] + branch[:, 0:128]
    block_ref[...] = block
    send_ref[:, 0:128] = block
    total = skip_ref[...] + branch[:, 128:256]
    slope_skip = slope_skip_ref[...]
    s_skip = sigmoid(total)
    active = total * (slope_skip + (1.0 - slope_skip) * s_skip)
    a_hi, a_lo = split(active)
    a_both = cat([a_hi, a_lo], 1)

    lane_frame = iota((T, LANES), 1) >> 3
    frame = iota((T, LANES), 0) & 15
    here = lane_frame == frame
    ahead_same = offset != -1
    packed = 0.0
    for c in range(2):
        rows = [wave_cot_ref[c : c + 1, q * LANES : (q + 1) * LANES] for q in range(T // 16)]
        final = jnp.where(
            (half == 1) & (j == last), edge_next_ref[c : c + 1, :], wave_next_ref[c : c + 1, 0:LANES]
        )
        spread_rows = cat([jnp.broadcast_to(r, (16, LANES)) for r in rows], 0)
        next_rows = cat([jnp.broadcast_to(r, (16, LANES)) for r in rows[1:] + [final]], 0)
        current = jnp.where(here, spread_rows, 0.0)
        following = jnp.where(lane_frame == frame + 1, spread_rows, 0.0)
        following = jnp.where((frame == 15) & (lane_frame == 0), next_rows, following)
        following = jnp.where(ahead_same, following, 0.0)
        hi, lo = split(cat([current, following], 1))
        packed = packed + mm(hi, select_hi[c]) + mm(lo, select_lo[c])
    packed = packed.astype(BF16)

    decoded = [0.0, 0.0]
    back = 0.0
    for n in range(2):
        enc = enc_ref[:, n * 256 : (n + 1) * 256]
        grad_enc = 0.0
        for c in range(2):
            chunk = slice(c * HIDDEN + n * 256, c * HIDDEN + (n + 1) * 256)
            bias = vec_ref[11:12, 2 * c * 128 + n * 128 : 2 * c * 128 + n * 128 + 128]
            bias = cat([bias, vec_ref[12:13, 2 * c * 128 + n * 128 : 2 * c * 128 + n * 128 + 128]], 1)
            logits = mm(a_both, wm_stack[:, chunk]) + mm(a_hi, wm_low[:, chunk]) + bias
            mask = sigmoid(logits)
            masked = mask * enc
            hi, lo = split(masked)
            b_hi, b_lo = basis_hi[n * 256 : (n + 1) * 256, :], basis_lo[n * 256 : (n + 1) * 256, :]
            decoded[c] = decoded[c] + mm(hi, b_hi) + mm(hi, b_lo) + mm(lo, b_hi)
            acc_basis[c, :, n * 256 : (n + 1) * 256] += mm_tn(packed, hi) + mm_tn(packed, lo)
            grad_masked = mm(packed, basis_back[:, chunk])
            grad_enc = grad_enc + grad_masked * mask
            grad_logits = grad_masked * masked * (1.0 - mask)
            hi, lo = split(grad_logits)
            logit_hi[c, :, n * 256 : (n + 1) * 256] = hi
            logit_lo[c, :, n * 256 : (n + 1) * 256] = lo
            back = back + mm(hi, wmt[chunk, :]) + mm(lo, wmt[chunk, :])
            acc_vec[2 : 3, chunk] += colsum(grad_logits)
        grad_enc_ref[:, n * 256 : (n + 1) * 256] = grad_enc
        send_ref[:, 256 + n * 256 : 256 + (n + 1) * 256] = grad_enc
    grad_active = back[:, 0:128] + back[:, 128:256]

    for c in range(2):
        tail = decoded[c][:, 128:256]
        shifted = pltpu.roll(tail, 1, 0)
        first = iota((T, LANES), 0) == 0
        shifted = jnp.where(first, carry[c : c + 1, :], shifted)
        carry[c : c + 1, :] = tail[T - 1 : T, :]
        value = decoded[c][:, 0:128] + jnp.where(offset == 0, 0.0, shifted)
        value = jnp.where(here, value, 0.0)
        lines = jnp.sum(value.reshape(T // 16, 16, LANES), axis=1)
        for q in range(T // 16):
            wave_ref[c : c + 1, q * LANES : (q + 1) * LANES] = lines[q : q + 1, :]

    u = 1.0 - s_skip
    grad_skip = grad_active * (slope_skip + (1.0 - slope_skip) * s_skip * (1.0 + total * u))
    grad_skip_ref[...] = grad_skip
    send_ref[:, 128:256] = grad_skip
    cot = cot_ref[...]
    acc_small[0:1, 0:128] += colsum(grad_active * (total * u))
    acc_small[1:2, 0:128] += colsum(cot)
    acc_small[2:3, 0:128] += colsum(grad_skip)
    g_hi, g_lo = split(cat([cot, grad_skip], 1))
    r = mm(g_hi, wot_hi[...]) + mm(g_hi, wot_lo[...]) + mm(g_lo, wot_hi[...])
    r_ref[...] = r

    @pl.when(j == 0)
    def _():
        down_ref[...] = r[0:128, :]

    @pl.when(j == last)
    def _():
        up_ref[0:128, :] = r[T - 128 : T, :]
        up_ref[128:136, :] = jnp.zeros((8, HIDDEN), F32)
        up_ref[128:130, 0:128] = carry[0:2, :]

    wide = pl.ds(pl.multiple_of(side * 256, 256), 256)
    n_hi, n_lo = norm_hi[:, wide], norm_lo[:, wide]
    acc_out[...] += mm_tn(n_hi, g_hi) + mm_tn(n_lo, g_hi) + mm_tn(n_hi, g_lo)
    l_hi, l_lo = logit_hi[side], logit_lo[side]
    both = mm_tn(a_both, l_hi)
    acc_mask[...] += both[0:128] + both[128:256] + mm_tn(a_hi, l_lo)
    acc_vec[0:1, 0:HIDDEN] += colsum(r * normed)
    acc_vec[1:2, 0:HIDDEN] += colsum(r)

    offset4 = iota((T, HIDDEN), 0) + (start - edge)
    taps = jnp.where((offset4 >= 0) & (offset4 < STEP), 0.0, vec(4)) + vec(5)
    taps = taps + jnp.where((offset4 < 0) & (offset4 >= -STEP), 0.0, vec(6))
    pull = inv * (slope + part * (1.0 + depth * (1.0 - s)))
    plain = pull * (vec(2) * taps)
    cross = pull * (depth - vec(7) - vec(3) * taps)
    q = r * vec(9)
    quantities = (q, q * normed, plain * q, plain, plain * normed, cross * q, cross, cross * normed)
    for i, value in enumerate(quantities):
        value = value[:, 0:128] + value[:, 128:256] + value[:, 256:384] + value[:, 384:512]
        entries[i, pl.ds(2 * j, 1), :] = colsum(jnp.where(after, 0.0, value))
        entries[i, pl.ds(2 * j + 1, 1), :] = colsum(jnp.where(after, value, 0.0))
    hot_b, hot_a = lane_items(ahead, items)
    onehot[pl.ds(2 * j, 1), :] = hot_b
    onehot[pl.ds(2 * j + 1, 1), :] = hot_a

    @pl.when(j == last)
    def _():
        hot = onehot[...]
        lines = [colsum(hot * jnp.sum(entries[i], axis=1, keepdims=True)) for i in range(8)]
        msg = cat(lines, 0)
        for i in range(msg_ref.shape[0]):
            msg_ref[i] = msg
        for ref, h in ((keep_ref, half), (give_ref, 1 - half)):
            own = pl.ds(pl.multiple_of(h * 128, 128), 128)
            ref[0:128, :] = acc_out[own, 0:128]
            ref[128:256, :] = acc_out[own, 128:256]
            pair = pl.ds(pl.multiple_of(h * 256, 256), 256)
            mask_part = acc_mask[:, pair]
            ref[256:384, :] = mask_part[:, 0:128]
            ref[384:512, :] = mask_part[:, 128:256]
            bias = acc_vec[2:3, pl.ds(pl.multiple_of(side * 512 + h * 256, 256), 256)]
            channels = pl.ds(pl.multiple_of(side * 256 + h * 128, 128), 128)
            ref[512:520, :] = cat(
                [
                    bias[:, 0:128], bias[:, 128:256], acc_vec[0:1, channels], acc_vec[1:2, channels],
                    acc_small[0:3, 0:128], jnp.zeros((1, LANES), F32),
                ], 0,
            )
            for k in range(4):
                cut = slice(k * 128, (k + 1) * 128)
                ref[520 + 16 * k : 536 + 16 * k, :] = (
                    acc_basis[0, 0:16, cut] + acc_basis[0, 32:48, cut]
                    + acc_basis[1, 48:64, cut] + acc_basis[1, 80:96, cut]
                )


def back_kernel(
    items, pos_ref, msg_in_ref, depth_ref, r_a_ref, r_b_ref, low_ref, high_ref, hidden_ref, mix_ref, cot_ref,
    vec_ref, table_in_ref, table_mid_ref, own_ref, core_ref, x_ref, far_ref, got_ref, block_in, skip_in, enc_in,
    grad_mix_ref, send_ref, keep_ref, give_ref, block_ref, skip_ref, enc_ref,
    gathered, sems, table, wt, ring, grad_hi, grad_lo, acc_w, acc_vec,
):
    j = pl.program_id(0)
    last = pl.num_programs(0) - 1
    half = pos_ref[1]
    me = pos_ref[2]
    side = me // 2
    own_rows = last * T

    def vec(row):
        return vec_ref[row : row + 1, :]

    @pl.when(j == 0)
    def _():
        copies = [
            pltpu.make_async_copy(ref.at[pl.ds(0, 128)], gathered.at[me ^ k], sems.at[k])
            for k, ref in enumerate((own_ref, core_ref, x_ref, far_ref))
        ]
        for copy in copies:
            copy.start()
        totals = 0.5 * jnp.sum(msg_in_ref[...], axis=0)
        lane = iota((1, LANES), 1)
        number = jnp.zeros((1, LANES), jnp.int32)
        for k in range(items):
            begin = pos_ref[2 + k] if k else 0
            number = jnp.where(lane == k, pos_ref[3 + k] - begin, number)
        number = jnp.maximum(number.astype(F32) * HIDDEN, 1.0)
        m1 = totals[0:1] / number
        m2 = totals[1:2] / number
        p1 = (totals[2:3] - m1 * totals[3:4] - m2 * totals[4:5]) / number
        p2 = (totals[5:6] - m1 * totals[6:7] - m2 * totals[7:8]) / number
        padded = table.shape[1]
        for i, value in enumerate((m1, m2, p1, p2)):
            table[i] = to_rows(value, padded)
        acc_w[...] = jnp.zeros_like(acc_w)
        acc_vec[...] = jnp.zeros_like(acc_vec)
        for copy in copies:
            copy.wait()
        for s in range(4):
            cut = slice(s * LANES, (s + 1) * LANES)
            hi, lo = split(gathered[s].T)
            wt[cut, 0:128] = hi
            wt[cut, 128:256] = lo

    block_ref[...] = got_ref[:, 0:128]
    skip_ref[...] = got_ref[:, 128:256]
    enc_ref[...] = got_ref[:, 256:768]

    begin = pos_ref[0] + half * own_rows + j * T - STEP
    edge, ahead = boundary(pos_ref, items, begin)
    row_b, row_a = item_rows(ahead, items)
    after = iota((T, HIDDEN), 0) + (begin - edge) >= 0

    def pick(ref, i, after, row_a, row_b):
        return jnp.where(after, ref[i, pl.ds(row_a, 1), :], ref[i, pl.ds(row_b, 1), :])

    depth = depth_ref[...]
    r = cat(
        [
            jnp.where(j == 0, low_ref[0:128, :], r_a_ref[...]),
            jnp.where(j == last, high_ref[...], r_b_ref[...]),
        ], 0,
    )
    slope = vec(8)
    s = sigmoid(depth)
    u = depth * (1.0 - s)
    part = (1.0 - slope) * s
    act = depth * (slope + part)
    inv = pick(table_mid_ref, 1, after, row_a, row_b)
    normed = (act - pick(table_mid_ref, 0, after, row_a, row_b)) * inv
    grad_act = inv * (r * vec(9) - pick(table, 0, after, row_a, row_b) - normed * pick(table, 1, after, row_a, row_b))
    in_low = jnp.where(j > 0, 1.0, 0.0)
    in_high = jnp.where(j < last, 1.0, 0.0)
    along = grad_act * u
    acc_vec[8:9, :] += in_low * colsum(along[0:128]) + in_high * colsum(along[128:256])

    @pl.when(j > 0)
    def _():
        ring[0:T, :] = ring[T : 2 * T, :]

    ring[T : 2 * T, :] = grad_act * (slope + part * (1.0 + u))

    @pl.when(j > 0)
    def _():
        start = pos_ref[0] + half * own_rows + (j - 1) * T
        edge, ahead = boundary(pos_ref, items, start)
        row_b, row_a = item_rows(ahead, items)
        offset = iota((T, HIDDEN), 0) + (start - edge)
        after = offset >= 0
        grad_low = jnp.where((offset >= 0) & (offset < STEP), 0.0, ring[0:T, :])
        grad_high = jnp.where((offset < 0) & (offset >= -STEP), 0.0, ring[T : 2 * T, :])
        grad_mid = ring[STEP : STEP + T, :]
        grad_norm = vec(5) * grad_mid + vec(4) * grad_high + vec(6) * grad_low
        hidden = hidden_ref[...]
        slope = vec(1)
        s = sigmoid(hidden)
        u = hidden * (1.0 - s)
        part = (1.0 - slope) * s
        act = hidden * (slope + part)
        inv = pick(table_in_ref, 1, after, row_a, row_b)
        normed = (act - pick(table_in_ref, 0, after, row_a, row_b)) * inv
        norm = normed * vec(2) + vec(3)
        grad_act = inv * (
            grad_norm * vec(2) - pick(table, 2, after, row_a, row_b) - normed * pick(table, 3, after, row_a, row_b)
        )
        grad_hidden = grad_act * (slope + part * (1.0 + u))
        sums = (
            grad_hidden, grad_act * u, grad_norm * normed, grad_norm, norm * grad_high, norm * grad_mid,
            norm * grad_low, grad_mid,
        )
        acc_vec[0:8, :] += cat([colsum(value) for value in sums], 0)
        hi, lo = split(grad_hidden)
        grad_hi[...] = hi
        grad_lo[...] = lo
        back = mm(hi, wt[...]) + mm(lo, wt[...])
        grad_mix = cot_ref[...] + back[:, 0:128] + back[:, 128:256]
        grad_mix_ref[...] = grad_mix
        send_ref[...] = grad_mix
        wide = pl.ds(pl.multiple_of(side * 256, 256), 256)
        m_hi, m_lo = split(mix_ref[...])
        both = mm_tn(cat([m_hi, m_lo], 1), grad_hi[:, wide])
        acc_w[...] += both[0:128] + both[128:256] + mm_tn(m_hi, grad_lo[:, wide])

    @pl.when(j == last)
    def _():
        for ref, h in ((keep_ref, half), (give_ref, 1 - half)):
            ref[0:128, :] = acc_w[:, pl.ds(pl.multiple_of(h * 128, 128), 128)]
            channels = pl.ds(pl.multiple_of(side * 256 + h * 128, 128), 128)
            ref[128:144, :] = acc_vec[:, channels]


def last_kernel(
    a_ref, b_ref, c_ref, d_ref, w_in, b_in, slope_in, gain_in, beta_in, w_depth, b_depth, slope_mid, gain_mid,
    beta_mid, w_out, b_out, slope_skip, w_mask, b_mask, basis,
):
    late = a_ref[...] + b_ref[...]
    w_in[...] = late[0:128]
    for ref, row in (
        (b_in, 128), (slope_in, 129), (gain_in, 130), (beta_in, 131), (b_depth, 135), (slope_mid, 136),
    ):
        ref[...] = late[row : row + 1]
    w_depth[...] = late[132:135]
    early = c_ref[...] + d_ref[...]
    w_out[:, 0:128] = early[0:128]
    w_out[:, 128:256] = early[128:256]
    w_mask[:, 0:128] = early[256:384]
    w_mask[:, 128:256] = early[384:512]
    b_mask[:, 0:128] = early[512:513]
    b_mask[:, 128:256] = early[513:514]
    gain_mid[...] = early[514:515]
    beta_mid[...] = early[515:516]
    slope_skip[...] = early[516:517]
    b_out[:, 0:128] = early[517:518]
    b_out[:, 128:256] = early[518:519]
    for k in range(4):
        basis[k * 128 : (k + 1) * 128, :] = early[520 + 16 * k : 536 + 16 * k].T


def local(
    mix_in, skip_in, encoded, lengths, w_in, b_in, slope_in, gain_in, beta_in, w_depth, b_depth, slope_mid, gain_mid,
    beta_mid, w_out, b_out, slope_skip, w_mask, b_mask, basis, cot_out, cot_wave,
):
    n_tm, n_src = lax.axis_size("tm"), lax.axis_size("src")
    devices = n_tm * n_src
    frames = mix_in.shape[0]
    own_rows = frames // 2
    items = lengths.shape[0]
    padded = -(-items // 8) * 8
    tiles = own_rows // T
    tm, me = lax.axis_index("tm"), lax.axis_index("src")
    half = me % 2
    pos = jnp.concatenate(
        [jnp.stack([tm * frames, half, me]).astype(jnp.int32), jnp.cumsum(lengths, dtype=jnp.int32)]
    )
    up = [(i, i + 1) for i in range(n_tm - 1)]
    down = [(j, i) for i, j in up]
    swap = [(i, i ^ 1) for i in range(n_src)]
    cross = [(i, i ^ 2) for i in range(n_src)]

    mix_prev = lax.ppermute(mix_in[frames - T :], "tm", up)
    mix_next = lax.ppermute(mix_in[:T], "tm", down)
    cot_next = lax.ppermute(cot_wave[:, :LANES], "tm", down)

    def params(**kw):
        return pltpu.CompilerParams(vmem_limit_bytes=50 * 2**20, **kw)

    def struct(*shape):
        return jax.ShapeDtypeStruct(shape, F32)

    def whole(shape):
        zeros = (0,) * len(shape)
        return pl.BlockSpec(shape, lambda i, pos: zeros)

    anywhere = pl.BlockSpec(memory_space=pl.ANY)

    def vmem(*shape):
        return pltpu.VMEM(shape, F32)

    def vmem16(*shape):
        return pltpu.VMEM(shape, BF16)

    def call(kernel, name, grid, in_specs, out_specs, out_shape, scratch, **kw):
        return pl.pallas_call(
            functools.partial(kernel, items),
            grid_spec=pltpu.PrefetchScalarGridSpec(
                num_scalar_prefetch=1, grid=(grid,), in_specs=in_specs, out_specs=out_specs, scratch_shapes=scratch
            ),
            out_shape=out_shape,
            compiler_params=params(dimension_semantics=("arbitrary",)),
            name=name,
            **kw,
        )

    message = struct(devices, 8, LANES)

    def exchange(msg):
        return lax.all_to_all(msg, ("tm", "src"), 0, 0)

    n1 = frames // T1
    msg1 = call(
        first_kernel, "first", n1,
        [pl.BlockSpec((T1, 128), lambda i, pos: (i, 0)), whole((128, 128)), whole((1, 128)), whole((1, 128))],
        whole(message.shape), message,
        [vmem(1, 2 * n1, 128), vmem(1, 2 * n1, 128), vmem(2 * n1, 128), vmem(2 * n1, 128)],
    )(pos, mix_in, w_in, b_in.reshape(1, 128), slope_in.reshape(1, 128))

    vectors = jnp.concatenate(
        [
            b_in[None], slope_in[None], gain_in[None], beta_in[None], w_depth, b_depth[None], slope_mid[None],
            gain_mid[None], beta_mid[None], b_mask.reshape(2, 128), jnp.zeros((3, 128), F32),
        ]
    )
    pack = jnp.concatenate([w_in, vectors, w_out[:, :128], w_out[:, 128:], w_mask[:, :128], w_mask[:, 128:]])
    pack_core = lax.ppermute(pack, "src", swap)
    pack_x = lax.ppermute(pack, "src", cross)
    pack_far = lax.ppermute(pack_x, "src", swap)
    packs = (pack, pack_core, pack_x, pack_far)

    msg1 = exchange(msg1)

    entries = -(-2 * (tiles + 1) // 8) * 8
    hidden, depth, msg2, vec, table_in = call(
        depth_kernel, "depth", tiles + 2,
        [
            whole(message.shape),
            pl.BlockSpec((T, 128), lambda i, pos: (jnp.clip(pos[1] * tiles + i - 1, 0, 2 * tiles - 1), 0)),
            whole((T, 128)), whole((T, 128)), anywhere, anywhere, anywhere, anywhere,
        ],
        [
            pl.BlockSpec((T, HIDDEN), lambda i, pos: (jnp.clip(i - 1, 0, tiles - 1), 0)),
            pl.BlockSpec((T, HIDDEN), lambda i, pos: (jnp.maximum(i - 1, 0), 0)),
            whole(message.shape), whole((NVEC, HIDDEN)), whole((2, padded, HIDDEN)),
        ],
        [
            struct(own_rows, HIDDEN), struct(own_rows + T, HIDDEN), message, struct(NVEC, HIDDEN),
            struct(2, padded, HIDDEN),
        ],
        [
            vmem(4, PACK_IN, 128), pltpu.SemaphoreType.DMA((4,)), vmem16(256, HIDDEN), vmem16(128, HIDDEN),
            vmem(2 * T, HIDDEN), vmem(4, entries, 128), vmem(4, entries, 128), vmem(entries, 128),
            vmem(entries, 128),
        ],
    )(pos, msg1, mix_in, mix_prev, mix_next, *packs)
    msg2 = exchange(msg2)

    def half_rows(width):
        return pl.BlockSpec((T, width), lambda i, pos: (pos[1] * tiles + i, 0))

    def rows(width):
        return pl.BlockSpec((T, width), lambda i, pos: (i, 0))

    def other_rows(width):
        return pl.BlockSpec(
            (T, width), lambda i, pos: ((1 - pos[1]) * tiles + jnp.minimum(i, tiles - 1), 0)
        )

    pack_early = 584
    (block_out, grad_skip, grad_enc, send, wave_half, r, r_up, r_down, keep, give, msg3, table_mid) = call(
        mask_kernel, "mask", tiles,
        [
            whole(message.shape),
            pl.BlockSpec((128, HIDDEN), lambda i, pos: (2 * i + 1, 0)),
            pl.BlockSpec((128, HIDDEN), lambda i, pos: (2 * i + 2, 0)),
            half_rows(128), half_rows(128), half_rows(HIDDEN), half_rows(128),
            pl.BlockSpec((2, T * STRIDE), lambda i, pos: (0, pos[1] * tiles + i)),
            pl.BlockSpec((2, T * STRIDE), lambda i, pos: (0, jnp.minimum(pos[1] * tiles + i + 1, 2 * tiles - 1))),
            whole((2, 128)), whole((HIDDEN, L)), whole((NVEC, HIDDEN)), whole((1, 256)), whole((1, 128)),
            anywhere, anywhere, anywhere, anywhere,
        ],
        [
            half_rows(128), half_rows(128), half_rows(HIDDEN), rows(768),
            pl.BlockSpec((2, T * STRIDE), lambda i, pos: (0, i)),
            rows(HIDDEN), whole((136, HIDDEN)), whole((128, HIDDEN)), whole((pack_early, 128)),
            whole((pack_early, 128)), whole(message.shape), whole((2, padded, HIDDEN)),
        ],
        [
            struct(frames, 128), struct(frames, 128), struct(frames, HIDDEN), struct(own_rows, 768),
            struct(2, own_rows * STRIDE), struct(own_rows, HIDDEN), struct(136, HIDDEN), struct(128, HIDDEN),
            struct(pack_early, 128), struct(pack_early, 128), message, struct(2, padded, HIDDEN),
        ],
        [
            vmem(4, 512, 128), pltpu.SemaphoreType.DMA((4,)), vmem16(HIDDEN, 256), vmem16(HIDDEN, 256),
            vmem16(256, HIDDEN), vmem16(256, HIDDEN), vmem16(256, 1024), vmem16(128, 1024), vmem16(1024, 256),
            vmem16(HIDDEN, 256), vmem16(HIDDEN, 256), vmem16(128, 1024), vmem16(2, 256, 128), vmem16(2, 256, 128),
            vmem16(T, HIDDEN), vmem16(T, HIDDEN), vmem16(2, T, HIDDEN), vmem16(2, T, HIDDEN), vmem(8, 128),
            vmem(256, 256), vmem(128, HIDDEN), vmem(2, 128, HIDDEN), vmem(8, 1024), vmem(8, 128),
            vmem(8, 2 * tiles, 128), vmem(2 * tiles, 128),
        ],
    )(
        pos, msg2, depth, depth, mix_in, skip_in, encoded, cot_out, cot_wave, cot_wave, cot_next, basis, vec,
        b_out.reshape(1, 256), slope_skip.reshape(1, 128), *packs,
    )

    both = ("tm", "src")
    later, earlier = [], []
    for i in range(n_tm):
        for s in range(n_src):
            here = i * n_src + s
            there = here + 1 if s % 2 == 0 else (i + 1) * n_src + s - 1
            if s % 2 == 0 or i + 1 < n_tm:
                later.append((here, there))
                earlier.append((there, here))
    got_low = lax.ppermute(r_up, both, later)
    got_high = lax.ppermute(r_down, both, earlier)
    got = lax.ppermute(send, "src", swap)
    early = keep + lax.ppermute(give, "src", swap)
    wave_other = lax.ppermute(wave_half, "src", swap)
    msg3 = exchange(msg3)

    grad_mix, mix_send, keep, give, block_out, grad_skip, grad_enc = call(
        back_kernel, "back", tiles + 1,
        [
            whole(message.shape), rows(HIDDEN),
            pl.BlockSpec((128, HIDDEN), lambda i, pos: (jnp.maximum(2 * i - 1, 0), 0)),
            pl.BlockSpec((128, HIDDEN), lambda i, pos: (jnp.minimum(2 * i, 2 * tiles - 1), 0)),
            whole((136, HIDDEN)), whole((128, HIDDEN)),
            pl.BlockSpec((T, HIDDEN), lambda i, pos: (jnp.maximum(i - 1, 0), 0)),
            pl.BlockSpec((T, 128), lambda i, pos: (pos[1] * tiles + jnp.maximum(i - 1, 0), 0)),
            pl.BlockSpec((T, 128), lambda i, pos: (pos[1] * tiles + jnp.maximum(i - 1, 0), 0)),
            whole((NVEC, HIDDEN)), whole((2, padded, HIDDEN)), whole((2, padded, HIDDEN)),
            anywhere, anywhere, anywhere, anywhere,
            pl.BlockSpec((T, 768), lambda i, pos: (jnp.minimum(i, tiles - 1), 0)), anywhere, anywhere, anywhere,
        ],
        [
            pl.BlockSpec((T, 128), lambda i, pos: (pos[1] * tiles + jnp.maximum(i - 1, 0), 0)),
            pl.BlockSpec((T, 128), lambda i, pos: (jnp.maximum(i - 1, 0), 0)),
            whole((144, 128)), whole((144, 128)), other_rows(128), other_rows(128), other_rows(HIDDEN),
        ],
        [
            struct(frames, 128), struct(own_rows, 128), struct(144, 128), struct(144, 128), struct(frames, 128),
            struct(frames, 128), struct(frames, HIDDEN),
        ],
        [
            vmem(4, 128, 128), pltpu.SemaphoreType.DMA((4,)), vmem(4, padded, HIDDEN), vmem16(HIDDEN, 256),
            vmem(2 * T, HIDDEN), vmem16(T, HIDDEN), vmem16(T, HIDDEN), vmem(128, 256),
            vmem(16, HIDDEN),
        ],
        input_output_aliases={18: 4, 19: 5, 20: 6},
    )(
        pos, msg3, depth, r, r, got_low, got_high, hidden, mix_in, cot_out, vec, table_in, table_mid, *packs, got,
        block_out, grad_skip, grad_enc,
    )

    starts = jnp.concatenate([jnp.zeros((1,), jnp.int32), pos[3:]])
    mine = pos[0] + half * own_rows
    theirs = pos[0] + (1 - half) * own_rows
    same_mine = jnp.where(jnp.any(starts == mine), 0.0, 1.0)
    edge_mine = jnp.where(same_mine > 0, got_low[128:130, :STRIDE], 0.0)
    wave_half = wave_half.at[:, :STRIDE].add(edge_mine)
    del theirs, wave_other
    wave_other = lax.ppermute(wave_half, "src", swap)
    first = jnp.where(half == 0, wave_half, wave_other)
    second = jnp.where(half == 0, wave_other, wave_half)
    wave = jnp.concatenate([first, second], axis=1)

    mix_got = lax.ppermute(mix_send, "src", swap)
    grad_mix = lax.dynamic_update_slice_in_dim(grad_mix, mix_got, (1 - half) * own_rows, 0)

    late = keep + lax.ppermute(give, "src", swap)
    bits = n_tm.bit_length() - 1
    for bit in range(bits):
        perm = [(i, i ^ (1 << bit)) for i in range(n_tm)]
        late_other = lax.ppermute(late, "tm", perm)
        early_other = lax.ppermute(early, "tm", perm)
        if bit < bits - 1:
            late, early = late + late_other, early + early_other

    outs = pl.pallas_call(
        last_kernel,
        out_shape=[
            struct(128, 128), struct(1, 128), struct(1, 128), struct(1, 128), struct(1, 128), struct(3, 128),
            struct(1, 128), struct(1, 128), struct(1, 128), struct(1, 128), struct(128, 256), struct(1, 256),
            struct(1, 128), struct(128, 256), struct(1, 256), struct(HIDDEN, L),
        ],
        compiler_params=params(),
        name="last",
    )(late, late_other, early, early_other)
    outs = [o.reshape(-1) if o.shape[0] == 1 else o for o in outs]
    return (block_out, wave, grad_mix, grad_skip, grad_enc, *outs)


def solution(mesh):
    frames, channels = P("tm", None), P("src")
    in_specs = (
        frames, frames, frames, P(), P(None, "src"), channels, channels, channels, channels, P(None, "src"), channels,
        channels, channels, channels, P("src", None), P(), P(), P(None, "src"), channels, P(), frames, P(None, "tm"),
    )
    out_specs = (
        frames, P(None, "tm"), frames, frames, frames, P(None, "src"), channels, channels, channels, channels,
        P(None, "src"), channels, channels, channels, channels, P("src", None), P(), P(), P(None, "src"), channels,
        P(),
    )
    return jax.shard_map(local, mesh=mesh, in_specs=in_specs, out_specs=out_specs, check_vma=False)
```

```python
import functools

import jax
import jax.numpy as jnp
from jax import lax
from jax.experimental import pallas as pl
from jax.experimental.pallas import tpu as pltpu
from jax.sharding import PartitionSpec as P

L = 16
STRIDE = L // 2
HIDDEN = 512
STEP = 128
EPS = 1e-05
T = 256
T1 = 512
TM = 512
ROWS = 32
LANES = 128
F32 = jnp.float32
BF16 = jnp.bfloat16
NVEC = 16
PACK_IN = 128 + NVEC
PACK = PACK_IN + 512
EARLY = 584
VMEM = 63 * 2**20 + 2**19
LOG2E = 1.4426950408889634


def split(x):
    hi = x.astype(BF16)
    return hi, (x - hi.astype(F32)).astype(BF16)


def mm(a, b):
    return lax.dot_general(a, b, (((1,), (0,)), ((), ())), preferred_element_type=F32)


def mm_tn(a, b):
    return lax.dot_general(a, b, (((0,), (0,)), ((), ())), preferred_element_type=F32)


def mm_nt(a, b):
    return lax.dot_general(a, b, (((1,), (1,)), ((), ())), preferred_element_type=F32)


def cat(parts, axis):
    return jnp.concatenate(parts, axis=axis)


def three(x, axis):
    hi, lo = x
    return cat([hi, lo, hi], axis)


def two_of(x, axis):
    hi, lo = x
    return cat([hi, hi, lo], axis)


def iota(shape, axis):
    return lax.broadcasted_iota(jnp.int32, shape, axis)


def sigmoid(x):
    return 1.0 / (1.0 + jnp.exp2(x * -LOG2E))


def colsum(x):
    return jnp.sum(x, axis=0, keepdims=True)


def fold(x):
    total = x[0:8]
    for i in range(8, x.shape[0], 8):
        total = total + x[i : i + 8]
    return total


def plus(a, b):
    return b if a is None else a + b


def column(c):
    return slice(c * LANES, (c + 1) * LANES)


def ones_block(rows):
    return jnp.where(iota((rows, LANES), 1) < 3, 1.0, 0.0).astype(BF16)


def bias_rows(bias, rows):
    hi, lo = split(bias)
    low = (bias - hi.astype(F32) - lo.astype(F32)).astype(BF16)
    place = iota((rows, bias.shape[1]), 0)
    zero = jnp.zeros((rows, bias.shape[1]), F32)
    out = jnp.where(place == 0, hi.astype(F32), zero)
    out = jnp.where(place == 1, lo.astype(F32), out)
    return jnp.where(place == 2, low.astype(F32), out).astype(BF16)


def item_ends(len_ref):
    ends, total = [], jnp.int32(0)
    for k in range(len_ref.shape[0]):
        total = total + len_ref[k]
        ends.append(total)
    return ends


def boundary(ends, start):
    ahead = jnp.where(start - STEP >= 0, 0, -1)
    for end in ends:
        ahead = ahead + (end <= start - STEP).astype(jnp.int32)
    edge = jnp.int32(0)
    for k, end in enumerate(ends):
        edge = jnp.where(ahead == k, end, edge)
    return edge, ahead


def item_rows(ahead, items):
    return jnp.maximum(ahead, 0), jnp.minimum(ahead + 1, items - 1)


def lane_items(ahead, items):
    lane = iota((1, LANES), 1)
    return (lane == ahead).astype(F32), (lane == ahead + 1).astype(F32)


def put_statistics(msg_ref, sums, squares, counts, onehot):
    groups = sums.shape[0]
    count = counts[:, :1]
    safe = jnp.maximum(count, 1.0)
    total = jnp.sum(jnp.sum(sums, axis=0), axis=1, keepdims=True)
    number = count * (groups * LANES)
    mean = total / jnp.maximum(number, 1.0)
    spread = 0.0
    for g in range(groups):
        away = sums[g] / safe - mean
        spread = spread + squares[g] + count * away * away
    spread = jnp.sum(spread, axis=1, keepdims=True)
    item_sum = colsum(onehot * total)
    item_number = colsum(onehot * number)
    item_mean = item_sum / jnp.maximum(item_number, 1.0)
    away = mean - item_mean
    item_spread = colsum(onehot * (spread + number * away * away))
    msg = cat(
        [item_sum, item_spread, item_number, item_mean, jnp.zeros((4, LANES), F32)], 0
    )
    for i in range(msg_ref.shape[0]):
        msg_ref[i] = msg


def to_rows(row, items_padded):
    wide = jnp.broadcast_to(row, (items_padded, LANES))
    own = iota((items_padded, LANES), 0) == iota((items_padded, LANES), 1)
    column = jnp.sum(jnp.where(own, wide, 0.0), axis=1, keepdims=True)
    return jnp.broadcast_to(column, (items_padded, LANES))


def merge_statistics(msg_ref, table_ref):
    msg = msg_ref[...]
    item_sum = jnp.sum(msg[:, 0:1, :], axis=0)
    number = jnp.sum(msg[:, 2:3, :], axis=0)
    mean = item_sum / jnp.maximum(number, 1.0)
    away = msg[:, 3:4, :] - mean[None]
    squares = jnp.sum(msg[:, 1:2, :] + msg[:, 2:3, :] * away * away, axis=0)
    inverse = lax.rsqrt(squares / jnp.maximum(number, 1.0) + EPS)
    padded = table_ref.shape[1]
    table_ref[0] = to_rows(mean, padded)
    table_ref[1] = to_rows(inverse, padded)


def put_entry(refs, groups, entry, sums, squares, number, hot):
    sums_ref, squares_ref, counts_ref, onehot_ref = refs
    row = pl.ds(entry, 1)
    for g in range(groups):
        sums_ref[g, row, :] = sums[g]
        squares_ref[g, row, :] = squares[g]
    counts_ref[row, :] = jnp.full((1, LANES), number, F32)
    onehot_ref[row, :] = hot


def general_entries(refs, acts, after, before, n_after, n_before, entry, ahead):
    hot_b, hot_a = lane_items(ahead, 0)
    for part, keep, number, hot in ((0, before, n_before, hot_b), (1, after, n_after, hot_a)):
        sums, squares = [], []
        for act in acts:
            total = colsum(jnp.where(keep, act, 0.0))
            away = act - total / jnp.maximum(number, 1.0)
            sums.append(total)
            squares.append(colsum(jnp.where(keep, away * away, 0.0)))
        put_entry(refs, len(acts), 2 * entry + part, sums, squares, number, hot)


def prep_kernel(
    top_ref, bottom_ref, cot_ref, w_in_ref, w_out_ref, w_mask_ref, b_in, slope_in, gain_in, beta_in, w_depth, b_depth,
    slope_mid, gain_mid, beta_mid, b_mask, pack_ref, wide_ref, low_ref, high_ref,
):
    pack_ref[0:128, :] = w_in_ref[...]
    vectors = (b_in, slope_in, gain_in, beta_in, w_depth, b_depth, slope_mid, gain_mid, beta_mid)
    bias = b_mask[...]
    pack_ref[128:144, :] = cat(
        [ref[...] for ref in vectors] + [bias[:, 0:128], bias[:, 128:256], jnp.zeros((3, LANES), F32)], 0
    )
    for k in range(2):
        wide_ref[128 * k : 128 * (k + 1), :] = w_out_ref[:, column(k)]
        wide_ref[128 * (k + 2) : 128 * (k + 3), :] = w_mask_ref[:, column(k)]
    low_ref[0:T, :] = top_ref[...]
    low_ref[T : T + 8, :] = cat([cot_ref[...], jnp.zeros((6, LANES), F32)], 0)
    high_ref[...] = bottom_ref[...]


def first_kernel(len_ref, mix_ref, w_in_ref, b_in, slope_in, msg_ref, sums, squares, counts, onehot):
    step = pl.program_id(0)
    last = pl.num_programs(0) - 1
    tiles = mix_ref.shape[0] // T1
    ends = item_ends(len_ref)
    weights = two_of(split(w_in_ref[...]), 0)
    slope = slope_in[...]
    keep = 1.0 - slope
    bias = b_in[...]
    refs = (sums, squares, counts, onehot)
    for t in range(tiles):
        j = step * tiles + t
        start = lax.axis_index("tm") * ((last + 1) * tiles * T1) + j * T1
        edge, ahead = boundary(ends, start)
        hidden = mm(three(split(mix_ref[t * T1 : (t + 1) * T1, :]), 1), weights)
        pieces, total = [], None
        for i in range(0, T1, ROWS):
            x = hidden[i : i + ROWS] + bias
            act = x * (slope + keep * sigmoid(x))
            pieces.append(act)
            total = plus(total, fold(act))
        total = colsum(total)
        mean = total / T1
        square = None
        for act in pieces:
            away = act - mean
            square = plus(square, fold(away * away))
        put_entry(refs, 1, 2 * j, [total], [colsum(square)], jnp.float32(T1), lane_items(ahead, 0)[0])
        nothing = jnp.zeros((1, LANES), F32)
        put_entry(refs, 1, 2 * j + 1, [nothing], [nothing], jnp.float32(0.0), nothing)

        @pl.when(edge < start + T1)
        def _():
            offset = iota((T1, LANES), 0) + (start - edge)
            n_before = jnp.clip(edge - start, 0, T1).astype(F32)
            act = cat(pieces, 0)
            general_entries(refs, [act], offset >= 0, offset < 0, T1 - n_before, n_before, j, ahead)

    @pl.when(step == last)
    def _():
        put_statistics(msg_ref, sums[...], squares[...], counts[...], onehot[...])


def depth_kernel(
    len_ref, msg_in_ref, mix_ref, prev_ref, next_ref, own_ref, core_ref, x_ref, far_ref,
    hidden_ref, depth_ref, msg_ref, vec_ref, table_ref,
    gathered, sems, weights, ring, sums, squares, counts, onehot,
):
    m = pl.program_id(0)
    last = pl.num_programs(0) - 1
    items = len_ref.shape[0]
    me = lax.axis_index("src")
    half = me & 1
    own_rows = (last - 1) * T

    @pl.when(m == 0)
    def _():
        copies = [
            pltpu.make_async_copy(ref, gathered.at[half ^ k], sems.at[k])
            for k, ref in enumerate((own_ref, core_ref, x_ref, far_ref))
        ]
        for copy in copies:
            copy.start()
        merge_statistics(msg_in_ref, table_ref)
        for ref in (sums, squares, counts, onehot):
            ref[...] = jnp.zeros_like(ref)
        for copy in copies:
            copy.wait()
        for s in range(4):
            cut = column(s)
            weights[0:384, cut] = two_of(split(gathered[s, 0:128, :]), 0)
            weights[384:512, cut] = bias_rows(gathered[s, 128:129, :], 128)
            vec_ref[:, cut] = gathered[s, 128 : 128 + NVEC, :]

    def vec(row, c):
        return vec_ref[row : row + 1, column(c)]

    ends = item_ends(len_ref)
    base = lax.axis_index("tm") * (2 * own_rows) + half * own_rows
    start = base + (m - 1) * T
    edge, ahead = boundary(ends, start)
    alone = edge >= start + T
    block = half * (own_rows // T) + m - 1
    top = 2 * (own_rows // T)
    new, old = m & 1, 1 - (m & 1)

    def norm_rows(alone):
        place = pl.multiple_of(jnp.clip(block, 0, top - 1) * T, T)
        mix = mix_ref[pl.ds(place, T), :]
        mix = jnp.where(block < 0, prev_ref[...], jnp.where(block >= top, next_ref[0:T, :], mix))
        mixed = split(mix)
        hidden = mm(cat([mixed[0], mixed[1], mixed[0], ones_block(T)], 1), weights[...])
        hidden_ref[...] = hidden
        row_b, row_a = item_rows(ahead, items)
        rows = iota((ROWS, LANES), 0) + (start - edge)
        for c in range(4):
            slope = vec(1, c)
            keep = 1.0 - slope
            scale_b = table_ref[1, pl.ds(row_b, 1), :] * vec(2, c)
            shift_b = vec(3, c) - table_ref[0, pl.ds(row_b, 1), :] * scale_b
            scale_a = table_ref[1, pl.ds(row_a, 1), :] * vec(2, c)
            shift_a = vec(3, c) - table_ref[0, pl.ds(row_a, 1), :] * scale_a
            for i in range(0, T, ROWS):
                x = hidden[i : i + ROWS, column(c)]
                act = x * (slope + keep * sigmoid(x))
                if alone:
                    value = act * scale_b + shift_b
                else:
                    after = rows + i >= 0
                    value = act * jnp.where(after, scale_a, scale_b) + jnp.where(after, shift_a, shift_b)
                ring[new, i : i + ROWS, column(c)] = value

    pl.when(alone)(lambda: norm_rows(True))
    pl.when(jnp.logical_not(alone))(lambda: norm_rows(False))

    begin = start - STEP
    edge2, ahead2 = boundary(ends, begin)
    plain = edge2 >= begin + T + STEP
    refs = (sums, squares, counts, onehot)

    def filtered(c, i, lower_weight, upper_weight):
        lower = ring[old, i : i + ROWS, column(c)]
        upper = ring[new, i : i + ROWS, column(c)]
        if i < STEP:
            middle = ring[old, i + STEP : i + STEP + ROWS, column(c)]
        else:
            middle = ring[new, i - STEP : i - STEP + ROWS, column(c)]
        return lower_weight * lower + vec(5, c) * middle + upper_weight * upper + vec(7, c)

    @pl.when((m > 0) & plain)
    def _():
        in_low = jnp.where(m > 1, 1.0, 0.0)
        in_high = jnp.where(m < last, 1.0, 0.0)
        number = STEP * (in_low + in_high)
        all_sums, all_squares = [], []
        for c in range(4):
            slope = vec(8, c)
            keep = 1.0 - slope
            acts, halves = [], [None, None]
            for i in range(0, T, ROWS):
                depth = filtered(c, i, vec(4, c), vec(6, c))
                depth_ref[i : i + ROWS, column(c)] = depth
                act = depth * (slope + keep * sigmoid(depth))
                acts.append(act)
                halves[i // STEP] = plus(halves[i // STEP], fold(act))
            total = in_low * colsum(halves[0]) + in_high * colsum(halves[1])
            mean = total / number
            halves = [None, None]
            for i, act in enumerate(acts):
                away = act - mean
                halves[i * ROWS // STEP] = plus(halves[i * ROWS // STEP], fold(away * away))
            all_sums.append(total)
            all_squares.append(in_low * colsum(halves[0]) + in_high * colsum(halves[1]))
        put_entry(refs, 4, 2 * (m - 1), all_sums, all_squares, number, lane_items(ahead2, 0)[0])

    @pl.when((m > 0) & jnp.logical_not(plain))
    def _():
        low = jnp.where(m == 1, STEP, 0)
        high = jnp.where(m == last, STEP, T)
        rows = iota((ROWS, LANES), 0) + (begin - edge2)
        acts = []
        for c in range(4):
            slope = vec(8, c)
            pieces = []
            for i in range(0, T, ROWS):
                offset = rows + i
                lower_weight = jnp.where((offset >= 0) & (offset < STEP), 0.0, vec(4, c))
                upper_weight = jnp.where((offset < 0) & (offset >= -STEP), 0.0, vec(6, c))
                depth = filtered(c, i, lower_weight, upper_weight)
                depth_ref[i : i + ROWS, column(c)] = depth
                pieces.append(depth * (slope + (1.0 - slope) * sigmoid(depth)))
            acts.append(cat(pieces, 0))
        row = iota((T, LANES), 0)
        own = (row >= low) & (row < high)
        offset = row + (begin - edge2)
        n_before = jnp.clip(edge2 - begin, low, high) - low
        n_after = (high - low - n_before).astype(F32)
        general_entries(
            refs, acts, own & (offset >= 0), own & (offset < 0), n_after, n_before.astype(F32), m - 1, ahead2
        )

    @pl.when(m == last)
    def _():
        put_statistics(msg_ref, sums[...], squares[...], counts[...], onehot[...])


def mask_kernel(
    len_ref, msg_in_ref, *refs,
):
    depth_refs = refs[: TM // STEP]
    (
        mix_ref, skip_ref, enc_ref, cot_ref, wave_cot_ref, wave_next_ref, edge_next_ref, basis_ref, vec_ref,
        b_out_ref, slope_skip_ref, own_ref, core_ref, x_ref, far_ref,
        block_ref, grad_skip_ref, grad_enc_ref, send_ref, wave_ref, r_ref, up_ref, down_ref, keep_ref, give_ref,
        msg_ref, table_ref,
        gathered, sems, w_out, w_out_t, w_mask, w_mask_t, decode, basis_back, select_hi, select_lo, normed_ref,
        pull_ref, carry, acc_out, acc_mask, acc_basis, acc_vec,
        acc_small, entries, onehot,
    ) = refs[TM // STEP :]
    j = pl.program_id(0)
    last = pl.num_programs(0) - 1
    items = len_ref.shape[0]
    me = lax.axis_index("src")
    half = me & 1
    side = me >> 1
    own_rows = (last + 1) * TM

    def vec(row, c):
        return vec_ref[row : row + 1, column(c)]

    @pl.when(j == 0)
    def _():
        copies = [
            pltpu.make_async_copy(ref, gathered.at[half ^ k], sems.at[k])
            for k, ref in enumerate((own_ref, core_ref, x_ref, far_ref))
        ]
        for copy in copies:
            copy.start()
        merge_statistics(msg_in_ref, table_ref)
        for ref in (acc_out, acc_mask, acc_basis, acc_vec, acc_small, carry, entries):
            ref[...] = jnp.zeros_like(ref)
        basis = split(basis_ref[...])
        b_hi, b_lo = basis
        col = iota((L, 2 * LANES), 1)
        row = iota((L, 2 * LANES), 0)
        spread = ((col & 7) == (row & 7)) & ((col >> 7) == (row >> 3))
        spread = spread.astype(F32).astype(BF16)
        wide = (mm_tn(b_hi, spread).astype(BF16), mm_tn(b_lo, spread).astype(BF16))
        for n in range(2):
            decode[n] = two_of([part[n * 256 : (n + 1) * 256] for part in wide], 0)
        for c in range(2):
            row = iota((LANES, L), 0) - 48 * c
            col = iota((LANES, L), 1)
            with_hi = ((row == col) | (row == col + 32)).astype(F32).astype(BF16)
            with_lo = (row == col + 16).astype(F32).astype(BF16)
            back = mm(with_hi, b_hi) + mm(with_lo, b_lo)
            basis_back[:, c * HIDDEN : (c + 1) * HIDDEN] = back.astype(BF16)
            row = iota((2 * LANES, LANES), 0)
            col = iota((2 * LANES, LANES), 1) - 48 * c
            place = (row & 7) + ((row >> 7) << 3)
            select_hi[c] = ((col == place) | (col == place + 16)).astype(F32).astype(BF16)
            select_lo[c] = (col == place + 32).astype(F32).astype(BF16)
        for copy in copies:
            copy.wait()
        for s in range(4):
            cut = column(s)
            for k in range(2):
                part = gathered[s, column(k), :]
                hi, lo = split(part)
                for place, value in ((0, hi), (256, hi), (512, lo)):
                    place = place + (s >> 1) * 768 + (s & 1) * 128
                    w_out[place : place + 128, column(k)] = value
                hi, lo = split(part.T)
                for place, value in ((0, hi), (256, hi), (512, lo)):
                    w_out_t[place + k * 128 : place + (k + 1) * 128, cut] = value
                part = gathered[s, column(2 + k), :]
                wide = slice(s * 256 + k * LANES, s * 256 + (k + 1) * LANES)
                w_mask[0:384, wide] = two_of(split(part * -LOG2E), 0)
                w_mask[384:512, wide] = bias_rows(vec_ref[11 + k : 12 + k, cut] * -LOG2E, 128)
                hi, lo = split(part.T)
                for place in (0, 256):
                    w_mask_t[s >> 1, s & 1, place + k * 128 : place + (k + 1) * 128, 0:128] = hi
                    w_mask_t[s >> 1, s & 1, place + k * 128 : place + (k + 1) * 128, 128:256] = lo

    ends = item_ends(len_ref)
    start = lax.axis_index("tm") * (2 * own_rows) + half * own_rows + j * TM
    edge, ahead = boundary(ends, start)
    row_b, row_a = item_rows(ahead, items)
    offset = iota((TM, LANES), 0) + (start - edge)

    after = offset >= 0
    inv_b, inv_a = table_ref[1, pl.ds(row_b, 1), :], table_ref[1, pl.ds(row_a, 1), :]
    shift_b, shift_a = -inv_b * table_ref[0, pl.ds(row_b, 1), :], -inv_a * table_ref[0, pl.ds(row_a, 1), :]
    inv = jnp.where(after, inv_a, inv_b)
    shift = jnp.where(after, shift_a, shift_b)
    norms = [[], []], [[], []]
    for c in range(4):
        slope = vec(8, c)
        keep = 1.0 - slope
        his, los = [], []
        for i in range(0, TM, ROWS):
            rows = slice(i, i + ROWS)
            depth = depth_refs[i // STEP][i % STEP : i % STEP + ROWS, column(c)]
            s = sigmoid(depth)
            part = keep * s
            mild = slope + part
            normed = depth * mild * inv[rows] + shift[rows]
            normed_ref[rows, column(c)] = normed
            pull_ref[rows, column(c)] = mild + part * (depth * (1.0 - s))
            hi, lo = split(normed * vec(9, c) + vec(10, c))
            his.append(hi)
            los.append(lo)
        norms[c >> 1][0].append(cat(his, 0))
        norms[c >> 1][1].append(cat(los, 0))
    branch = [
        mm(cat(his + los + his, 1), w_out[768 * k : 768 * (k + 1), :]) for k, (his, los) in enumerate(norms)
    ]
    branch = branch[0] + branch[1]
    slope_skip = slope_skip_ref[...]
    keep = 1.0 - slope_skip
    totals, skips, actives = [], [], []
    for i in range(0, TM, ROWS):
        rows = slice(i, i + ROWS)
        block = mix_ref[rows, :] + (branch[rows, 0:128] + b_out_ref[:, 0:128])
        block_ref[rows, :] = block
        send_ref[rows, 0:128] = block
        total = skip_ref[rows, :] + (branch[rows, 128:256] + b_out_ref[:, 128:256])
        s = sigmoid(total)
        part = keep * s
        mild = slope_skip + part
        rest = total * (1.0 - s)
        totals.append(rest)
        skips.append(mild + part * rest)
        actives.append(split(total * mild))
    a_hi, a_lo = cat([a for a, _ in actives], 0), cat([a for _, a in actives], 0)
    query = cat([a_hi, a_lo, a_hi, ones_block(TM)], 1)

    lane_frame = iota((16, LANES), 1) >> 3
    frame = iota((16, LANES), 0)
    here = jnp.where(lane_frame == frame, 1.0, 0.0)
    coming = jnp.where(lane_frame == ((frame + 1) & 15), 1.0, 0.0)
    final_row = frame == 15
    packed = None
    waves = [wave_cot_ref[0:1, :], wave_cot_ref[1:2, :]]
    finals = [
        jnp.where((half == 1) & (j == last), edge_next_ref[T + c : T + c + 1, :], wave_next_ref[c : c + 1, :])
        for c in range(2)
    ]
    for c in range(2):
        wave = jnp.where(side == 0, waves[c], waves[1 - c])
        final = jnp.where(side == 0, finals[c], finals[1 - c])
        for part, select in zip(split(cat([wave, final], 1)), (select_hi, select_lo)):
            part = part.astype(F32)
            lines = [part[:, column(q)] for q in range(TM // 16 + 1)]
            pieces = []
            for q in range(TM // 16):
                following = jnp.where(final_row, lines[q + 1], lines[q]) * coming
                pieces.append(cat([lines[q] * here, following], 1).astype(BF16))
            packed = plus(packed, mm(cat(pieces, 0), select[c]))
    lane = iota((1, LANES), 1)
    lane = jnp.where(lane < 48, lane, lane - 48)
    packed = jnp.where((offset == -1) & ((lane & 15) >= 8), 0.0, packed).astype(BF16)

    decoded = [None, None]
    back = [None, None]
    masked, grads_hi, grads_lo = [[], []], [], []
    chunks = [[slice(c * HIDDEN + n * 256, c * HIDDEN + (n + 1) * 256) for c in range(2)] for n in range(2)]
    all_grads = [[mm(packed, basis_back[:, chunk]) for chunk in pair] for pair in chunks]
    all_logits = [[mm(query, w_mask[:, chunk]) for chunk in pair] for pair in chunks]
    for n in range(2):
        logits, grads = all_logits[n], all_grads[n]
        blocks = [[[], []] for _ in range(4)]
        for b in range(2):
            col = column(2 * n + b)
            bias_sum = None
            pieces = [[[], []] for _ in range(4)]
            for i in range(0, TM, ROWS):
                rows = slice(i, i + ROWS)
                enc = enc_ref[rows, col]
                grad_enc = None
                for c in range(2):
                    mask = 1.0 / (1.0 + jnp.exp2(logits[c][rows, column(b)]))
                    grad = grads[c][rows, column(b)]
                    grad_enc = plus(grad_enc, grad * mask)
                    value = mask * enc
                    for k, part in enumerate(split(value)):
                        pieces[c][k].append(part)
                    grad_logits = grad * value * (1.0 - mask)
                    if c == 0:
                        bias_sum = plus(bias_sum, fold(grad_logits))
                    for k, part in enumerate(split(grad_logits)):
                        pieces[2 + c][k].append(part)
                grad_enc_ref[rows, col] = grad_enc
                send_ref[rows, 256 + (2 * n + b) * 128 : 256 + (2 * n + b + 1) * 128] = grad_enc
            acc_vec[2:3, (2 * n + b) * 128 : (2 * n + b + 1) * 128] += colsum(bias_sum)
            for block, piece in zip(blocks, pieces):
                for k in range(2):
                    block[k].append(cat(piece[k], 0))
        for c in range(2):
            hi, lo = blocks[c]
            masked[c].append(cat(hi + lo, 1))
            decoded[c] = plus(decoded[c], mm(cat(hi + lo + hi, 1), decode[n]))
            hi, lo = blocks[2 + c]
            back[c] = plus(back[c], mm(cat(hi + lo, 1), w_mask_t[c, n]))
            if c == 0:
                grads_hi = grads_hi + hi
                grads_lo = grads_lo + lo
    back = back[0] + back[1]
    own_grads = cat(grads_hi + grads_lo, 1)

    pieces, along, cot_sum, skip_sum = [], None, None, None
    for k, i in enumerate(range(0, TM, ROWS)):
        rows = slice(i, i + ROWS)
        grad_active = back[rows, 0:128] + back[rows, 128:256]
        grad_skip = grad_active * skips[k]
        along = plus(along, fold(grad_active * totals[k]))
        grad_skip_ref[rows, :] = grad_skip
        send_ref[rows, 128:256] = grad_skip
        cot = cot_ref[rows, :]
        cot_sum = plus(cot_sum, fold(cot))
        skip_sum = plus(skip_sum, fold(grad_skip))
        pieces.append(split(cat([cot, grad_skip], 1)))
    acc_small[0:1, :] += colsum(along)
    acc_small[1:2, :] += colsum(cot_sum)
    acc_small[2:3, :] += colsum(skip_sum)
    g_hi, g_lo = cat([p for p, _ in pieces], 0), cat([p for _, p in pieces], 0)
    r_ref[...] = mm(three((g_hi, g_lo), 1), w_out_t[...])

    first_row = iota((8, LANES), 0) == 0
    waves = []
    for c in range(2):
        tail = decoded[c][:, 128:256]
        shifted = pltpu.roll(tail, 1, 0)
        shifted = cat([jnp.where(first_row, carry[c : c + 1, :], shifted[0:8]), shifted[8:]], 0)
        carry[c : c + 1, :] = tail[TM - 1 : TM, :]
        value = decoded[c][:, 0:128] + jnp.where(offset == 0, 0.0, shifted)
        lines = []
        for q in range(TM // 16):
            line = value[q * 16 : (q + 1) * 16] * here
            lines.append(colsum(line[0:8] + line[8:16]))
        waves.append(cat(lines, 1))
    wave_ref[0:1, :] = jnp.where(side == 0, waves[0], waves[1])
    wave_ref[1:2, :] = jnp.where(side == 0, waves[1], waves[0])

    @pl.when(j == 0)
    def _():
        down_ref[...] = r_ref[0:128, :]

    @pl.when(j == last)
    def _():
        up_ref[0:128, :] = r_ref[TM - 128 : TM, :]
        up_ref[128:136, :] = jnp.zeros((8, HIDDEN), F32)
        up_ref[128:129, 0:128] = jnp.where(side == 0, carry[0:1, :], carry[1:2, :])
        up_ref[129:130, 0:128] = jnp.where(side == 0, carry[1:2, :], carry[0:1, :])

    own_norms = cat(norms[0][0] + norms[0][1] + norms[0][0], 1)

    def weight_gradients(rows):
        for n in range(2):
            for c in range(2):
                values = masked[c][n]
                acc_basis[c, :, 256 * n : 256 * (n + 1)] += mm_tn(
                    cat([packed[rows]] * 2, 0), cat([values[rows, 0:256], values[rows, 256:512]], 0)
                )
            yield
        acc_mask[...] += mm_tn(
            three((a_hi[rows], a_lo[rows]), 0), two_of((own_grads[rows, 0:512], own_grads[rows, 512:1024]), 0)
        )
        yield
        acc_out[...] += mm_tn(
            cat([own_norms[rows, 256 * k : 256 * (k + 1)] for k in range(3)], 0), two_of((g_hi[rows], g_lo[rows]), 0)
        )
        yield

    for k in range(TM // T):
        rows = slice(k * T, (k + 1) * T)
        begin = start + k * T
        edge2, ahead2 = boundary(ends, begin)
        plain = edge2 >= begin + T + STEP
        entry = 2 * (j * (TM // T) + k)
        hot_b, hot_a = lane_items(ahead2, items)
        onehot[pl.ds(entry, 1), :] = hot_b
        onehot[pl.ds(entry + 1, 1), :] = hot_a
        row_b2, row_a2 = item_rows(ahead2, items)

        @pl.when(plain)
        def _():
            products = weight_gradients(rows)
            inverse = table_ref[1, pl.ds(row_b2, 1), :]
            lines = [[None] * 8, [None] * 8]
            for c in range(4):
                next(products)
                taps = vec(4, c) + vec(5, c) + vec(6, c)
                level = vec(7, c) + vec(3, c) * taps
                sums = [None] * 8
                for i in range(k * T, (k + 1) * T, ROWS):
                    cut = slice(i, i + ROWS)
                    r, normed, pull = r_ref[cut, column(c)], normed_ref[cut, column(c)], pull_ref[cut, column(c)]
                    depth = depth_refs[i // STEP][i % STEP : i % STEP + ROWS, column(c)] - level
                    pull_r, pull_n = pull * r, pull * normed
                    values = (
                        r, r * normed, pull_r, pull, pull_n, pull_r * depth, pull * depth, pull_n * depth,
                    )
                    sums = [plus(s, fold(value)) for s, value in zip(sums, values)]
                sums = [colsum(s) for s in sums]
                if c < 2:
                    acc_vec[0:1, column(c)] += sums[1]
                    acc_vec[1:2, column(c)] += sums[0]
                gain, flat = vec(9, c), vec(2, c) * taps * inverse
                scales = (gain, gain, flat * gain, flat, flat, inverse * gain, inverse, inverse)
                lines[c >> 1] = [plus(line, s * scale) for line, s, scale in zip(lines[c >> 1], sums, scales)]
            for i in range(8):
                entries[i, pl.ds(entry, 1), :] = lines[0][i] + lines[1][i]

        @pl.when(jnp.logical_not(plain))
        def _():
            products = weight_gradients(rows)
            place = iota((ROWS, LANES), 0) + (begin - k * T - edge2)
            inv_b, inv_a = table_ref[1, pl.ds(row_b2, 1), :], table_ref[1, pl.ds(row_a2, 1), :]
            before, behind = [None] * 8, [None] * 8
            for c in range(4):
                next(products)
                sum_r, sum_rn = None, None
                for i in range(k * T, (k + 1) * T, ROWS):
                    cut = slice(i, i + ROWS)
                    offset = place + i
                    after = offset >= 0
                    taps = jnp.where(after & (offset < STEP), 0.0, vec(4, c)) + vec(5, c)
                    taps = taps + jnp.where((offset < 0) & (offset >= -STEP), 0.0, vec(6, c))
                    r, normed = r_ref[cut, column(c)], normed_ref[cut, column(c)]
                    pull = pull_ref[cut, column(c)] * jnp.where(after, inv_a, inv_b)
                    depth = depth_refs[i // STEP][i % STEP : i % STEP + ROWS, column(c)]
                    flat = pull * (vec(2, c) * taps)
                    cross = pull * (depth - vec(7, c) - vec(3, c) * taps)
                    r_normed = r * normed
                    sum_r, sum_rn = plus(sum_r, fold(r)), plus(sum_rn, fold(r_normed))
                    q = r * vec(9, c)
                    values = (
                        q, q * normed, flat * q, flat, flat * normed, cross * q, cross, cross * normed,
                    )
                    before = [plus(s, fold(jnp.where(after, 0.0, value))) for s, value in zip(before, values)]
                    behind = [plus(s, fold(jnp.where(after, value, 0.0))) for s, value in zip(behind, values)]
                if c < 2:
                    acc_vec[0:1, column(c)] += colsum(sum_rn)
                    acc_vec[1:2, column(c)] += colsum(sum_r)
            for i in range(8):
                entries[i, pl.ds(entry, 1), :] = colsum(before[i])
                entries[i, pl.ds(entry + 1, 1), :] = colsum(behind[i])

    @pl.when(j == last)
    def _():
        hot = onehot[...]
        lines = [colsum(hot * jnp.sum(entries[i], axis=1, keepdims=True)) for i in range(8)]
        msg = cat(lines, 0)
        for i in range(msg_ref.shape[0]):
            msg_ref[i] = msg
        for ref, h in ((keep_ref, half), (give_ref, 1 - half)):
            own = pl.ds(pl.multiple_of(h * 128, 128), 128)
            ref[0:128, :] = acc_out[own, 0:128]
            ref[128:256, :] = acc_out[own, 128:256]
            for k in range(2):
                pair = pl.ds(pl.multiple_of(h * 256 + k * 128, 128), 128)
                ref[256 + 128 * k : 384 + 128 * k, :] = acc_mask[:, pair]
            bias = acc_vec[2:3, pl.ds(pl.multiple_of(h * 256, 256), 256)]
            ref[512:520, :] = cat(
                [
                    bias[:, 0:128], bias[:, 128:256], acc_vec[0:1, own], acc_vec[1:2, own],
                    acc_small[0:3, :], jnp.zeros((1, LANES), F32),
                ], 0,
            )
            for k in range(4):
                cut = column(k)
                ref[520 + 16 * k : 536 + 16 * k, :] = (acc_basis[0, 0:16, cut] + acc_basis[0, 32:48, cut]) + (
                    acc_basis[1, 48:64, cut] + acc_basis[1, 80:96, cut]
                )


def back_kernel(
    len_ref, msg_in_ref, depth_ref, r_a_ref, r_b_ref, low_ref, high_ref, hidden_ref, mix_ref, cot_ref,
    vec_ref, table_in_ref, table_mid_ref, own_ref, core_ref, x_ref, far_ref,
    grad_mix_ref, send_ref, keep_ref, give_ref, edge_ref,
    gathered, sems, table, weights, ring, acc_w, acc_vec,
):
    j = pl.program_id(0)
    last = pl.num_programs(0) - 1
    items = len_ref.shape[0]
    me = lax.axis_index("src")
    half = me & 1
    side = me >> 1
    own_rows = last * T

    def vec(row, c):
        return vec_ref[row : row + 1, column(c)]

    ends = item_ends(len_ref)

    @pl.when(j == 0)
    def _():
        copies = [
            pltpu.make_async_copy(ref.at[pl.ds(0, 128)], gathered.at[half ^ k], sems.at[k])
            for k, ref in enumerate((own_ref, core_ref, x_ref, far_ref))
        ]
        for copy in copies:
            copy.start()
        totals = 0.5 * jnp.sum(msg_in_ref[...], axis=0)
        lane = iota((1, LANES), 1)
        number = jnp.zeros((1, LANES), jnp.int32)
        for k in range(items):
            number = jnp.where(lane == k, len_ref[k], number)
        number = jnp.maximum(number.astype(F32) * HIDDEN, 1.0)
        m1 = totals[0:1] / number
        m2 = totals[1:2] / number
        p1 = (totals[2:3] - m1 * totals[3:4] - m2 * totals[4:5]) / number
        p2 = (totals[5:6] - m1 * totals[6:7] - m2 * totals[7:8]) / number
        padded = table.shape[1]
        for i, value in enumerate((m1, m2, p1, p2)):
            table[i] = to_rows(value, padded)
        acc_w[...] = jnp.zeros_like(acc_w)
        acc_vec[...] = jnp.zeros_like(acc_vec)
        edge_ref[...] = low_ref[128:136, 0:128]
        for copy in copies:
            copy.wait()
        for s in range(4):
            cut = column(s)
            hi, lo = split(gathered[s].T)
            for place in (0, 256):
                place = place + (s >> 1) * 512 + (s & 1) * 128
                weights[place : place + 128, 0:128] = hi
                weights[place : place + 128, 128:256] = lo

    base = lax.axis_index("tm") * (2 * own_rows) + half * own_rows
    new, old = j & 1, 1 - (j & 1)

    def chooser(begin, alone, edge, ahead):
        row_b, row_a = item_rows(ahead, items)

        def pick(ref, i):
            value_b = ref[i, pl.ds(row_b, 1), :]
            return value_b, value_b if alone else ref[i, pl.ds(row_a, 1), :]

        def choose(pair, i):
            if alone:
                return pair[0]
            return jnp.where(iota((ROWS, LANES), 0) + (begin - edge) + i >= 0, pair[1], pair[0])

        return pick, choose

    begin = base + j * T - STEP
    edge, ahead = boundary(ends, begin)
    alone = edge >= begin + T

    def filter_rows(alone):
        pick, choose = chooser(begin, alone, edge, ahead)
        means, inverses = pick(table_mid_ref, 0), pick(table_mid_ref, 1)
        firsts, seconds = pick(table, 0), pick(table, 1)
        shifts = tuple(-a * b for a, b in zip(means, inverses))
        firsts = tuple(a * b for a, b in zip(firsts, inverses))
        seconds = tuple(a * b for a, b in zip(seconds, inverses))
        for c in range(4):
            slope, gain = vec(8, c), vec(9, c)
            keep = 1.0 - slope
            halves = [None, None]
            for i in range(0, T, ROWS):
                if i < STEP:
                    r = jnp.where(j == 0, low_ref[i : i + ROWS, column(c)], r_a_ref[i : i + ROWS, column(c)])
                else:
                    cut = slice(i - STEP, i - STEP + ROWS)
                    r = jnp.where(j == last, high_ref[cut, column(c)], r_b_ref[cut, column(c)])
                depth = depth_ref[i : i + ROWS, column(c)]
                s = sigmoid(depth)
                u = depth * (1.0 - s)
                part = keep * s
                mild = slope + part
                inv = choose(inverses, i)
                normed = depth * mild * inv + choose(shifts, i)
                grad_act = r * (gain * inv) - choose(firsts, i) - normed * choose(seconds, i)
                if c < 2:
                    halves[i // STEP] = plus(halves[i // STEP], fold(grad_act * u))
                ring[new, i : i + ROWS, column(c)] = grad_act * (mild + part * u)
            if c < 2:
                in_low = jnp.where(j > 0, 1.0, 0.0)
                in_high = jnp.where(j < last, 1.0, 0.0)
                acc_vec[8:9, column(c)] += in_low * colsum(halves[0]) + in_high * colsum(halves[1])

    pl.when(alone)(lambda: filter_rows(True))
    pl.when(jnp.logical_not(alone))(lambda: filter_rows(False))

    start = base + (j - 1) * T
    edge2, ahead2 = boundary(ends, start)
    plain = edge2 >= start + T + STEP

    def norm_rows(plain):
        pick, choose = chooser(start, plain, edge2, ahead2)
        means, inverses = pick(table_in_ref, 0), pick(table_in_ref, 1)
        firsts, seconds = pick(table, 2), pick(table, 3)
        shifts = tuple(-a * b for a, b in zip(means, inverses))
        firsts = tuple(a * b for a, b in zip(firsts, inverses))
        seconds = tuple(a * b for a, b in zip(seconds, inverses))
        rows = iota((ROWS, LANES), 0) + (start - edge2)
        his, los = [[], [], [], []], [[], [], [], []]
        for c in range(4):
            slope, gain, bias = vec(1, c), vec(2, c), vec(3, c)
            keep = 1.0 - slope
            sums = [None] * 8
            for i in range(0, T, ROWS):
                cut = slice(i, i + ROWS)
                grad_low, grad_high = ring[old, cut, column(c)], ring[new, cut, column(c)]
                if i < STEP:
                    grad_mid = ring[old, i + STEP : i + STEP + ROWS, column(c)]
                else:
                    grad_mid = ring[new, i - STEP : i - STEP + ROWS, column(c)]
                if not plain:
                    offset = rows + i
                    grad_low = jnp.where((offset >= 0) & (offset < STEP), 0.0, grad_low)
                    grad_high = jnp.where((offset < 0) & (offset >= -STEP), 0.0, grad_high)
                grad_norm = vec(5, c) * grad_mid + vec(4, c) * grad_high + vec(6, c) * grad_low
                hidden = hidden_ref[cut, column(c)]
                s = sigmoid(hidden)
                u = hidden * (1.0 - s)
                part = keep * s
                mild = slope + part
                inv = choose(inverses, i)
                normed = hidden * mild * inv + choose(shifts, i)
                grad_act = grad_norm * (gain * inv) - choose(firsts, i) - normed * choose(seconds, i)
                grad_hidden = grad_act * (mild + part * u)
                if c < 2:
                    norm = normed * gain + bias
                    values = (
                        grad_hidden, grad_act * u, grad_norm * normed, grad_norm, norm * grad_high, norm * grad_mid,
                        norm * grad_low, grad_mid,
                    )
                    sums = [plus(s, fold(value)) for s, value in zip(sums, values)]
                hi, lo = split(grad_hidden)
                his[c].append(hi)
                los[c].append(lo)
            if c < 2:
                acc_vec[0:8, column(c)] += cat([colsum(s) for s in sums], 0)
        hi, lo = [cat(p, 0) for p in his], [cat(p, 0) for p in los]
        own = mm(cat(hi[0:2] + lo[0:2], 1), weights[0:512, :])
        back = own + mm(cat(hi[2:4] + lo[2:4], 1), weights[512:1024, :])
        grad_mix = cot_ref[...] + (back[:, 0:128] + back[:, 128:256])
        grad_mix_ref[...] = grad_mix
        send_ref[...] = grad_mix
        mixed = cat(split(mix_ref[...]), 1)
        acc_w[...] += mm_tn(cat([cat(hi[0:2], 1), cat(lo[0:2], 1)], 1), mixed)

    pl.when((j > 0) & plain)(lambda: norm_rows(True))
    pl.when((j > 0) & jnp.logical_not(plain))(lambda: norm_rows(False))

    @pl.when(j == last)
    def _():
        for ref, h in ((keep_ref, half), (give_ref, 1 - half)):
            own = pl.ds(pl.multiple_of(h * 128, 128), 128)
            rest = pl.ds(pl.multiple_of(256 + h * 128, 128), 128)
            ref[0:128, :] = (acc_w[own, 0:128] + (acc_w[own, 128:256] + acc_w[rest, 0:128])).T
            ref[128:144, :] = acc_vec[:, own]


def pass_kernel(len_ref, got_ref, block_in, skip_in, enc_in, block_ref, skip_ref, enc_ref):
    block_ref[...] = got_ref[:, 0:128]
    skip_ref[...] = got_ref[:, 128:256]
    enc_ref[...] = got_ref[:, 256:768]


def merge_kernel(len_ref, got_ref, mix_in, mine_ref, other_ref, edge_ref, edge_other_ref, mix_ref, wave_ref):
    me = lax.axis_index("src")
    half = me & 1
    mix_ref[...] = got_ref[...]
    width = mine_ref.shape[1]
    frames = width // STRIDE
    base = lax.axis_index("tm") * (2 * frames)
    ends = item_ends(len_ref)
    lane = iota((2, LANES), 1)
    for part, edge, h in ((mine_ref, edge_ref, half), (other_ref, edge_other_ref, 1 - half)):
        place = base + h * frames
        new = place == 0
        for end in ends:
            new = new | (end == place)
        place = pl.multiple_of(h * width, width)
        wave_ref[:, pl.ds(place, width)] = part[...]
        first = part[:, 0:128] + jnp.where((lane < STRIDE) & jnp.logical_not(new), edge[0:2, :], 0.0)
        wave_ref[:, pl.ds(place, LANES)] = first


def last_kernel(
    a_ref, b_ref, c_ref, d_ref, w_in, b_in, slope_in, gain_in, beta_in, w_depth, b_depth, slope_mid,
    gain_mid, beta_mid, w_out, b_out, slope_skip, w_mask, b_mask, basis,
):
    late = a_ref[...] + b_ref[...]
    w_in[...] = late[0:128]
    for ref, row in (
        (b_in, 128), (slope_in, 129), (gain_in, 130), (beta_in, 131), (b_depth, 135), (slope_mid, 136),
    ):
        ref[...] = late[row : row + 1]
    w_depth[...] = late[132:135]
    early = c_ref[...] + d_ref[...]
    w_out[:, 0:128] = early[0:128]
    w_out[:, 128:256] = early[128:256]
    w_mask[:, 0:128] = early[256:384]
    w_mask[:, 128:256] = early[384:512]
    b_mask[:, 0:128] = early[512:513]
    b_mask[:, 128:256] = early[513:514]
    gain_mid[...] = early[514:515]
    beta_mid[...] = early[515:516]
    slope_skip[...] = early[516:517]
    b_out[:, 0:128] = early[517:518]
    b_out[:, 128:256] = early[518:519]
    for k in range(4):
        basis[:, column(k)] = early[520 + 16 * k : 536 + 16 * k]


def local(
    mix_in, skip_in, encoded, lengths, w_in, b_in, slope_in, gain_in, beta_in, w_depth, b_depth, slope_mid, gain_mid,
    beta_mid, w_out, b_out, slope_skip, w_mask, b_mask, basis, cot_out, cot_wave,
):
    n_tm, n_src = lax.axis_size("tm"), lax.axis_size("src")
    devices = n_tm * n_src
    frames = mix_in.shape[0]
    own_rows = frames // 2
    items = lengths.shape[0]
    padded = -(-items // 8) * 8
    tiles = own_rows // T
    tiles_m = own_rows // TM
    up = [(i, i + 1) for i in range(n_tm - 1)]
    down = [(j, i) for i, j in up]
    swap = [(i, i ^ 1) for i in range(n_src)]
    cross = [(i, i ^ 2) for i in range(n_src)]

    def half():
        return lax.axis_index("src") & 1

    def struct(*shape):
        return jax.ShapeDtypeStruct(shape, F32)

    def whole(*shape):
        zeros = (0,) * len(shape)
        return pl.BlockSpec(shape, lambda i, n: zeros)

    anywhere = pl.BlockSpec(memory_space=pl.ANY)

    def vmem(*shape):
        return pltpu.VMEM(shape, F32)

    def vmem16(*shape):
        return pltpu.VMEM(shape, BF16)

    def call(kernel, name, grid, in_specs, out_specs, out_shape, scratch, us, **kw):
        return pl.pallas_call(
            kernel,
            grid_spec=pltpu.PrefetchScalarGridSpec(
                num_scalar_prefetch=1, grid=(grid,), in_specs=in_specs, out_specs=out_specs, scratch_shapes=scratch
            ),
            out_shape=out_shape,
            compiler_params=pltpu.CompilerParams(
                vmem_limit_bytes=VMEM, dimension_semantics=("arbitrary",)
            ),
            cost_estimate=pl.CostEstimate(flops=0, bytes_accessed=us * 3_600_000, transcendentals=0),
            name=name,
            **kw,
        )

    msg_shape = (devices, 8, LANES)
    message = struct(*msg_shape)

    def exchange(msg):
        return lax.all_to_all(msg, ("tm", "src"), 0, 0)

    def line(vector):
        return vector.reshape(1, -1)

    def fixed(*shape):
        return pl.BlockSpec(shape, lambda i: (0,) * len(shape))

    n1 = frames // T1
    vectors = (
        line(b_in), line(slope_in), line(gain_in), line(beta_in), w_depth, line(b_depth), line(slope_mid),
        line(gain_mid), line(beta_mid), line(b_mask),
    )
    pack, wide, low, high = pl.pallas_call(
        prep_kernel,
        grid=(1,),
        in_specs=[
            fixed(T, 128), pl.BlockSpec((T, 128), lambda i: (frames // T - 1, 0)), fixed(2, LANES), fixed(128, 128),
            fixed(128, 256), fixed(128, 256), *[fixed(*v.shape) for v in vectors],
        ],
        out_specs=[fixed(PACK_IN, 128), fixed(512, 128), fixed(T + 8, 128), fixed(T, 128)],
        out_shape=[struct(PACK_IN, 128), struct(512, 128), struct(T + 8, 128), struct(T, 128)],
        compiler_params=pltpu.CompilerParams(vmem_limit_bytes=VMEM),
        name="prep",
    )(mix_in, mix_in, cot_wave, w_in, w_out, w_mask, *vectors)
    pack_x = lax.ppermute(pack, "src", cross)
    pack_core = lax.ppermute(pack, "src", swap)
    mix_prev = lax.ppermute(high, "tm", up)
    mix_next = lax.ppermute(low, "tm", down)
    msg1 = call(
        first_kernel, "first", 2,
        [pl.BlockSpec((frames // 2, 128), lambda i, n: (i, 0)), whole(128, 128), whole(1, 128), whole(1, 128)],
        whole(*msg_shape), message,
        [vmem(1, 2 * n1, 128), vmem(1, 2 * n1, 128), vmem(2 * n1, 128), vmem(2 * n1, 128)], 4,
    )(lengths, mix_in, w_in, line(b_in), line(slope_in))
    msg1, pack_x, pack_core, mix_prev, mix_next = lax.optimization_barrier(
        (msg1, pack_x, pack_core, mix_prev, mix_next)
    )
    pack_far = lax.ppermute(pack_x, "src", swap)
    packs = (pack, pack_core, pack_x, pack_far)
    msg1 = exchange(msg1)
    wide_x = lax.ppermute(wide, "src", cross)
    wide_core = lax.ppermute(wide, "src", swap)
    wide_far = lax.ppermute(wide_x, "src", swap)
    wides = (wide, wide_core, wide_x, wide_far)

    entries = -(-2 * (tiles + 1) // 8) * 8
    hidden, depth, msg2, vec, table_in = call(
        depth_kernel, "depth", tiles + 2,
        [
            whole(*msg_shape),
            whole(frames, 128), whole(T, 128), whole(T + 8, 128), anywhere, anywhere, anywhere, anywhere,
        ],
        [
            pl.BlockSpec((T, HIDDEN), lambda i, n: (i, 0)),
            pl.BlockSpec((T, HIDDEN), lambda i, n: (jnp.maximum(i - 1, 0), 0)),
            whole(*msg_shape), whole(NVEC, HIDDEN), whole(2, padded, LANES),
        ],
        [
            struct(own_rows + 2 * T, HIDDEN), struct(own_rows + T, HIDDEN), message, struct(NVEC, HIDDEN),
            struct(2, padded, LANES),
        ],
        [
            vmem(4, PACK_IN, 128), pltpu.SemaphoreType.DMA((4,)), vmem16(512, HIDDEN), vmem(2, T, HIDDEN),
            vmem(4, entries, 128), vmem(4, entries, 128), vmem(entries, 128), vmem(entries, 128),
        ], 8,
    )(lengths, msg1, mix_in, mix_prev, mix_next, *packs)
    msg2 = exchange(msg2)

    def half_rows(width):
        return pl.BlockSpec((TM, width), lambda i, n: (half() * tiles_m + i, 0))

    def rows_m(width):
        return pl.BlockSpec((TM, width), lambda i, n: (i, 0))

    def depth_piece(k):
        return pl.BlockSpec((STEP, HIDDEN), lambda i, n: (TM // STEP * i + 1 + k, 0))

    pieces = TM // STEP
    (block_out, grad_skip, grad_enc, send, wave_half, r, r_up, r_down, keep, give, msg3, table_mid) = call(
        mask_kernel, "mask", tiles_m,
        [
            whole(*msg_shape), *[depth_piece(k) for k in range(pieces)],
            half_rows(128), half_rows(128), half_rows(HIDDEN), half_rows(128),
            pl.BlockSpec((2, TM * STRIDE), lambda i, n: (0, half() * tiles_m + i)),
            pl.BlockSpec(
                (2, LANES),
                lambda i, n: (0, jnp.minimum((half() * tiles_m + i + 1) * (TM // 16), (2 * tiles_m) * (TM // 16) - 1)),
            ),
            whole(T + 8, 128), whole(L, HIDDEN), whole(NVEC, HIDDEN), whole(1, 256), whole(1, 128),
            anywhere, anywhere, anywhere, anywhere,
        ],
        [
            half_rows(128), half_rows(128), half_rows(HIDDEN), rows_m(768),
            pl.BlockSpec((2, TM * STRIDE), lambda i, n: (0, i)),
            rows_m(HIDDEN), whole(136, HIDDEN), whole(128, HIDDEN), whole(EARLY, 128), whole(EARLY, 128),
            whole(*msg_shape), whole(2, padded, LANES),
        ],
        [
            struct(frames, 128), struct(frames, 128), struct(frames, HIDDEN), struct(own_rows, 768),
            struct(2, own_rows * STRIDE), struct(own_rows, HIDDEN), struct(136, HIDDEN), struct(128, HIDDEN),
            struct(EARLY, 128), struct(EARLY, 128), message, struct(2, padded, LANES),
        ],
        [
            vmem(4, 512, 128), pltpu.SemaphoreType.DMA((4,)), vmem16(1536, 256), vmem16(768, HIDDEN),
            vmem16(512, 1024), vmem16(2, 2, 512, 256), vmem16(2, 768, 256), vmem16(128, 1024), vmem16(2, 256, 128),
            vmem16(2, 256, 128), vmem(TM, HIDDEN), vmem(TM, HIDDEN), vmem(8, 128), vmem(256, 256), vmem(128, HIDDEN),
            vmem(2, 128, HIDDEN), vmem(8, HIDDEN), vmem(8, 128),
            vmem(8, 2 * tiles, 128), vmem(2 * tiles, 128),
        ], 28,
    )(
        lengths, msg2, *[depth] * pieces, mix_in, skip_in, encoded, cot_out, cot_wave, cot_wave, mix_next, basis.T, vec,
        line(b_out), line(slope_skip), *wides,
    )

    both = ("tm", "src")
    later, earlier = [], []
    for i in range(n_tm):
        for s in range(n_src):
            here = i * n_src + s
            there = here + 1 if s % 2 == 0 else (i + 1) * n_src + s - 1
            if s % 2 == 0 or i + 1 < n_tm:
                later.append((here, there))
                earlier.append((there, here))
    hops = [[(i, i ^ (1 << bit)) for i in range(n_tm)] for bit in range(n_tm.bit_length() - 1)]
    early = keep + lax.ppermute(give, "src", swap)
    got_low = lax.ppermute(r_up, both, later)
    got_high = lax.ppermute(r_down, both, earlier)
    msg3 = exchange(msg3)
    early_other = lax.ppermute(early, "tm", hops[0])
    msg3, got_low, got_high, early, early_other, send, wave_half = lax.optimization_barrier(
        (msg3, got_low, got_high, early, early_other, send, wave_half)
    )
    early = early + early_other
    early_other = lax.ppermute(early, "tm", hops[-1])
    got = lax.ppermute(send, "src", swap)
    wave_other = lax.ppermute(wave_half, "src", swap)

    def rows(width):
        return pl.BlockSpec((T, width), lambda i, n: (i, 0))

    def own_tile(width):
        return pl.BlockSpec((T, width), lambda i, n: (half() * tiles + jnp.maximum(i - 1, 0), 0))

    def other_rows(width):
        return pl.BlockSpec((own_rows // 2, width), lambda i, n: ((1 - half()) * 2 + i, 0))

    grad_mix, mix_send, keep, give, edge = call(
        back_kernel, "back", tiles + 1,
        [
            whole(*msg_shape), rows(HIDDEN),
            pl.BlockSpec((STEP, HIDDEN), lambda i, n: (jnp.maximum(2 * i - 1, 0), 0)),
            pl.BlockSpec((STEP, HIDDEN), lambda i, n: (jnp.minimum(2 * i, 2 * tiles - 1), 0)),
            whole(136, HIDDEN), whole(128, HIDDEN),
            pl.BlockSpec((T, HIDDEN), lambda i, n: (jnp.maximum(i, 1), 0)), own_tile(128), own_tile(128),
            whole(NVEC, HIDDEN), whole(2, padded, LANES), whole(2, padded, LANES),
            anywhere, anywhere, anywhere, anywhere,
        ],
        [
            own_tile(128), pl.BlockSpec((T, 128), lambda i, n: (jnp.maximum(i - 1, 0), 0)),
            whole(144, 128), whole(144, 128), whole(8, 128),
        ],
        [
            struct(frames, 128), struct(own_rows, 128), struct(144, 128), struct(144, 128), struct(8, 128),
        ],
        [
            vmem(4, 128, 128), pltpu.SemaphoreType.DMA((4,)), vmem(4, padded, LANES), vmem16(1024, 256),
            vmem(2, T, HIDDEN), vmem(512, 256), vmem(16, HIDDEN),
        ], 13,
    )(
        lengths, msg3, depth, r, r, got_low, got_high, hidden, mix_in, cot_out, vec, table_in, table_mid, *packs,
    )

    grad_mix, mix_send, keep, give, edge, early, early_other = lax.optimization_barrier(
        (grad_mix, mix_send, keep, give, edge, early, early_other)
    )
    late = keep + lax.ppermute(give, "src", swap)
    mix_got = lax.ppermute(mix_send, "src", swap)
    edge_other = lax.ppermute(edge, "src", swap)
    late_other = lax.ppermute(late, "tm", hops[-1])
    early = early + early_other
    early_other = lax.ppermute(early, "tm", hops[1])
    block_out, grad_skip, grad_enc = call(
        pass_kernel, "pass", 2,
        [pl.BlockSpec((own_rows // 2, 768), lambda i, n: (i, 0)), anywhere, anywhere, anywhere],
        [other_rows(128), other_rows(128), other_rows(HIDDEN)],
        [struct(frames, 128), struct(frames, 128), struct(frames, HIDDEN)], [], 4,
        input_output_aliases={2: 0, 3: 1, 4: 2},
    )(lengths, got, block_out, grad_skip, grad_enc)
    late, late_other, block_out, grad_skip, grad_enc = lax.optimization_barrier(
        (late, late_other, block_out, grad_skip, grad_enc)
    )
    late = late + late_other
    late_other = lax.ppermute(late, "tm", hops[0])
    wave_width = own_rows * STRIDE
    grad_mix, wave = call(
        merge_kernel, "merge", 1,
        [
            whole(own_rows, 128), anywhere, whole(2, wave_width), whole(2, wave_width), whole(8, 128), whole(8, 128),
        ],
        [pl.BlockSpec((own_rows, 128), lambda i, n: (1 - half(), 0)), whole(2, 2 * wave_width)],
        [struct(frames, 128), struct(2, 2 * wave_width)], [], 2,
        input_output_aliases={2: 0},
    )(lengths, mix_got, grad_mix, wave_half, wave_other, edge, edge_other)
    late, late_other, grad_mix, wave = lax.optimization_barrier((late, late_other, grad_mix, wave))
    for hop in hops[1:-1]:
        late = late + late_other
        late_other = lax.ppermute(late, "tm", hop)
    for hop in hops[2:-1]:
        early = early + early_other
        early_other = lax.ppermute(early, "tm", hop)

    outs = pl.pallas_call(
        last_kernel,
        in_specs=[pl.BlockSpec(memory_space=pltpu.VMEM)] * 4,
        out_shape=[
            struct(128, 128), struct(1, 128), struct(1, 128), struct(1, 128), struct(1, 128), struct(3, 128),
            struct(1, 128), struct(1, 128), struct(1, 128), struct(1, 128), struct(128, 256), struct(1, 256),
            struct(1, 128), struct(128, 256), struct(1, 256), struct(L, HIDDEN),
        ],
        compiler_params=pltpu.CompilerParams(vmem_limit_bytes=VMEM),
        name="last",
    )(late, late_other, early, early_other)
    outs = [o.reshape(-1) if o.shape[0] == 1 else o for o in outs[:-1]] + [outs[-1].T]
    return (block_out, wave, grad_mix, grad_skip, grad_enc, *outs)


def solution(mesh):
    frames, channels = P("tm", None), P("src")
    in_specs = (
        frames, frames, frames, P(), P(None, "src"), channels, channels, channels, channels, P(None, "src"), channels,
        channels, channels, channels, P("src", None), P(), P(), P(None, "src"), channels, P(), frames, P(None, "tm"),
    )
    out_specs = (
        frames, P(None, "tm"), frames, frames, frames, P(None, "src"), channels, channels, channels, channels,
        P(None, "src"), channels, channels, channels, channels, P("src", None), P(), P(), P(None, "src"), channels,
        P(),
    )
    return jax.shard_map(local, mesh=mesh, in_specs=in_specs, out_specs=out_specs, check_vma=False)
```

```python
import functools

import jax
import jax.numpy as jnp
from jax import lax
from jax.experimental import pallas as pl
from jax.experimental.pallas import tpu as pltpu
from jax.sharding import PartitionSpec as P

L = 16
STRIDE = L // 2
HIDDEN = 512
STEP = 128
EPS = 1e-05
T = 256
T1 = 512
TM = 512
ROWS = 32
LANES = 128
F32 = jnp.float32
BF16 = jnp.bfloat16
NVEC = 16
PACK_IN = 128 + NVEC
PACK = PACK_IN + 512
EARLY = 584
VMEM = 64 * 2**20 - 2**15
LOG2E = 1.4426950408889634


def split(x):
    hi = x.astype(BF16)
    return hi, (x - hi.astype(F32)).astype(BF16)


def mm(a, b):
    return lax.dot_general(a, b, (((1,), (0,)), ((), ())), preferred_element_type=F32)


def mm_tn(a, b):
    return lax.dot_general(a, b, (((0,), (0,)), ((), ())), preferred_element_type=F32)


def mm_nt(a, b):
    return lax.dot_general(a, b, (((1,), (1,)), ((), ())), preferred_element_type=F32)


def cat(parts, axis):
    return jnp.concatenate(parts, axis=axis)


def three(x, axis):
    hi, lo = x
    return cat([hi, lo, hi], axis)


def two_of(x, axis):
    hi, lo = x
    return cat([hi, hi, lo], axis)


def iota(shape, axis):
    return lax.broadcasted_iota(jnp.int32, shape, axis)


def sigmoid(x):
    return 1.0 / (1.0 + jnp.exp2(x * -LOG2E))


def colsum(x):
    return jnp.sum(x, axis=0, keepdims=True)


def fold(x):
    total = x[0:8]
    for i in range(8, x.shape[0], 8):
        total = total + x[i : i + 8]
    return total


def plus(a, b):
    return b if a is None else a + b


def column(c):
    return slice(c * LANES, (c + 1) * LANES)


def ones_block(rows):
    return jnp.where(iota((rows, LANES), 1) < 3, 1.0, 0.0).astype(BF16)


def bias_rows(bias, rows):
    hi, lo = split(bias)
    low = (bias - hi.astype(F32) - lo.astype(F32)).astype(BF16)
    place = iota((rows, bias.shape[1]), 0)
    zero = jnp.zeros((rows, bias.shape[1]), F32)
    out = jnp.where(place == 0, hi.astype(F32), zero)
    out = jnp.where(place == 1, lo.astype(F32), out)
    return jnp.where(place == 2, low.astype(F32), out).astype(BF16)


def item_ends(len_ref):
    ends, total = [], jnp.int32(0)
    for k in range(len_ref.shape[0]):
        total = total + len_ref[k]
        ends.append(total)
    return ends


def boundary(ends, start):
    ahead = jnp.where(start - STEP >= 0, 0, -1)
    for end in ends:
        ahead = ahead + (end <= start - STEP).astype(jnp.int32)
    edge = jnp.int32(0)
    for k, end in enumerate(ends):
        edge = jnp.where(ahead == k, end, edge)
    return edge, ahead


def item_rows(ahead, items):
    return jnp.maximum(ahead, 0), jnp.minimum(ahead + 1, items - 1)


def lane_items(ahead, items):
    lane = iota((1, LANES), 1)
    return (lane == ahead).astype(F32), (lane == ahead + 1).astype(F32)


def put_statistics(msg_ref, sums, squares, counts, onehot):
    groups = sums.shape[0]
    count = counts[:, :1]
    safe = jnp.maximum(count, 1.0)
    total = jnp.sum(jnp.sum(sums, axis=0), axis=1, keepdims=True)
    number = count * (groups * LANES)
    mean = total / jnp.maximum(number, 1.0)
    spread = 0.0
    for g in range(groups):
        away = sums[g] / safe - mean
        spread = spread + squares[g] + count * away * away
    spread = jnp.sum(spread, axis=1, keepdims=True)
    item_sum = colsum(onehot * total)
    item_number = colsum(onehot * number)
    item_mean = item_sum / jnp.maximum(item_number, 1.0)
    away = mean - item_mean
    item_spread = colsum(onehot * (spread + number * away * away))
    msg = cat(
        [item_sum, item_spread, item_number, item_mean, jnp.zeros((4, LANES), F32)], 0
    )
    for i in range(msg_ref.shape[0]):
        msg_ref[i] = msg


def to_rows(row, items_padded):
    wide = jnp.broadcast_to(row, (items_padded, LANES))
    own = iota((items_padded, LANES), 0) == iota((items_padded, LANES), 1)
    column = jnp.sum(jnp.where(own, wide, 0.0), axis=1, keepdims=True)
    return jnp.broadcast_to(column, (items_padded, LANES))


def merge_statistics(msg_ref, table_ref):
    msg = msg_ref[...]
    item_sum = jnp.sum(msg[:, 0:1, :], axis=0)
    number = jnp.sum(msg[:, 2:3, :], axis=0)
    mean = item_sum / jnp.maximum(number, 1.0)
    away = msg[:, 3:4, :] - mean[None]
    squares = jnp.sum(msg[:, 1:2, :] + msg[:, 2:3, :] * away * away, axis=0)
    inverse = lax.rsqrt(squares / jnp.maximum(number, 1.0) + EPS)
    padded = table_ref.shape[1]
    table_ref[0] = to_rows(mean, padded)
    table_ref[1] = to_rows(inverse, padded)


def put_entry(refs, groups, entry, sums, squares, number, hot):
    sums_ref, squares_ref, counts_ref, onehot_ref = refs
    row = pl.ds(entry, 1)
    for g in range(groups):
        sums_ref[g, row, :] = sums[g]
        squares_ref[g, row, :] = squares[g]
    counts_ref[row, :] = jnp.full((1, LANES), number, F32)
    onehot_ref[row, :] = hot


def general_entries(refs, acts, after, before, n_after, n_before, entry, ahead):
    hot_b, hot_a = lane_items(ahead, 0)
    for part, keep, number, hot in ((0, before, n_before, hot_b), (1, after, n_after, hot_a)):
        sums, squares = [], []
        for act in acts:
            total = colsum(jnp.where(keep, act, 0.0))
            away = act - total / jnp.maximum(number, 1.0)
            sums.append(total)
            squares.append(colsum(jnp.where(keep, away * away, 0.0)))
        put_entry(refs, len(acts), 2 * entry + part, sums, squares, number, hot)


def prep_kernel(
    top_ref, bottom_ref, cot_ref, w_in_ref, w_out_ref, w_mask_ref, b_in, slope_in, gain_in, beta_in, w_depth, b_depth,
    slope_mid, gain_mid, beta_mid, b_mask, pack_ref, wide_ref, low_ref, high_ref,
):
    pack_ref[0:128, :] = w_in_ref[...]
    vectors = (b_in, slope_in, gain_in, beta_in, w_depth, b_depth, slope_mid, gain_mid, beta_mid)
    bias = b_mask[...]
    pack_ref[128:144, :] = cat(
        [ref[...] for ref in vectors] + [bias[:, 0:128], bias[:, 128:256], jnp.zeros((3, LANES), F32)], 0
    )
    for k in range(2):
        wide_ref[128 * k : 128 * (k + 1), :] = w_out_ref[:, column(k)]
        wide_ref[128 * (k + 2) : 128 * (k + 3), :] = w_mask_ref[:, column(k)]
    low_ref[0:T, :] = top_ref[...]
    low_ref[T : T + 8, :] = cat([cot_ref[...], jnp.zeros((6, LANES), F32)], 0)
    high_ref[...] = bottom_ref[...]


def first_kernel(len_ref, mix_ref, w_in_ref, b_in, slope_in, msg_ref, sums, squares, counts, onehot):
    step = pl.program_id(0)
    last = pl.num_programs(0) - 1
    tiles = mix_ref.shape[0] // T1
    ends = item_ends(len_ref)
    weights = two_of(split(w_in_ref[...]), 0)
    slope = slope_in[...]
    keep = 1.0 - slope
    bias = b_in[...]
    refs = (sums, squares, counts, onehot)
    for t in range(tiles):
        j = step * tiles + t
        start = lax.axis_index("tm") * ((last + 1) * tiles * T1) + j * T1
        edge, ahead = boundary(ends, start)
        hidden = mm(three(split(mix_ref[t * T1 : (t + 1) * T1, :]), 1), weights)
        pieces, total = [], None
        for i in range(0, T1, ROWS):
            x = hidden[i : i + ROWS] + bias
            act = x * (slope + keep * sigmoid(x))
            pieces.append(act)
            total = plus(total, fold(act))
        total = colsum(total)
        mean = total / T1
        square = None
        for act in pieces:
            away = act - mean
            square = plus(square, fold(away * away))
        put_entry(refs, 1, 2 * j, [total], [colsum(square)], jnp.float32(T1), lane_items(ahead, 0)[0])
        nothing = jnp.zeros((1, LANES), F32)
        put_entry(refs, 1, 2 * j + 1, [nothing], [nothing], jnp.float32(0.0), nothing)

        @pl.when(edge < start + T1)
        def _():
            offset = iota((T1, LANES), 0) + (start - edge)
            n_before = jnp.clip(edge - start, 0, T1).astype(F32)
            act = cat(pieces, 0)
            general_entries(refs, [act], offset >= 0, offset < 0, T1 - n_before, n_before, j, ahead)

    @pl.when(step == last)
    def _():
        put_statistics(msg_ref, sums[...], squares[...], counts[...], onehot[...])


def depth_kernel(
    len_ref, msg_in_ref, mix_ref, prev_ref, next_ref, own_ref, core_ref, x_ref, far_ref,
    hidden_ref, depth_ref, msg_ref, vec_ref, table_ref,
    gathered, sems, weights, ring, sums, squares, counts, onehot,
):
    m = pl.program_id(0)
    last = pl.num_programs(0) - 1
    items = len_ref.shape[0]
    me = lax.axis_index("src")
    half = me & 1
    own_rows = (last - 1) * T

    @pl.when(m == 0)
    def _():
        copies = [
            pltpu.make_async_copy(ref, gathered.at[half ^ k], sems.at[k])
            for k, ref in enumerate((own_ref, core_ref, x_ref, far_ref))
        ]
        for copy in copies:
            copy.start()
        merge_statistics(msg_in_ref, table_ref)
        for ref in (sums, squares, counts, onehot):
            ref[...] = jnp.zeros_like(ref)
        for copy in copies:
            copy.wait()
        for s in range(4):
            cut = column(s)
            weights[0:384, cut] = two_of(split(gathered[s, 0:128, :]), 0)
            weights[384:512, cut] = bias_rows(gathered[s, 128:129, :], 128)
            vec_ref[:, cut] = gathered[s, 128 : 128 + NVEC, :]

    def vec(row, c):
        return vec_ref[row : row + 1, column(c)]

    ends = item_ends(len_ref)
    base = lax.axis_index("tm") * (2 * own_rows) + half * own_rows
    start = base + (m - 1) * T
    edge, ahead = boundary(ends, start)
    alone = edge >= start + T
    block = half * (own_rows // T) + m - 1
    top = 2 * (own_rows // T)
    new, old = m & 1, 1 - (m & 1)

    def norm_rows(alone):
        place = pl.multiple_of(jnp.clip(block, 0, top - 1) * T, T)
        mix = mix_ref[pl.ds(place, T), :]
        mix = jnp.where(block < 0, prev_ref[...], jnp.where(block >= top, next_ref[0:T, :], mix))
        mixed = split(mix)
        hidden = mm(cat([mixed[0], mixed[1], mixed[0], ones_block(T)], 1), weights[...])
        hidden_ref[...] = hidden
        row_b, row_a = item_rows(ahead, items)
        rows = iota((ROWS, LANES), 0) + (start - edge)
        for c in range(4):
            slope = vec(1, c)
            keep = 1.0 - slope
            scale_b = table_ref[1, pl.ds(row_b, 1), :] * vec(2, c)
            shift_b = vec(3, c) - table_ref[0, pl.ds(row_b, 1), :] * scale_b
            scale_a = table_ref[1, pl.ds(row_a, 1), :] * vec(2, c)
            shift_a = vec(3, c) - table_ref[0, pl.ds(row_a, 1), :] * scale_a
            for i in range(0, T, ROWS):
                x = hidden[i : i + ROWS, column(c)]
                act = x * (slope + keep * sigmoid(x))
                if alone:
                    value = act * scale_b + shift_b
                else:
                    after = rows + i >= 0
                    value = act * jnp.where(after, scale_a, scale_b) + jnp.where(after, shift_a, shift_b)
                ring[new, i : i + ROWS, column(c)] = value

    pl.when(alone)(lambda: norm_rows(True))
    pl.when(jnp.logical_not(alone))(lambda: norm_rows(False))

    begin = start - STEP
    edge2, ahead2 = boundary(ends, begin)
    plain = edge2 >= begin + T + STEP
    refs = (sums, squares, counts, onehot)

    def filtered(c, i, lower_weight, upper_weight):
        lower = ring[old, i : i + ROWS, column(c)]
        upper = ring[new, i : i + ROWS, column(c)]
        if i < STEP:
            middle = ring[old, i + STEP : i + STEP + ROWS, column(c)]
        else:
            middle = ring[new, i - STEP : i - STEP + ROWS, column(c)]
        return lower_weight * lower + vec(5, c) * middle + upper_weight * upper + vec(7, c)

    @pl.when((m > 0) & plain)
    def _():
        in_low = jnp.where(m > 1, 1.0, 0.0)
        in_high = jnp.where(m < last, 1.0, 0.0)
        number = STEP * (in_low + in_high)
        all_sums, all_squares = [], []
        for c in range(4):
            slope = vec(8, c)
            keep = 1.0 - slope
            acts, halves = [], [None, None]
            for i in range(0, T, ROWS):
                depth = filtered(c, i, vec(4, c), vec(6, c))
                depth_ref[i : i + ROWS, column(c)] = depth
                act = depth * (slope + keep * sigmoid(depth))
                acts.append(act)
                halves[i // STEP] = plus(halves[i // STEP], fold(act))
            total = in_low * colsum(halves[0]) + in_high * colsum(halves[1])
            mean = total / number
            halves = [None, None]
            for i, act in enumerate(acts):
                away = act - mean
                halves[i * ROWS // STEP] = plus(halves[i * ROWS // STEP], fold(away * away))
            all_sums.append(total)
            all_squares.append(in_low * colsum(halves[0]) + in_high * colsum(halves[1]))
        put_entry(refs, 4, 2 * (m - 1), all_sums, all_squares, number, lane_items(ahead2, 0)[0])

    @pl.when((m > 0) & jnp.logical_not(plain))
    def _():
        low = jnp.where(m == 1, STEP, 0)
        high = jnp.where(m == last, STEP, T)
        rows = iota((ROWS, LANES), 0) + (begin - edge2)
        acts = []
        for c in range(4):
            slope = vec(8, c)
            pieces = []
            for i in range(0, T, ROWS):
                offset = rows + i
                lower_weight = jnp.where((offset >= 0) & (offset < STEP), 0.0, vec(4, c))
                upper_weight = jnp.where((offset < 0) & (offset >= -STEP), 0.0, vec(6, c))
                depth = filtered(c, i, lower_weight, upper_weight)
                depth_ref[i : i + ROWS, column(c)] = depth
                pieces.append(depth * (slope + (1.0 - slope) * sigmoid(depth)))
            acts.append(cat(pieces, 0))
        row = iota((T, LANES), 0)
        own = (row >= low) & (row < high)
        offset = row + (begin - edge2)
        n_before = jnp.clip(edge2 - begin, low, high) - low
        n_after = (high - low - n_before).astype(F32)
        general_entries(
            refs, acts, own & (offset >= 0), own & (offset < 0), n_after, n_before.astype(F32), m - 1, ahead2
        )

    @pl.when(m == last)
    def _():
        put_statistics(msg_ref, sums[...], squares[...], counts[...], onehot[...])


def cotangent_kernel(len_ref, wave_cot_ref, wave_next_ref, edge_next_ref, after_ref, packed_ref):
    j = pl.program_id(0)
    last = pl.num_programs(0) - 1
    me = lax.axis_index("src")
    half = me & 1
    side = me >> 1
    own_rows = (last + 1) * TM
    start = lax.axis_index("tm") * (2 * own_rows) + half * own_rows + j * TM
    edge, _ = boundary(item_ends(len_ref), start)
    offset = iota((TM, LANES), 0) + (start - edge)
    selects_hi, selects_lo = [], []
    for c in range(2):
        row = iota((2 * LANES, LANES), 0)
        col = iota((2 * LANES, LANES), 1) - 48 * c
        place = (row & 7) + ((row >> 7) << 3)
        selects_hi.append(((col == place) | (col == place + 16)).astype(F32).astype(BF16))
        selects_lo.append((col == place + 32).astype(F32).astype(BF16))

    lane_frame = iota((16, LANES), 1) >> 3
    frame = iota((16, LANES), 0)
    here = jnp.where(lane_frame == frame, 1.0, 0.0)
    coming = jnp.where(lane_frame == ((frame + 1) & 15), 1.0, 0.0)
    final_row = frame == 15
    packed = None
    waves = [wave_cot_ref[0:1, :], wave_cot_ref[1:2, :]]
    finals = [
        jnp.where((half == 1) & (j == last), edge_next_ref[T + c : T + c + 1, :], wave_next_ref[c : c + 1, :])
        for c in range(2)
    ]
    for c in range(2):
        wave = jnp.where(side == 0, waves[c], waves[1 - c])
        final = jnp.where(side == 0, finals[c], finals[1 - c])
        for part, select in zip(split(cat([wave, final], 1)), (selects_hi, selects_lo)):
            part = part.astype(F32)
            lines = [part[:, column(q)] for q in range(TM // 16 + 1)]
            pieces = []
            for q in range(TM // 16):
                following = jnp.where(final_row, lines[q + 1], lines[q]) * coming
                pieces.append(cat([lines[q] * here, following], 1).astype(BF16))
            packed = plus(packed, mm(cat(pieces, 0), select[c]))
    lane = iota((1, LANES), 1)
    lane = jnp.where(lane < 48, lane, lane - 48)
    packed_ref[...] = jnp.where((offset == -1) & ((lane & 15) >= 8), 0.0, packed).astype(BF16)


def mask_kernel(
    len_ref, msg_in_ref, *refs,
):
    depth_refs = refs[: TM // STEP]
    (
        mix_ref, skip_ref, enc_ref, cot_ref, packed_ref, basis_ref, vec_ref,
        b_out_ref, slope_skip_ref, own_ref, core_ref, x_ref, far_ref,
        block_ref, grad_skip_ref, grad_enc_ref, send_ref, wave_ref, r_ref, up_ref, down_ref, keep_ref, give_ref,
        msg_ref, table_ref,
        gathered, sems, w_out, w_out_t, w_mask, w_mask_t, decode, basis_back, normed_ref,
        pull_ref, carry, acc_out, acc_mask, acc_basis, acc_vec,
        acc_small, entries, onehot,
    ) = refs[TM // STEP :]
    j = pl.program_id(0)
    last = pl.num_programs(0) - 1
    items = len_ref.shape[0]
    me = lax.axis_index("src")
    half = me & 1
    side = me >> 1
    own_rows = (last + 1) * TM

    def vec(row, c):
        return vec_ref[row : row + 1, column(c)]

    @pl.when(j == 0)
    def _():
        copies = [
            pltpu.make_async_copy(ref, gathered.at[half ^ k], sems.at[k])
            for k, ref in enumerate((own_ref, core_ref, x_ref, far_ref))
        ]
        for copy in copies:
            copy.start()
        merge_statistics(msg_in_ref, table_ref)
        for ref in (acc_out, acc_mask, acc_basis, acc_vec, acc_small, carry, entries):
            ref[...] = jnp.zeros_like(ref)
        basis = split(basis_ref[...])
        b_hi, b_lo = basis
        col = iota((L, 2 * LANES), 1)
        row = iota((L, 2 * LANES), 0)
        spread = ((col & 7) == (row & 7)) & ((col >> 7) == (row >> 3))
        spread = spread.astype(F32).astype(BF16)
        wide = (mm_tn(b_hi, spread).astype(BF16), mm_tn(b_lo, spread).astype(BF16))
        for n in range(2):
            decode[n] = two_of([part[n * 256 : (n + 1) * 256] for part in wide], 0)
        for c in range(2):
            row = iota((LANES, L), 0) - 48 * c
            col = iota((LANES, L), 1)
            with_hi = ((row == col) | (row == col + 32)).astype(F32).astype(BF16)
            with_lo = (row == col + 16).astype(F32).astype(BF16)
            back = mm(with_hi, b_hi) + mm(with_lo, b_lo)
            basis_back[:, c * HIDDEN : (c + 1) * HIDDEN] = back.astype(BF16)
        for copy in copies:
            copy.wait()
        for s in range(4):
            cut = column(s)
            for k in range(2):
                part = gathered[s, column(k), :]
                hi, lo = split(part)
                for place, value in ((0, hi), (256, hi), (512, lo)):
                    place = place + (s >> 1) * 768 + (s & 1) * 128
                    w_out[place : place + 128, column(k)] = value
                hi, lo = split(part.T)
                for place, value in ((0, hi), (256, hi), (512, lo)):
                    w_out_t[place + k * 128 : place + (k + 1) * 128, cut] = value
                part = gathered[s, column(2 + k), :]
                wide = slice(s * 256 + k * LANES, s * 256 + (k + 1) * LANES)
                w_mask[0:384, wide] = two_of(split(part * -LOG2E), 0)
                w_mask[384:512, wide] = bias_rows(vec_ref[11 + k : 12 + k, cut] * -LOG2E, 128)
                hi, lo = split(part.T)
                for place in (0, 256):
                    w_mask_t[s >> 1, s & 1, place + k * 128 : place + (k + 1) * 128, 0:128] = hi
                    w_mask_t[s >> 1, s & 1, place + k * 128 : place + (k + 1) * 128, 128:256] = lo

    ends = item_ends(len_ref)
    start = lax.axis_index("tm") * (2 * own_rows) + half * own_rows + j * TM
    edge, ahead = boundary(ends, start)
    row_b, row_a = item_rows(ahead, items)
    offset = iota((TM, LANES), 0) + (start - edge)

    lane_frame = iota((16, LANES), 1) >> 3
    here = jnp.where(lane_frame == iota((16, LANES), 0), 1.0, 0.0)
    packed = packed_ref[...]

    chunks = [[slice(c * HIDDEN + n * 256, c * HIDDEN + (n + 1) * 256) for c in range(2)] for n in range(2)]
    all_grads = [[None, None], [None, None]]
    after = offset >= 0
    inv_b, inv_a = table_ref[1, pl.ds(row_b, 1), :], table_ref[1, pl.ds(row_a, 1), :]
    shift_b, shift_a = -inv_b * table_ref[0, pl.ds(row_b, 1), :], -inv_a * table_ref[0, pl.ds(row_a, 1), :]
    inv = jnp.where(after, inv_a, inv_b)
    shift = jnp.where(after, shift_a, shift_b)
    norms = [[], []], [[], []]
    for c in range(4):
        slope = vec(8, c)
        keep = 1.0 - slope
        his, los = [], []
        for i in range(0, TM, ROWS):
            rows = slice(i, i + ROWS)
            depth = depth_refs[i // STEP][i % STEP : i % STEP + ROWS, column(c)]
            s = sigmoid(depth)
            part = keep * s
            mild = slope + part
            normed = depth * mild * inv[rows] + shift[rows]
            normed_ref[rows, column(c)] = normed
            pull_ref[rows, column(c)] = mild + part * (depth * (1.0 - s))
            hi, lo = split(normed * vec(9, c) + vec(10, c))
            his.append(hi)
            los.append(lo)
        norms[c >> 1][0].append(cat(his, 0))
        norms[c >> 1][1].append(cat(los, 0))
        all_grads[c >> 1][c & 1] = mm(packed, basis_back[:, chunks[c >> 1][c & 1]])
    branch = [
        mm(cat(his + los + his, 1), w_out[768 * k : 768 * (k + 1), :]) for k, (his, los) in enumerate(norms)
    ]
    branch = branch[0] + branch[1]
    slope_skip = slope_skip_ref[...]
    keep = 1.0 - slope_skip
    totals, skips, actives = [], [], []
    for i in range(0, TM, ROWS):
        rows = slice(i, i + ROWS)
        block = mix_ref[rows, :] + (branch[rows, 0:128] + b_out_ref[:, 0:128])
        block_ref[rows, :] = block
        send_ref[rows, 0:128] = block
        total = skip_ref[rows, :] + (branch[rows, 128:256] + b_out_ref[:, 128:256])
        s = sigmoid(total)
        part = keep * s
        mild = slope_skip + part
        rest = total * (1.0 - s)
        totals.append(rest)
        skips.append(mild + part * rest)
        actives.append(split(total * mild))
    a_hi, a_lo = cat([a for a, _ in actives], 0), cat([a for _, a in actives], 0)
    query = cat([a_hi, a_lo, a_hi, ones_block(TM)], 1)

    decoded = [None, None]
    back = [None, None]
    masked, grads_hi, grads_lo = [[], []], [], []
    all_logits = [[mm(query, w_mask[:, chunk]) for chunk in chunks[0]], [None, None]]

    def logits_of(c):
        all_logits[1][c] = mm(query, w_mask[:, chunks[1][c]])

    def decode_of(n, c):
        hi, lo = all_blocks[n][c]
        decoded[c] = plus(decoded[c], mm(cat(hi + lo + hi, 1), decode[n]))

    def back_of(n, c):
        hi, lo = all_blocks[n][2 + c]
        back[c] = plus(back[c], mm(cat(hi + lo, 1), w_mask_t[c, n]))

    all_blocks = [[[[], []] for _ in range(4)] for _ in range(2)]
    for n in range(2):
        if n == 0:
            waiting = [functools.partial(logits_of, c) for c in range(2)]
        else:
            waiting = [functools.partial(f, 0, c) for f in (back_of, decode_of) for c in range(2)]
        every = 2 * (TM // ROWS) // len(waiting)
        logits, grads = all_logits[n], all_grads[n]
        blocks = all_blocks[n]
        for b in range(2):
            col = column(2 * n + b)
            bias_sum = None
            pieces = [[[], []] for _ in range(4)]
            for k, i in enumerate(range(0, TM, ROWS)):
                if (b * (TM // ROWS) + k) % every == 0 and waiting:
                    waiting.pop(0)()
                rows = slice(i, i + ROWS)
                enc = enc_ref[rows, col]
                grad_enc = None
                for c in range(2):
                    mask = 1.0 / (1.0 + jnp.exp2(logits[c][rows, column(b)]))
                    grad = grads[c][rows, column(b)]
                    grad_enc = plus(grad_enc, grad * mask)
                    value = mask * enc
                    for h, part in enumerate(split(value)):
                        pieces[c][h].append(part)
                    grad_logits = grad * value * (1.0 - mask)
                    if c == 0:
                        bias_sum = plus(bias_sum, fold(grad_logits))
                    for h, part in enumerate(split(grad_logits)):
                        pieces[2 + c][h].append(part)
                grad_enc_ref[rows, col] = grad_enc
                send_ref[rows, 256 + (2 * n + b) * 128 : 256 + (2 * n + b + 1) * 128] = grad_enc
            acc_vec[2:3, (2 * n + b) * 128 : (2 * n + b + 1) * 128] += colsum(bias_sum)
            for block, piece in zip(blocks, pieces):
                for h in range(2):
                    block[h].append(cat(piece[h], 0))
        for c in range(2):
            masked[c].append(cat(blocks[c][0] + blocks[c][1], 1))
        grads_hi = grads_hi + blocks[2][0]
        grads_lo = grads_lo + blocks[2][1]
    for c in range(2):
        back_of(1, c)
    for c in range(2):
        decode_of(1, c)
    back = back[0] + back[1]
    own_grads = cat(grads_hi + grads_lo, 1)

    pieces, along, cot_sum, skip_sum = [], None, None, None
    for k, i in enumerate(range(0, TM, ROWS)):
        rows = slice(i, i + ROWS)
        grad_active = back[rows, 0:128] + back[rows, 128:256]
        grad_skip = grad_active * skips[k]
        along = plus(along, fold(grad_active * totals[k]))
        grad_skip_ref[rows, :] = grad_skip
        send_ref[rows, 128:256] = grad_skip
        cot = cot_ref[rows, :]
        cot_sum = plus(cot_sum, fold(cot))
        skip_sum = plus(skip_sum, fold(grad_skip))
        pieces.append(split(cat([cot, grad_skip], 1)))
    acc_small[0:1, :] += colsum(along)
    acc_small[1:2, :] += colsum(cot_sum)
    acc_small[2:3, :] += colsum(skip_sum)
    g_hi, g_lo = cat([p for p, _ in pieces], 0), cat([p for _, p in pieces], 0)
    r_ref[...] = mm(three((g_hi, g_lo), 1), w_out_t[...])

    first_row = iota((8, LANES), 0) == 0
    waves = []
    for c in range(2):
        tail = decoded[c][:, 128:256]
        shifted = pltpu.roll(tail, 1, 0)
        shifted = cat([jnp.where(first_row, carry[c : c + 1, :], shifted[0:8]), shifted[8:]], 0)
        carry[c : c + 1, :] = tail[TM - 1 : TM, :]
        value = decoded[c][:, 0:128] + jnp.where(offset == 0, 0.0, shifted)
        lines = []
        for q in range(TM // 16):
            line = value[q * 16 : (q + 1) * 16] * here
            lines.append(colsum(line[0:8] + line[8:16]))
        waves.append(cat(lines, 1))
    wave_ref[0:1, :] = jnp.where(side == 0, waves[0], waves[1])
    wave_ref[1:2, :] = jnp.where(side == 0, waves[1], waves[0])

    @pl.when(j == 0)
    def _():
        down_ref[...] = r_ref[0:128, :]

    @pl.when(j == last)
    def _():
        up_ref[0:128, :] = r_ref[TM - 128 : TM, :]
        up_ref[128:136, :] = jnp.zeros((8, HIDDEN), F32)
        up_ref[128:129, 0:128] = jnp.where(side == 0, carry[0:1, :], carry[1:2, :])
        up_ref[129:130, 0:128] = jnp.where(side == 0, carry[1:2, :], carry[0:1, :])

    own_norms = cat(norms[0][0] + norms[0][1] + norms[0][0], 1)

    def weight_gradients(rows):
        for n in range(2):
            for c in range(2):
                values = masked[c][n]
                acc_basis[c, :, 256 * n : 256 * (n + 1)] += mm_tn(
                    cat([packed[rows]] * 2, 0), cat([values[rows, 0:256], values[rows, 256:512]], 0)
                )
            yield
        acc_mask[...] += mm_tn(
            three((a_hi[rows], a_lo[rows]), 0), two_of((own_grads[rows, 0:512], own_grads[rows, 512:1024]), 0)
        )
        yield
        acc_out[...] += mm_tn(
            cat([own_norms[rows, 256 * k : 256 * (k + 1)] for k in range(3)], 0), two_of((g_hi[rows], g_lo[rows]), 0)
        )
        yield

    for k in range(TM // T):
        rows = slice(k * T, (k + 1) * T)
        begin = start + k * T
        edge2, ahead2 = boundary(ends, begin)
        plain = edge2 >= begin + T + STEP
        entry = 2 * (j * (TM // T) + k)
        hot_b, hot_a = lane_items(ahead2, items)
        onehot[pl.ds(entry, 1), :] = hot_b
        onehot[pl.ds(entry + 1, 1), :] = hot_a
        row_b2, row_a2 = item_rows(ahead2, items)

        @pl.when(plain)
        def _():
            products = weight_gradients(rows)
            inverse = table_ref[1, pl.ds(row_b2, 1), :]
            lines = [[None] * 8, [None] * 8]
            for c in range(4):
                next(products)
                taps = vec(4, c) + vec(5, c) + vec(6, c)
                level = vec(7, c) + vec(3, c) * taps
                sums = [None] * 8
                for i in range(k * T, (k + 1) * T, ROWS):
                    cut = slice(i, i + ROWS)
                    r, normed, pull = r_ref[cut, column(c)], normed_ref[cut, column(c)], pull_ref[cut, column(c)]
                    depth = depth_refs[i // STEP][i % STEP : i % STEP + ROWS, column(c)] - level
                    pull_r, pull_n = pull * r, pull * normed
                    values = (
                        r, r * normed, pull_r, pull, pull_n, pull_r * depth, pull * depth, pull_n * depth,
                    )
                    sums = [plus(s, fold(value)) for s, value in zip(sums, values)]
                sums = [colsum(s) for s in sums]
                if c < 2:
                    acc_vec[0:1, column(c)] += sums[1]
                    acc_vec[1:2, column(c)] += sums[0]
                gain, flat = vec(9, c), vec(2, c) * taps * inverse
                scales = (gain, gain, flat * gain, flat, flat, inverse * gain, inverse, inverse)
                lines[c >> 1] = [plus(line, s * scale) for line, s, scale in zip(lines[c >> 1], sums, scales)]
            for i in range(8):
                entries[i, pl.ds(entry, 1), :] = lines[0][i] + lines[1][i]

        @pl.when(jnp.logical_not(plain))
        def _():
            products = weight_gradients(rows)
            place = iota((ROWS, LANES), 0) + (begin - k * T - edge2)
            inv_b, inv_a = table_ref[1, pl.ds(row_b2, 1), :], table_ref[1, pl.ds(row_a2, 1), :]
            before, behind = [None] * 8, [None] * 8
            for c in range(4):
                next(products)
                sum_r, sum_rn = None, None
                for i in range(k * T, (k + 1) * T, ROWS):
                    cut = slice(i, i + ROWS)
                    offset = place + i
                    after = offset >= 0
                    taps = jnp.where(after & (offset < STEP), 0.0, vec(4, c)) + vec(5, c)
                    taps = taps + jnp.where((offset < 0) & (offset >= -STEP), 0.0, vec(6, c))
                    r, normed = r_ref[cut, column(c)], normed_ref[cut, column(c)]
                    pull = pull_ref[cut, column(c)] * jnp.where(after, inv_a, inv_b)
                    depth = depth_refs[i // STEP][i % STEP : i % STEP + ROWS, column(c)]
                    flat = pull * (vec(2, c) * taps)
                    cross = pull * (depth - vec(7, c) - vec(3, c) * taps)
                    r_normed = r * normed
                    sum_r, sum_rn = plus(sum_r, fold(r)), plus(sum_rn, fold(r_normed))
                    q = r * vec(9, c)
                    values = (
                        q, q * normed, flat * q, flat, flat * normed, cross * q, cross, cross * normed,
                    )
                    before = [plus(s, fold(jnp.where(after, 0.0, value))) for s, value in zip(before, values)]
                    behind = [plus(s, fold(jnp.where(after, value, 0.0))) for s, value in zip(behind, values)]
                if c < 2:
                    acc_vec[0:1, column(c)] += colsum(sum_rn)
                    acc_vec[1:2, column(c)] += colsum(sum_r)
            for i in range(8):
                entries[i, pl.ds(entry, 1), :] = colsum(before[i])
                entries[i, pl.ds(entry + 1, 1), :] = colsum(behind[i])

    @pl.when(j == last)
    def _():
        hot = onehot[...]
        lines = [colsum(hot * jnp.sum(entries[i], axis=1, keepdims=True)) for i in range(8)]
        msg = cat(lines, 0)
        for i in range(msg_ref.shape[0]):
            msg_ref[i] = msg
        for ref, h in ((keep_ref, half), (give_ref, 1 - half)):
            own = pl.ds(pl.multiple_of(h * 128, 128), 128)
            ref[0:128, :] = acc_out[own, 0:128]
            ref[128:256, :] = acc_out[own, 128:256]
            for k in range(2):
                pair = pl.ds(pl.multiple_of(h * 256 + k * 128, 128), 128)
                ref[256 + 128 * k : 384 + 128 * k, :] = acc_mask[:, pair]
            bias = acc_vec[2:3, pl.ds(pl.multiple_of(h * 256, 256), 256)]
            ref[512:520, :] = cat(
                [
                    bias[:, 0:128], bias[:, 128:256], acc_vec[0:1, own], acc_vec[1:2, own],
                    acc_small[0:3, :], jnp.zeros((1, LANES), F32),
                ], 0,
            )
            for k in range(4):
                cut = column(k)
                ref[520 + 16 * k : 536 + 16 * k, :] = (acc_basis[0, 0:16, cut] + acc_basis[0, 32:48, cut]) + (
                    acc_basis[1, 48:64, cut] + acc_basis[1, 80:96, cut]
                )


def back_kernel(
    len_ref, msg_in_ref, depth_ref, r_a_ref, r_b_ref, low_ref, high_ref, hidden_ref, mix_ref, cot_ref,
    vec_ref, table_in_ref, table_mid_ref, own_ref, core_ref, x_ref, far_ref, got_ref, block_in, skip_in, enc_in,
    grad_mix_ref, send_ref, keep_ref, give_ref, edge_ref, block_ref, skip_ref, enc_ref,
    gathered, sems, table, weights, ring, acc_w, acc_vec,
):
    j = pl.program_id(0)
    last = pl.num_programs(0) - 1
    items = len_ref.shape[0]
    me = lax.axis_index("src")
    half = me & 1
    side = me >> 1
    own_rows = last * T

    def vec(row, c):
        return vec_ref[row : row + 1, column(c)]

    ends = item_ends(len_ref)

    @pl.when(j == 0)
    def _():
        copies = [
            pltpu.make_async_copy(ref.at[pl.ds(0, 128)], gathered.at[half ^ k], sems.at[k])
            for k, ref in enumerate((own_ref, core_ref, x_ref, far_ref))
        ]
        for copy in copies:
            copy.start()
        totals = 0.5 * jnp.sum(msg_in_ref[...], axis=0)
        lane = iota((1, LANES), 1)
        number = jnp.zeros((1, LANES), jnp.int32)
        for k in range(items):
            number = jnp.where(lane == k, len_ref[k], number)
        number = jnp.maximum(number.astype(F32) * HIDDEN, 1.0)
        m1 = totals[0:1] / number
        m2 = totals[1:2] / number
        p1 = (totals[2:3] - m1 * totals[3:4] - m2 * totals[4:5]) / number
        p2 = (totals[5:6] - m1 * totals[6:7] - m2 * totals[7:8]) / number
        padded = table.shape[1]
        for i, value in enumerate((m1, m2, p1, p2)):
            table[i] = to_rows(value, padded)
        acc_w[...] = jnp.zeros_like(acc_w)
        acc_vec[...] = jnp.zeros_like(acc_vec)
        edge_ref[...] = low_ref[128:136, 0:128]
        for copy in copies:
            copy.wait()
        for s in range(4):
            cut = column(s)
            hi, lo = split(gathered[s].T)
            for place in (0, 256):
                place = place + (s >> 1) * 512 + (s & 1) * 128
                weights[place : place + 128, 0:128] = hi
                weights[place : place + 128, 128:256] = lo

    block_ref[...] = got_ref[:, 0:128]
    skip_ref[...] = got_ref[:, 128:256]
    enc_ref[...] = got_ref[:, 256:768]

    base = lax.axis_index("tm") * (2 * own_rows) + half * own_rows
    new, old = j & 1, 1 - (j & 1)

    def chooser(begin, alone, edge, ahead):
        row_b, row_a = item_rows(ahead, items)

        def pick(ref, i):
            value_b = ref[i, pl.ds(row_b, 1), :]
            return value_b, value_b if alone else ref[i, pl.ds(row_a, 1), :]

        def choose(pair, i):
            if alone:
                return pair[0]
            return jnp.where(iota((ROWS, LANES), 0) + (begin - edge) + i >= 0, pair[1], pair[0])

        return pick, choose

    begin = base + j * T - STEP
    edge, ahead = boundary(ends, begin)
    alone = edge >= begin + T

    def filter_rows(alone):
        pick, choose = chooser(begin, alone, edge, ahead)
        means, inverses = pick(table_mid_ref, 0), pick(table_mid_ref, 1)
        firsts, seconds = pick(table, 0), pick(table, 1)
        shifts = tuple(-a * b for a, b in zip(means, inverses))
        firsts = tuple(a * b for a, b in zip(firsts, inverses))
        seconds = tuple(a * b for a, b in zip(seconds, inverses))
        for c in range(4):
            slope, gain = vec(8, c), vec(9, c)
            keep = 1.0 - slope
            halves = [None, None]
            for i in range(0, T, ROWS):
                if i < STEP:
                    r = jnp.where(j == 0, low_ref[i : i + ROWS, column(c)], r_a_ref[i : i + ROWS, column(c)])
                else:
                    cut = slice(i - STEP, i - STEP + ROWS)
                    r = jnp.where(j == last, high_ref[cut, column(c)], r_b_ref[cut, column(c)])
                depth = depth_ref[i : i + ROWS, column(c)]
                s = sigmoid(depth)
                u = depth * (1.0 - s)
                part = keep * s
                mild = slope + part
                inv = choose(inverses, i)
                normed = depth * mild * inv + choose(shifts, i)
                grad_act = r * (gain * inv) - choose(firsts, i) - normed * choose(seconds, i)
                if c < 2:
                    halves[i // STEP] = plus(halves[i // STEP], fold(grad_act * u))
                ring[new, i : i + ROWS, column(c)] = grad_act * (mild + part * u)
            if c < 2:
                in_low = jnp.where(j > 0, 1.0, 0.0)
                in_high = jnp.where(j < last, 1.0, 0.0)
                acc_vec[8:9, column(c)] += in_low * colsum(halves[0]) + in_high * colsum(halves[1])

    pl.when(alone)(lambda: filter_rows(True))
    pl.when(jnp.logical_not(alone))(lambda: filter_rows(False))

    start = base + (j - 1) * T
    edge2, ahead2 = boundary(ends, start)
    plain = edge2 >= start + T + STEP

    def norm_rows(plain):
        pick, choose = chooser(start, plain, edge2, ahead2)
        means, inverses = pick(table_in_ref, 0), pick(table_in_ref, 1)
        firsts, seconds = pick(table, 2), pick(table, 3)
        shifts = tuple(-a * b for a, b in zip(means, inverses))
        firsts = tuple(a * b for a, b in zip(firsts, inverses))
        seconds = tuple(a * b for a, b in zip(seconds, inverses))
        rows = iota((ROWS, LANES), 0) + (start - edge2)
        his, los = [[], [], [], []], [[], [], [], []]
        for c in range(4):
            slope, gain, bias = vec(1, c), vec(2, c), vec(3, c)
            keep = 1.0 - slope
            sums = [None] * 8
            for i in range(0, T, ROWS):
                cut = slice(i, i + ROWS)
                grad_low, grad_high = ring[old, cut, column(c)], ring[new, cut, column(c)]
                if i < STEP:
                    grad_mid = ring[old, i + STEP : i + STEP + ROWS, column(c)]
                else:
                    grad_mid = ring[new, i - STEP : i - STEP + ROWS, column(c)]
                if not plain:
                    offset = rows + i
                    grad_low = jnp.where((offset >= 0) & (offset < STEP), 0.0, grad_low)
                    grad_high = jnp.where((offset < 0) & (offset >= -STEP), 0.0, grad_high)
                grad_norm = vec(5, c) * grad_mid + vec(4, c) * grad_high + vec(6, c) * grad_low
                hidden = hidden_ref[cut, column(c)]
                s = sigmoid(hidden)
                u = hidden * (1.0 - s)
                part = keep * s
                mild = slope + part
                inv = choose(inverses, i)
                normed = hidden * mild * inv + choose(shifts, i)
                grad_act = grad_norm * (gain * inv) - choose(firsts, i) - normed * choose(seconds, i)
                grad_hidden = grad_act * (mild + part * u)
                if c < 2:
                    norm = normed * gain + bias
                    values = (
                        grad_hidden, grad_act * u, grad_norm * normed, grad_norm, norm * grad_high, norm * grad_mid,
                        norm * grad_low, grad_mid,
                    )
                    sums = [plus(s, fold(value)) for s, value in zip(sums, values)]
                hi, lo = split(grad_hidden)
                his[c].append(hi)
                los[c].append(lo)
            if c < 2:
                acc_vec[0:8, column(c)] += cat([colsum(s) for s in sums], 0)
        hi, lo = [cat(p, 0) for p in his], [cat(p, 0) for p in los]
        own = mm(cat(hi[0:2] + lo[0:2], 1), weights[0:512, :])
        back = own + mm(cat(hi[2:4] + lo[2:4], 1), weights[512:1024, :])
        grad_mix = cot_ref[...] + (back[:, 0:128] + back[:, 128:256])
        grad_mix_ref[...] = grad_mix
        send_ref[...] = grad_mix
        mixed = cat(split(mix_ref[...]), 1)
        acc_w[...] += mm_tn(cat([cat(hi[0:2], 1), cat(lo[0:2], 1)], 1), mixed)

    pl.when((j > 0) & plain)(lambda: norm_rows(True))
    pl.when((j > 0) & jnp.logical_not(plain))(lambda: norm_rows(False))

    @pl.when(j == last)
    def _():
        for ref, h in ((keep_ref, half), (give_ref, 1 - half)):
            own = pl.ds(pl.multiple_of(h * 128, 128), 128)
            rest = pl.ds(pl.multiple_of(256 + h * 128, 128), 128)
            ref[0:128, :] = (acc_w[own, 0:128] + (acc_w[own, 128:256] + acc_w[rest, 0:128])).T
            ref[128:144, :] = acc_vec[:, own]


def merge_kernel(len_ref, got_ref, mix_in, mine_ref, other_ref, edge_ref, edge_other_ref, mix_ref, wave_ref):
    me = lax.axis_index("src")
    half = me & 1
    mix_ref[...] = got_ref[...]
    width = mine_ref.shape[1]
    frames = width // STRIDE
    base = lax.axis_index("tm") * (2 * frames)
    ends = item_ends(len_ref)
    lane = iota((2, LANES), 1)
    for part, edge, h in ((mine_ref, edge_ref, half), (other_ref, edge_other_ref, 1 - half)):
        place = base + h * frames
        new = place == 0
        for end in ends:
            new = new | (end == place)
        place = pl.multiple_of(h * width, width)
        wave_ref[:, pl.ds(place, width)] = part[...]
        first = part[:, 0:128] + jnp.where((lane < STRIDE) & jnp.logical_not(new), edge[0:2, :], 0.0)
        wave_ref[:, pl.ds(place, LANES)] = first


def total_of(refs):
    values = [ref[...] for ref in refs]
    while len(values) > 1:
        values = [a + b for a, b in zip(values[0::2], values[1::2])]
    return values[0]


def last_kernel(count, early_ref, early_other_ref, *refs):
    lates = refs[:count]
    (
        w_in, b_in, slope_in, gain_in, beta_in, w_depth, b_depth, slope_mid,
    gain_mid, beta_mid, w_out, b_out, slope_skip, w_mask, b_mask, basis,
    ) = refs[count:]
    late = total_of(lates)
    w_in[...] = late[0:128]
    for ref, row in (
        (b_in, 128), (slope_in, 129), (gain_in, 130), (beta_in, 131), (b_depth, 135), (slope_mid, 136),
    ):
        ref[...] = late[row : row + 1]
    w_depth[...] = late[132:135]
    early = early_ref[...] + early_other_ref[...]
    w_out[:, 0:128] = early[0:128]
    w_out[:, 128:256] = early[128:256]
    w_mask[:, 0:128] = early[256:384]
    w_mask[:, 128:256] = early[384:512]
    b_mask[:, 0:128] = early[512:513]
    b_mask[:, 128:256] = early[513:514]
    gain_mid[...] = early[514:515]
    beta_mid[...] = early[515:516]
    slope_skip[...] = early[516:517]
    b_out[:, 0:128] = early[517:518]
    b_out[:, 128:256] = early[518:519]
    for k in range(4):
        basis[:, column(k)] = early[520 + 16 * k : 536 + 16 * k]


def local(
    mix_in, skip_in, encoded, lengths, w_in, b_in, slope_in, gain_in, beta_in, w_depth, b_depth, slope_mid, gain_mid,
    beta_mid, w_out, b_out, slope_skip, w_mask, b_mask, basis, cot_out, cot_wave,
):
    n_tm, n_src = lax.axis_size("tm"), lax.axis_size("src")
    devices = n_tm * n_src
    frames = mix_in.shape[0]
    own_rows = frames // 2
    items = lengths.shape[0]
    padded = -(-items // 8) * 8
    tiles = own_rows // T
    tiles_m = own_rows // TM
    up = [(i, i + 1) for i in range(n_tm - 1)]
    down = [(j, i) for i, j in up]
    swap = [(i, i ^ 1) for i in range(n_src)]
    cross = [(i, i ^ 2) for i in range(n_src)]

    def half():
        return lax.axis_index("src") & 1

    def struct(*shape):
        return jax.ShapeDtypeStruct(shape, F32)

    def whole(*shape):
        zeros = (0,) * len(shape)
        return pl.BlockSpec(shape, lambda i, n: zeros)

    anywhere = pl.BlockSpec(memory_space=pl.ANY)

    def vmem(*shape):
        return pltpu.VMEM(shape, F32)

    def vmem16(*shape):
        return pltpu.VMEM(shape, BF16)

    def call(kernel, name, grid, in_specs, out_specs, out_shape, scratch, us, **kw):
        return pl.pallas_call(
            kernel,
            grid_spec=pltpu.PrefetchScalarGridSpec(
                num_scalar_prefetch=1, grid=(grid,), in_specs=in_specs, out_specs=out_specs, scratch_shapes=scratch
            ),
            out_shape=out_shape,
            compiler_params=pltpu.CompilerParams(
                vmem_limit_bytes=VMEM, dimension_semantics=("arbitrary",)
            ),
            cost_estimate=pl.CostEstimate(flops=0, bytes_accessed=us * 3_600_000, transcendentals=0),
            name=name,
            **kw,
        )

    msg_shape = (devices, 8, LANES)
    message = struct(*msg_shape)

    def exchange(msg):
        return lax.all_to_all(msg, ("tm", "src"), 0, 0)

    def line(vector):
        return vector.reshape(1, -1)

    def fixed(*shape):
        return pl.BlockSpec(shape, lambda i: (0,) * len(shape))

    n1 = frames // T1
    vectors = (
        line(b_in), line(slope_in), line(gain_in), line(beta_in), w_depth, line(b_depth), line(slope_mid),
        line(gain_mid), line(beta_mid), line(b_mask),
    )
    pack, wide, low, high = pl.pallas_call(
        prep_kernel,
        grid=(1,),
        in_specs=[
            fixed(T, 128), pl.BlockSpec((T, 128), lambda i: (frames // T - 1, 0)), fixed(2, LANES), fixed(128, 128),
            fixed(128, 256), fixed(128, 256), *[fixed(*v.shape) for v in vectors],
        ],
        out_specs=[fixed(PACK_IN, 128), fixed(512, 128), fixed(T + 8, 128), fixed(T, 128)],
        out_shape=[struct(PACK_IN, 128), struct(512, 128), struct(T + 8, 128), struct(T, 128)],
        compiler_params=pltpu.CompilerParams(vmem_limit_bytes=VMEM),
        name="prep",
    )(mix_in, mix_in, cot_wave, w_in, w_out, w_mask, *vectors)
    pack_x = lax.ppermute(pack, "src", cross)
    pack_core = lax.ppermute(pack, "src", swap)
    mix_prev = lax.ppermute(high, "tm", up)
    mix_next = lax.ppermute(low, "tm", down)
    msg1 = call(
        first_kernel, "first", 2,
        [pl.BlockSpec((frames // 2, 128), lambda i, n: (i, 0)), whole(128, 128), whole(1, 128), whole(1, 128)],
        whole(*msg_shape), message,
        [vmem(1, 2 * n1, 128), vmem(1, 2 * n1, 128), vmem(2 * n1, 128), vmem(2 * n1, 128)], 4,
    )(lengths, mix_in, w_in, line(b_in), line(slope_in))
    msg1, pack_x, pack_core, mix_prev, mix_next = lax.optimization_barrier(
        (msg1, pack_x, pack_core, mix_prev, mix_next)
    )
    pack_far = lax.ppermute(pack_x, "src", swap)
    packs = (pack, pack_core, pack_x, pack_far)
    msg1 = exchange(msg1)
    wide_x = lax.ppermute(wide, "src", cross)
    wide_core = lax.ppermute(wide, "src", swap)
    wide_far = lax.ppermute(wide_x, "src", swap)
    wides = (wide, wide_core, wide_x, wide_far)

    entries = -(-2 * (tiles + 1) // 8) * 8
    hidden, depth, msg2, vec, table_in = call(
        depth_kernel, "depth", tiles + 2,
        [
            whole(*msg_shape),
            whole(frames, 128), whole(T, 128), whole(T + 8, 128), anywhere, anywhere, anywhere, anywhere,
        ],
        [
            pl.BlockSpec((T, HIDDEN), lambda i, n: (i, 0)),
            pl.BlockSpec((T, HIDDEN), lambda i, n: (jnp.maximum(i - 1, 0), 0)),
            whole(*msg_shape), whole(NVEC, HIDDEN), whole(2, padded, LANES),
        ],
        [
            struct(own_rows + 2 * T, HIDDEN), struct(own_rows + T, HIDDEN), message, struct(NVEC, HIDDEN),
            struct(2, padded, LANES),
        ],
        [
            vmem(4, PACK_IN, 128), pltpu.SemaphoreType.DMA((4,)), vmem16(512, HIDDEN), vmem(2, T, HIDDEN),
            vmem(4, entries, 128), vmem(4, entries, 128), vmem(entries, 128), vmem(entries, 128),
        ], 8,
    )(lengths, msg1, mix_in, mix_prev, mix_next, *packs)
    msg2 = exchange(msg2)

    def half_rows(width):
        return pl.BlockSpec((TM, width), lambda i, n: (half() * tiles_m + i, 0))

    def rows_m(width):
        return pl.BlockSpec((TM, width), lambda i, n: (i, 0))

    def depth_piece(k):
        return pl.BlockSpec((STEP, HIDDEN), lambda i, n: (TM // STEP * i + 1 + k, 0))

    packed = call(
        cotangent_kernel, "cotangent", tiles_m,
        [
            pl.BlockSpec((2, TM * STRIDE), lambda i, n: (0, half() * tiles_m + i)),
            pl.BlockSpec(
                (2, LANES),
                lambda i, n: (0, jnp.minimum((half() * tiles_m + i + 1) * (TM // 16), (2 * tiles_m) * (TM // 16) - 1)),
            ),
            whole(T + 8, 128), anywhere,
        ],
        rows_m(128), jax.ShapeDtypeStruct((own_rows, 128), BF16), [], 6,
    )(lengths, cot_wave, cot_wave, mix_next, vec)
    pieces = TM // STEP
    (block_out, grad_skip, grad_enc, send, wave_half, r, r_up, r_down, keep, give, msg3, table_mid) = call(
        mask_kernel, "mask", tiles_m,
        [
            whole(*msg_shape), *[depth_piece(k) for k in range(pieces)],
            half_rows(128), half_rows(128), half_rows(HIDDEN), half_rows(128),
            rows_m(128), whole(L, HIDDEN), whole(NVEC, HIDDEN), whole(1, 256), whole(1, 128),
            anywhere, anywhere, anywhere, anywhere,
        ],
        [
            half_rows(128), half_rows(128), half_rows(HIDDEN), rows_m(768),
            pl.BlockSpec((2, TM * STRIDE), lambda i, n: (0, i)),
            rows_m(HIDDEN), whole(136, HIDDEN), whole(128, HIDDEN), whole(EARLY, 128), whole(EARLY, 128),
            whole(*msg_shape), whole(2, padded, LANES),
        ],
        [
            struct(frames, 128), struct(frames, 128), struct(frames, HIDDEN), struct(own_rows, 768),
            struct(2, own_rows * STRIDE), struct(own_rows, HIDDEN), struct(136, HIDDEN), struct(128, HIDDEN),
            struct(EARLY, 128), struct(EARLY, 128), message, struct(2, padded, LANES),
        ],
        [
            vmem(4, 512, 128), pltpu.SemaphoreType.DMA((4,)), vmem16(1536, 256), vmem16(768, HIDDEN),
            vmem16(512, 1024), vmem16(2, 2, 512, 256), vmem16(2, 768, 256), vmem16(128, 1024), vmem(TM, HIDDEN), vmem(TM, HIDDEN), vmem(8, 128), vmem(256, 256), vmem(128, HIDDEN),
            vmem(2, 128, HIDDEN), vmem(8, HIDDEN), vmem(8, 128),
            vmem(8, 2 * tiles, 128), vmem(2 * tiles, 128),
        ], 28,
    )(
        lengths, msg2, *[depth] * pieces, mix_in, skip_in, encoded, cot_out, packed, basis.T, vec,
        line(b_out), line(slope_skip), *wides,
    )

    both = ("tm", "src")
    later, earlier = [], []
    for i in range(n_tm):
        for s in range(n_src):
            here = i * n_src + s
            there = here + 1 if s % 2 == 0 else (i + 1) * n_src + s - 1
            if s % 2 == 0 or i + 1 < n_tm:
                later.append((here, there))
                earlier.append((there, here))
    hops = [[(i, i ^ (1 << bit)) for i in range(n_tm)] for bit in range(n_tm.bit_length() - 1)]
    early = keep + lax.ppermute(give, "src", swap)
    got_low = lax.ppermute(r_up, both, later)
    got_high = lax.ppermute(r_down, both, earlier)
    msg3 = exchange(msg3)
    early, send, wave_half = lax.optimization_barrier((early, send, wave_half))
    early_other = lax.ppermute(early, "tm", hops[0])
    got = lax.ppermute(send, "src", swap)
    wave_other = lax.ppermute(wave_half, "src", swap)
    msg3, got_low, got_high, early, early_other, got, wave_other = lax.optimization_barrier(
        (msg3, got_low, got_high, early, early_other, got, wave_other)
    )
    early = early + early_other
    early_other = lax.ppermute(early, "tm", hops[-1])

    def rows(width):
        return pl.BlockSpec((T, width), lambda i, n: (i, 0))

    def own_tile(width):
        return pl.BlockSpec((T, width), lambda i, n: (half() * tiles + jnp.maximum(i - 1, 0), 0))

    def other_rows(width):
        return pl.BlockSpec((T, width), lambda i, n: ((1 - half()) * tiles + jnp.minimum(i, tiles - 1), 0))

    grad_mix, mix_send, keep, give, edge, block_out, grad_skip, grad_enc = call(
        back_kernel, "back", tiles + 1,
        [
            whole(*msg_shape), rows(HIDDEN),
            pl.BlockSpec((STEP, HIDDEN), lambda i, n: (jnp.maximum(2 * i - 1, 0), 0)),
            pl.BlockSpec((STEP, HIDDEN), lambda i, n: (jnp.minimum(2 * i, 2 * tiles - 1), 0)),
            whole(136, HIDDEN), whole(128, HIDDEN),
            pl.BlockSpec((T, HIDDEN), lambda i, n: (jnp.maximum(i, 1), 0)), own_tile(128), own_tile(128),
            whole(NVEC, HIDDEN), whole(2, padded, LANES), whole(2, padded, LANES),
            anywhere, anywhere, anywhere, anywhere,
            pl.BlockSpec((T, 768), lambda i, n: (jnp.minimum(i, tiles - 1), 0)), anywhere, anywhere, anywhere,
        ],
        [
            own_tile(128), pl.BlockSpec((T, 128), lambda i, n: (jnp.maximum(i - 1, 0), 0)),
            whole(144, 128), whole(144, 128), whole(8, 128), other_rows(128), other_rows(128), other_rows(HIDDEN),
        ],
        [
            struct(frames, 128), struct(own_rows, 128), struct(144, 128), struct(144, 128), struct(8, 128),
            struct(frames, 128), struct(frames, 128), struct(frames, HIDDEN),
        ],
        [
            vmem(4, 128, 128), pltpu.SemaphoreType.DMA((4,)), vmem(4, padded, LANES), vmem16(1024, 256),
            vmem(2, T, HIDDEN), vmem(512, 256), vmem(16, HIDDEN),
        ], 13,
        input_output_aliases={18: 5, 19: 6, 20: 7},
    )(
        lengths, msg3, depth, r, r, got_low, got_high, hidden, mix_in, cot_out, vec, table_in, table_mid, *packs, got,
        block_out, grad_skip, grad_enc,
    )

    grad_mix, mix_send, keep, give, edge, early_other = lax.optimization_barrier(
        (grad_mix, mix_send, keep, give, edge, early_other)
    )
    late = keep + lax.ppermute(give, "src", swap)
    mix_got = lax.ppermute(mix_send, "src", swap)
    edge_other = lax.ppermute(edge, "src", swap)
    late, early, early_other = lax.optimization_barrier((late, early, early_other))
    late_other = lax.ppermute(late, "tm", hops[0])
    early = early + early_other
    for hop in hops[1:-1]:
        early_other = lax.ppermute(early, "tm", hop)
        if hop is not hops[-2]:
            early = early + early_other
    late, late_other, early, mix_got, edge_other = lax.optimization_barrier(
        (late, late_other, early, mix_got, edge_other)
    )
    late = late + late_other
    lates = [late]
    for k in range(1, n_tm // 2):
        lates.append(lax.ppermute(late, "tm", [(i, i ^ (2 * k)) for i in range(n_tm)]))
    wave_width = own_rows * STRIDE
    late, mix_got, edge_other = lax.optimization_barrier((late, mix_got, edge_other))
    grad_mix, wave = call(
        merge_kernel, "merge", 1,
        [
            whole(own_rows, 128), anywhere, whole(2, wave_width), whole(2, wave_width), whole(8, 128), whole(8, 128),
        ],
        [pl.BlockSpec((own_rows, 128), lambda i, n: (1 - half(), 0)), whole(2, 2 * wave_width)],
        [struct(frames, 128), struct(2, 2 * wave_width)], [], 3,
        input_output_aliases={2: 0},
    )(lengths, mix_got, grad_mix, wave_half, wave_other, edge, edge_other)
    *lates, grad_mix, wave = lax.optimization_barrier((*lates, grad_mix, wave))

    parts = (early, early_other, *lates)
    shapes = (
        (128, 128), (1, 128), (1, 128), (1, 128), (1, 128), (3, 128), (1, 128), (1, 128), (1, 128), (1, 128), (128, 256),
        (1, 256), (1, 128), (128, 256), (1, 256), (L, HIDDEN),
    )
    outs = pl.pallas_call(
        functools.partial(last_kernel, len(lates)),
        grid=(1,),
        in_specs=[fixed(*part.shape) for part in parts],
        out_specs=[fixed(*shape) for shape in shapes],
        out_shape=[struct(*shape) for shape in shapes],
        compiler_params=pltpu.CompilerParams(vmem_limit_bytes=VMEM),
        name="last",
    )(*parts)
    outs = [o.reshape(-1) if o.shape[0] == 1 else o for o in outs[:-1]] + [outs[-1].T]
    return (block_out, wave, grad_mix, grad_skip, grad_enc, *outs)


def solution(mesh):
    frames, channels = P("tm", None), P("src")
    in_specs = (
        frames, frames, frames, P(), P(None, "src"), channels, channels, channels, channels, P(None, "src"), channels,
        channels, channels, channels, P("src", None), P(), P(), P(None, "src"), channels, P(), frames, P(None, "tm"),
    )
    out_specs = (
        frames, P(None, "tm"), frames, frames, frames, P(None, "src"), channels, channels, channels, channels,
        P(None, "src"), channels, channels, channels, channels, P("src", None), P(), P(), P(None, "src"), channels,
        P(),
    )
    return jax.shard_map(local, mesh=mesh, in_specs=in_specs, out_specs=out_specs, check_vma=False)
```

```python
import functools

import jax
import jax.numpy as jnp
from jax import lax
from jax.experimental import pallas as pl
from jax.experimental.pallas import tpu as pltpu
from jax.sharding import PartitionSpec as P

L = 16
STRIDE = L // 2
HIDDEN = 512
STEP = 128
EPS = 1e-05
T = 256
T1 = 512
TM = 512
ROWS = 32
LANES = 128
F32 = jnp.float32
BF16 = jnp.bfloat16
NVEC = 16
PACK_IN = 128 + NVEC
PACK = PACK_IN + 512
EARLY = 584
VMEM = 64 * 2**20 - 2**15
LOG2E = 1.4426950408889634


def split(x):
    hi = x.astype(BF16)
    return hi, (x - hi.astype(F32)).astype(BF16)


def mm(a, b):
    return lax.dot_general(a, b, (((1,), (0,)), ((), ())), preferred_element_type=F32)


def mm_tn(a, b):
    return lax.dot_general(a, b, (((0,), (0,)), ((), ())), preferred_element_type=F32)


def mm_nt(a, b):
    return lax.dot_general(a, b, (((1,), (1,)), ((), ())), preferred_element_type=F32)


def cat(parts, axis):
    return jnp.concatenate(parts, axis=axis)


def three(x, axis):
    hi, lo = x
    return cat([hi, lo, hi], axis)


def two_of(x, axis):
    hi, lo = x
    return cat([hi, hi, lo], axis)


def iota(shape, axis):
    return lax.broadcasted_iota(jnp.int32, shape, axis)


def sigmoid(x):
    return 1.0 / (1.0 + jnp.exp2(x * -LOG2E))


def colsum(x):
    return jnp.sum(x, axis=0, keepdims=True)


def fold(x):
    total = x[0:8]
    for i in range(8, x.shape[0], 8):
        total = total + x[i : i + 8]
    return total


def plus(a, b):
    return b if a is None else a + b


def column(c):
    return slice(c * LANES, (c + 1) * LANES)


def ones_block(rows):
    return jnp.where(iota((rows, LANES), 1) < 3, 1.0, 0.0).astype(BF16)


def bias_rows(bias, rows):
    hi, lo = split(bias)
    low = (bias - hi.astype(F32) - lo.astype(F32)).astype(BF16)
    place = iota((rows, bias.shape[1]), 0)
    zero = jnp.zeros((rows, bias.shape[1]), F32)
    out = jnp.where(place == 0, hi.astype(F32), zero)
    out = jnp.where(place == 1, lo.astype(F32), out)
    return jnp.where(place == 2, low.astype(F32), out).astype(BF16)


def item_ends(len_ref):
    ends, total = [], jnp.int32(0)
    for k in range(len_ref.shape[0]):
        total = total + len_ref[k]
        ends.append(total)
    return ends


def boundary(ends, start):
    ahead = jnp.where(start - STEP >= 0, 0, -1)
    for end in ends:
        ahead = ahead + (end <= start - STEP).astype(jnp.int32)
    edge = jnp.int32(0)
    for k, end in enumerate(ends):
        edge = jnp.where(ahead == k, end, edge)
    return edge, ahead


def item_rows(ahead, items):
    return jnp.maximum(ahead, 0), jnp.minimum(ahead + 1, items - 1)


def lane_items(ahead, items):
    lane = iota((1, LANES), 1)
    return (lane == ahead).astype(F32), (lane == ahead + 1).astype(F32)


def put_statistics(msg_ref, sums, squares, counts, onehot):
    groups = sums.shape[0]
    count = counts[:, :1]
    safe = jnp.maximum(count, 1.0)
    total = jnp.sum(jnp.sum(sums, axis=0), axis=1, keepdims=True)
    number = count * (groups * LANES)
    mean = total / jnp.maximum(number, 1.0)
    spread = 0.0
    for g in range(groups):
        away = sums[g] / safe - mean
        spread = spread + squares[g] + count * away * away
    spread = jnp.sum(spread, axis=1, keepdims=True)
    item_sum = colsum(onehot * total)
    item_number = colsum(onehot * number)
    item_mean = item_sum / jnp.maximum(item_number, 1.0)
    away = mean - item_mean
    item_spread = colsum(onehot * (spread + number * away * away))
    msg = cat(
        [item_sum, item_spread, item_number, item_mean, jnp.zeros((4, LANES), F32)], 0
    )
    for i in range(msg_ref.shape[0]):
        msg_ref[i] = msg


def to_rows(row, items_padded):
    wide = jnp.broadcast_to(row, (items_padded, LANES))
    own = iota((items_padded, LANES), 0) == iota((items_padded, LANES), 1)
    column = jnp.sum(jnp.where(own, wide, 0.0), axis=1, keepdims=True)
    return jnp.broadcast_to(column, (items_padded, LANES))


def merge_statistics(msg_ref, table_ref):
    msg = msg_ref[...]
    item_sum = jnp.sum(msg[:, 0:1, :], axis=0)
    number = jnp.sum(msg[:, 2:3, :], axis=0)
    mean = item_sum / jnp.maximum(number, 1.0)
    away = msg[:, 3:4, :] - mean[None]
    squares = jnp.sum(msg[:, 1:2, :] + msg[:, 2:3, :] * away * away, axis=0)
    inverse = lax.rsqrt(squares / jnp.maximum(number, 1.0) + EPS)
    padded = table_ref.shape[1]
    table_ref[0] = to_rows(mean, padded)
    table_ref[1] = to_rows(inverse, padded)


def put_entry(refs, groups, entry, sums, squares, number, hot):
    sums_ref, squares_ref, counts_ref, onehot_ref = refs
    row = pl.ds(entry, 1)
    for g in range(groups):
        sums_ref[g, row, :] = sums[g]
        squares_ref[g, row, :] = squares[g]
    counts_ref[row, :] = jnp.full((1, LANES), number, F32)
    onehot_ref[row, :] = hot


def general_entries(refs, acts, after, before, n_after, n_before, entry, ahead):
    hot_b, hot_a = lane_items(ahead, 0)
    for part, keep, number, hot in ((0, before, n_before, hot_b), (1, after, n_after, hot_a)):
        sums, squares = [], []
        for act in acts:
            total = colsum(jnp.where(keep, act, 0.0))
            away = act - total / jnp.maximum(number, 1.0)
            sums.append(total)
            squares.append(colsum(jnp.where(keep, away * away, 0.0)))
        put_entry(refs, len(acts), 2 * entry + part, sums, squares, number, hot)


def prep_kernel(
    top_ref, bottom_ref, cot_ref, w_in_ref, w_out_ref, w_mask_ref, b_in, slope_in, gain_in, beta_in, w_depth, b_depth,
    slope_mid, gain_mid, beta_mid, b_mask, pack_ref, wide_ref, low_ref, high_ref,
):
    pack_ref[0:128, :] = w_in_ref[...]
    vectors = (b_in, slope_in, gain_in, beta_in, w_depth, b_depth, slope_mid, gain_mid, beta_mid)
    bias = b_mask[...]
    pack_ref[128:144, :] = cat(
        [ref[...] for ref in vectors] + [bias[:, 0:128], bias[:, 128:256], jnp.zeros((3, LANES), F32)], 0
    )
    for k in range(2):
        wide_ref[128 * k : 128 * (k + 1), :] = w_out_ref[:, column(k)]
        wide_ref[128 * (k + 2) : 128 * (k + 3), :] = w_mask_ref[:, column(k)]
    low_ref[0:T, :] = top_ref[...]
    low_ref[T : T + 8, :] = cat([cot_ref[...], jnp.zeros((6, LANES), F32)], 0)
    high_ref[...] = bottom_ref[...]


def first_kernel(len_ref, mix_ref, w_in_ref, b_in, slope_in, msg_ref, sums, squares, counts, onehot):
    step = pl.program_id(0)
    last = pl.num_programs(0) - 1
    tiles = mix_ref.shape[0] // T1
    ends = item_ends(len_ref)
    weights = two_of(split(w_in_ref[...]), 0)
    slope = slope_in[...]
    keep = 1.0 - slope
    bias = b_in[...]
    refs = (sums, squares, counts, onehot)
    for t in range(tiles):
        j = step * tiles + t
        start = lax.axis_index("tm") * ((last + 1) * tiles * T1) + j * T1
        edge, ahead = boundary(ends, start)
        hidden = mm(three(split(mix_ref[t * T1 : (t + 1) * T1, :]), 1), weights)
        pieces, total = [], None
        for i in range(0, T1, ROWS):
            x = hidden[i : i + ROWS] + bias
            act = x * (slope + keep * sigmoid(x))
            pieces.append(act)
            total = plus(total, fold(act))
        total = colsum(total)
        mean = total / T1
        square = None
        for act in pieces:
            away = act - mean
            square = plus(square, fold(away * away))
        put_entry(refs, 1, 2 * j, [total], [colsum(square)], jnp.float32(T1), lane_items(ahead, 0)[0])
        nothing = jnp.zeros((1, LANES), F32)
        put_entry(refs, 1, 2 * j + 1, [nothing], [nothing], jnp.float32(0.0), nothing)

        @pl.when(edge < start + T1)
        def _():
            offset = iota((T1, LANES), 0) + (start - edge)
            n_before = jnp.clip(edge - start, 0, T1).astype(F32)
            act = cat(pieces, 0)
            general_entries(refs, [act], offset >= 0, offset < 0, T1 - n_before, n_before, j, ahead)

    @pl.when(step == last)
    def _():
        put_statistics(msg_ref, sums[...], squares[...], counts[...], onehot[...])


def depth_kernel(
    len_ref, msg_in_ref, mix_ref, prev_ref, next_ref, own_ref, core_ref, x_ref, far_ref,
    hidden_ref, depth_ref, msg_ref, vec_ref, table_ref,
    gathered, weights, ring, sums, squares, counts, onehot,
):
    m = pl.program_id(0)
    last = pl.num_programs(0) - 1
    items = len_ref.shape[0]
    me = lax.axis_index("src")
    half = me & 1
    own_rows = (last - 1) * T

    @pl.when(m == 0)
    def _():
        for k, ref in enumerate((own_ref, core_ref, x_ref, far_ref)):
            gathered[half ^ k] = ref[...]
        merge_statistics(msg_in_ref, table_ref)
        for ref in (sums, squares, counts, onehot):
            ref[...] = jnp.zeros_like(ref)
        for s in range(4):
            cut = column(s)
            weights[0:384, cut] = two_of(split(gathered[s, 0:128, :]), 0)
            weights[384:512, cut] = bias_rows(gathered[s, 128:129, :], 128)
            vec_ref[:, cut] = gathered[s, 128 : 128 + NVEC, :]

    def vec(row, c):
        return vec_ref[row : row + 1, column(c)]

    ends = item_ends(len_ref)
    base = lax.axis_index("tm") * (2 * own_rows) + half * own_rows
    start = base + (m - 1) * T
    edge, ahead = boundary(ends, start)
    alone = edge >= start + T
    block = half * (own_rows // T) + m - 1
    top = 2 * (own_rows // T)
    new, old = m & 1, 1 - (m & 1)

    def norm_rows(alone):
        place = pl.multiple_of(jnp.clip(block, 0, top - 1) * T, T)
        mix = mix_ref[pl.ds(place, T), :]
        mix = jnp.where(block < 0, prev_ref[...], jnp.where(block >= top, next_ref[0:T, :], mix))
        mixed = split(mix)
        hidden = mm(cat([mixed[0], mixed[1], mixed[0], ones_block(T)], 1), weights[...])
        hidden_ref[...] = hidden
        row_b, row_a = item_rows(ahead, items)
        rows = iota((ROWS, LANES), 0) + (start - edge)
        for c in range(4):
            slope = vec(1, c)
            keep = 1.0 - slope
            scale_b = table_ref[1, pl.ds(row_b, 1), :] * vec(2, c)
            shift_b = vec(3, c) - table_ref[0, pl.ds(row_b, 1), :] * scale_b
            scale_a = table_ref[1, pl.ds(row_a, 1), :] * vec(2, c)
            shift_a = vec(3, c) - table_ref[0, pl.ds(row_a, 1), :] * scale_a
            for i in range(0, T, ROWS):
                x = hidden[i : i + ROWS, column(c)]
                act = x * (slope + keep * sigmoid(x))
                if alone:
                    value = act * scale_b + shift_b
                else:
                    after = rows + i >= 0
                    value = act * jnp.where(after, scale_a, scale_b) + jnp.where(after, shift_a, shift_b)
                ring[new, i : i + ROWS, column(c)] = value

    pl.when(alone)(lambda: norm_rows(True))
    pl.when(jnp.logical_not(alone))(lambda: norm_rows(False))

    begin = start - STEP
    edge2, ahead2 = boundary(ends, begin)
    plain = edge2 >= begin + T + STEP
    refs = (sums, squares, counts, onehot)

    def filtered(c, i, lower_weight, upper_weight):
        lower = ring[old, i : i + ROWS, column(c)]
        upper = ring[new, i : i + ROWS, column(c)]
        if i < STEP:
            middle = ring[old, i + STEP : i + STEP + ROWS, column(c)]
        else:
            middle = ring[new, i - STEP : i - STEP + ROWS, column(c)]
        return lower_weight * lower + vec(5, c) * middle + upper_weight * upper + vec(7, c)

    @pl.when((m > 0) & plain)
    def _():
        in_low = jnp.where(m > 1, 1.0, 0.0)
        in_high = jnp.where(m < last, 1.0, 0.0)
        number = STEP * (in_low + in_high)
        all_sums, all_squares = [], []
        for c in range(4):
            slope = vec(8, c)
            keep = 1.0 - slope
            acts, halves = [], [None, None]
            for i in range(0, T, ROWS):
                depth = filtered(c, i, vec(4, c), vec(6, c))
                depth_ref[i : i + ROWS, column(c)] = depth
                act = depth * (slope + keep * sigmoid(depth))
                acts.append(act)
                halves[i // STEP] = plus(halves[i // STEP], fold(act))
            total = in_low * colsum(halves[0]) + in_high * colsum(halves[1])
            mean = total / number
            halves = [None, None]
            for i, act in enumerate(acts):
                away = act - mean
                halves[i * ROWS // STEP] = plus(halves[i * ROWS // STEP], fold(away * away))
            all_sums.append(total)
            all_squares.append(in_low * colsum(halves[0]) + in_high * colsum(halves[1]))
        put_entry(refs, 4, 2 * (m - 1), all_sums, all_squares, number, lane_items(ahead2, 0)[0])

    @pl.when((m > 0) & jnp.logical_not(plain))
    def _():
        low = jnp.where(m == 1, STEP, 0)
        high = jnp.where(m == last, STEP, T)
        rows = iota((ROWS, LANES), 0) + (begin - edge2)
        acts = []
        for c in range(4):
            slope = vec(8, c)
            pieces = []
            for i in range(0, T, ROWS):
                offset = rows + i
                lower_weight = jnp.where((offset >= 0) & (offset < STEP), 0.0, vec(4, c))
                upper_weight = jnp.where((offset < 0) & (offset >= -STEP), 0.0, vec(6, c))
                depth = filtered(c, i, lower_weight, upper_weight)
                depth_ref[i : i + ROWS, column(c)] = depth
                pieces.append(depth * (slope + (1.0 - slope) * sigmoid(depth)))
            acts.append(cat(pieces, 0))
        row = iota((T, LANES), 0)
        own = (row >= low) & (row < high)
        offset = row + (begin - edge2)
        n_before = jnp.clip(edge2 - begin, low, high) - low
        n_after = (high - low - n_before).astype(F32)
        general_entries(
            refs, acts, own & (offset >= 0), own & (offset < 0), n_after, n_before.astype(F32), m - 1, ahead2
        )

    @pl.when(m == last)
    def _():
        put_statistics(msg_ref, sums[...], squares[...], counts[...], onehot[...])


def cotangent_kernel(len_ref, wave_cot_ref, wave_next_ref, edge_next_ref, after_ref, packed_ref):
    j = pl.program_id(0)
    last = pl.num_programs(0) - 1
    me = lax.axis_index("src")
    half = me & 1
    side = me >> 1
    own_rows = (last + 1) * TM
    start = lax.axis_index("tm") * (2 * own_rows) + half * own_rows + j * TM
    edge, _ = boundary(item_ends(len_ref), start)
    offset = iota((TM, LANES), 0) + (start - edge)
    selects_hi, selects_lo = [], []
    for c in range(2):
        row = iota((2 * LANES, LANES), 0)
        col = iota((2 * LANES, LANES), 1) - 48 * c
        place = (row & 7) + ((row >> 7) << 3)
        selects_hi.append(((col == place) | (col == place + 16)).astype(F32).astype(BF16))
        selects_lo.append((col == place + 32).astype(F32).astype(BF16))

    lane_frame = iota((16, LANES), 1) >> 3
    frame = iota((16, LANES), 0)
    here = jnp.where(lane_frame == frame, 1.0, 0.0)
    coming = jnp.where(lane_frame == ((frame + 1) & 15), 1.0, 0.0)
    final_row = frame == 15
    packed = None
    waves = [wave_cot_ref[0:1, :], wave_cot_ref[1:2, :]]
    finals = [
        jnp.where((half == 1) & (j == last), edge_next_ref[T + c : T + c + 1, :], wave_next_ref[c : c + 1, :])
        for c in range(2)
    ]
    for c in range(2):
        wave = jnp.where(side == 0, waves[c], waves[1 - c])
        final = jnp.where(side == 0, finals[c], finals[1 - c])
        for part, select in zip(split(cat([wave, final], 1)), (selects_hi, selects_lo)):
            part = part.astype(F32)
            lines = [part[:, column(q)] for q in range(TM // 16 + 1)]
            pieces = []
            for q in range(TM // 16):
                following = jnp.where(final_row, lines[q + 1], lines[q]) * coming
                pieces.append(cat([lines[q] * here, following], 1).astype(BF16))
            packed = plus(packed, mm(cat(pieces, 0), select[c]))
    lane = iota((1, LANES), 1)
    lane = jnp.where(lane < 48, lane, lane - 48)
    packed_ref[...] = jnp.where((offset == -1) & ((lane & 15) >= 8), 0.0, packed).astype(BF16)


def mask_kernel(
    len_ref, msg_in_ref, *refs,
):
    depth_refs = refs[: TM // STEP]
    (
        mix_ref, skip_ref, enc_ref, cot_ref, packed_ref, basis_ref, vec_ref,
        b_out_ref, slope_skip_ref, own_ref, core_ref, x_ref, far_ref,
        block_ref, grad_skip_ref, grad_enc_ref, send_ref, wave_ref, r_ref, up_ref, down_ref, keep_ref, give_ref,
        msg_ref, table_ref, w_out_t,
        gathered, w_out, w_mask, w_mask_t, decode, basis_back, normed_ref,
        pull_ref, carry, acc_out, acc_mask, acc_basis, acc_vec,
        acc_small, entries, onehot,
    ) = refs[TM // STEP :]
    j = pl.program_id(0)
    last = pl.num_programs(0) - 1
    items = len_ref.shape[0]
    me = lax.axis_index("src")
    half = me & 1
    side = me >> 1
    own_rows = (last + 1) * TM

    def vec(row, c):
        return vec_ref[row : row + 1, column(c)]

    @pl.when(j == 0)
    def _():
        for k, ref in enumerate((own_ref, core_ref, x_ref, far_ref)):
            gathered[half ^ k] = ref[...]
        merge_statistics(msg_in_ref, table_ref)
        for ref in (acc_out, acc_mask, acc_basis, acc_vec, acc_small, carry, entries):
            ref[...] = jnp.zeros_like(ref)
        basis = split(basis_ref[...])
        b_hi, b_lo = basis
        col = iota((L, 2 * LANES), 1)
        row = iota((L, 2 * LANES), 0)
        spread = ((col & 7) == (row & 7)) & ((col >> 7) == (row >> 3))
        spread = spread.astype(F32).astype(BF16)
        wide = (mm_tn(b_hi, spread).astype(BF16), mm_tn(b_lo, spread).astype(BF16))
        for n in range(2):
            decode[n] = two_of([part[n * 256 : (n + 1) * 256] for part in wide], 0)
        for c in range(2):
            row = iota((LANES, L), 0) - 48 * c
            col = iota((LANES, L), 1)
            with_hi = ((row == col) | (row == col + 32)).astype(F32).astype(BF16)
            with_lo = (row == col + 16).astype(F32).astype(BF16)
            back = mm(with_hi, b_hi) + mm(with_lo, b_lo)
            basis_back[:, c * HIDDEN : (c + 1) * HIDDEN] = back.astype(BF16)
        for s in range(4):
            cut = column(s)
            for k in range(2):
                part = gathered[s, column(k), :]
                hi, lo = split(part)
                for place, value in ((0, hi), (256, hi), (512, lo)):
                    place = place + (s >> 1) * 768 + (s & 1) * 128
                    w_out[place : place + 128, column(k)] = value
                hi, lo = split(part.T)
                for place, value in ((0, hi), (256, hi), (512, lo)):
                    w_out_t[place + k * 128 : place + (k + 1) * 128, cut] = value
                part = gathered[s, column(2 + k), :]
                wide = slice(s * 256 + k * LANES, s * 256 + (k + 1) * LANES)
                w_mask[0:384, wide] = two_of(split(part * -LOG2E), 0)
                w_mask[384:512, wide] = bias_rows(vec_ref[11 + k : 12 + k, cut] * -LOG2E, 128)
                hi, lo = split(part.T)
                for place in (0, 256):
                    w_mask_t[s >> 1, s & 1, place + k * 128 : place + (k + 1) * 128, 0:128] = hi
                    w_mask_t[s >> 1, s & 1, place + k * 128 : place + (k + 1) * 128, 128:256] = lo

    ends = item_ends(len_ref)
    start = lax.axis_index("tm") * (2 * own_rows) + half * own_rows + j * TM
    edge, ahead = boundary(ends, start)
    row_b, row_a = item_rows(ahead, items)
    offset = iota((TM, LANES), 0) + (start - edge)

    lane_frame = iota((16, LANES), 1) >> 3
    here = jnp.where(lane_frame == iota((16, LANES), 0), 1.0, 0.0)
    packed = packed_ref[...]

    chunks = [[slice(c * HIDDEN + n * 256, c * HIDDEN + (n + 1) * 256) for c in range(2)] for n in range(2)]
    all_grads = [[None, None], [None, None]]
    after = offset >= 0
    inv_b, inv_a = table_ref[1, pl.ds(row_b, 1), :], table_ref[1, pl.ds(row_a, 1), :]
    shift_b, shift_a = -inv_b * table_ref[0, pl.ds(row_b, 1), :], -inv_a * table_ref[0, pl.ds(row_a, 1), :]
    inv = jnp.where(after, inv_a, inv_b)
    shift = jnp.where(after, shift_a, shift_b)
    norms = [[], []], [[], []]
    for c in range(4):
        slope = vec(8, c)
        keep = 1.0 - slope
        his, los = [], []
        for i in range(0, TM, ROWS):
            rows = slice(i, i + ROWS)
            depth = depth_refs[i // STEP][i % STEP : i % STEP + ROWS, column(c)]
            s = sigmoid(depth)
            part = keep * s
            mild = slope + part
            normed = depth * mild * inv[rows] + shift[rows]
            normed_ref[rows, column(c)] = normed
            pull_ref[rows, column(c)] = mild + part * (depth * (1.0 - s))
            hi, lo = split(normed * vec(9, c) + vec(10, c))
            his.append(hi)
            los.append(lo)
        norms[c >> 1][0].append(cat(his, 0))
        norms[c >> 1][1].append(cat(los, 0))
        all_grads[c >> 1][c & 1] = mm(packed, basis_back[:, chunks[c >> 1][c & 1]])
    branch = [
        mm(cat(his + los + his, 1), w_out[768 * k : 768 * (k + 1), :]) for k, (his, los) in enumerate(norms)
    ]
    branch = branch[0] + branch[1]
    slope_skip = slope_skip_ref[...]
    keep = 1.0 - slope_skip
    totals, skips, actives = [], [], []
    for i in range(0, TM, ROWS):
        rows = slice(i, i + ROWS)
        block = mix_ref[rows, :] + (branch[rows, 0:128] + b_out_ref[:, 0:128])
        block_ref[rows, :] = block
        send_ref[rows, 0:128] = block
        total = skip_ref[rows, :] + (branch[rows, 128:256] + b_out_ref[:, 128:256])
        s = sigmoid(total)
        part = keep * s
        mild = slope_skip + part
        rest = total * (1.0 - s)
        totals.append(rest)
        skips.append(mild + part * rest)
        actives.append(split(total * mild))
    a_hi, a_lo = cat([a for a, _ in actives], 0), cat([a for _, a in actives], 0)
    query = cat([a_hi, a_lo, a_hi, ones_block(TM)], 1)

    decoded = [None, None]
    back = [None, None]
    masked, grads_hi, grads_lo = [[], []], [], []
    all_logits = [[mm(query, w_mask[:, chunk]) for chunk in chunks[0]], [None, None]]

    def logits_of(c):
        all_logits[1][c] = mm(query, w_mask[:, chunks[1][c]])

    def decode_of(n, c):
        hi, lo = all_blocks[n][c]
        decoded[c] = plus(decoded[c], mm(cat(hi + lo + hi, 1), decode[n]))

    def back_of(n, c):
        hi, lo = all_blocks[n][2 + c]
        back[c] = plus(back[c], mm(cat(hi + lo, 1), w_mask_t[c, n]))

    all_blocks = [[[[], []] for _ in range(4)] for _ in range(2)]
    for n in range(2):
        if n == 0:
            waiting = [functools.partial(logits_of, c) for c in range(2)]
        else:
            waiting = [functools.partial(f, 0, c) for f in (back_of, decode_of) for c in range(2)]
        every = 2 * (TM // ROWS) // len(waiting)
        logits, grads = all_logits[n], all_grads[n]
        blocks = all_blocks[n]
        for b in range(2):
            col = column(2 * n + b)
            bias_sum = None
            pieces = [[[], []] for _ in range(4)]
            for k, i in enumerate(range(0, TM, ROWS)):
                if (b * (TM // ROWS) + k) % every == 0 and waiting:
                    waiting.pop(0)()
                rows = slice(i, i + ROWS)
                enc = enc_ref[rows, col]
                grad_enc = None
                for c in range(2):
                    mask = 1.0 / (1.0 + jnp.exp2(logits[c][rows, column(b)]))
                    grad = grads[c][rows, column(b)]
                    grad_enc = plus(grad_enc, grad * mask)
                    value = mask * enc
                    for h, part in enumerate(split(value)):
                        pieces[c][h].append(part)
                    grad_logits = grad * value * (1.0 - mask)
                    if c == 0:
                        bias_sum = plus(bias_sum, fold(grad_logits))
                    for h, part in enumerate(split(grad_logits)):
                        pieces[2 + c][h].append(part)
                grad_enc_ref[rows, col] = grad_enc
                send_ref[rows, 256 + (2 * n + b) * 128 : 256 + (2 * n + b + 1) * 128] = grad_enc
            acc_vec[2:3, (2 * n + b) * 128 : (2 * n + b + 1) * 128] += colsum(bias_sum)
            for block, piece in zip(blocks, pieces):
                for h in range(2):
                    block[h].append(cat(piece[h], 0))
        for c in range(2):
            masked[c].append(cat(blocks[c][0] + blocks[c][1], 1))
        grads_hi = grads_hi + blocks[2][0]
        grads_lo = grads_lo + blocks[2][1]
    for c in range(2):
        back_of(1, c)
    for c in range(2):
        decode_of(1, c)
    back = back[0] + back[1]
    own_grads = cat(grads_hi + grads_lo, 1)

    pieces, along, cot_sum, skip_sum = [], None, None, None
    for k, i in enumerate(range(0, TM, ROWS)):
        rows = slice(i, i + ROWS)
        grad_active = back[rows, 0:128] + back[rows, 128:256]
        grad_skip = grad_active * skips[k]
        along = plus(along, fold(grad_active * totals[k]))
        grad_skip_ref[rows, :] = grad_skip
        send_ref[rows, 128:256] = grad_skip
        cot = cot_ref[rows, :]
        cot_sum = plus(cot_sum, fold(cot))
        skip_sum = plus(skip_sum, fold(grad_skip))
        pieces.append(split(cat([cot, grad_skip], 1)))
    acc_small[0:1, :] += colsum(along)
    acc_small[1:2, :] += colsum(cot_sum)
    acc_small[2:3, :] += colsum(skip_sum)
    g_hi, g_lo = cat([p for p, _ in pieces], 0), cat([p for _, p in pieces], 0)
    r_ref[...] = mm(three((g_hi, g_lo), 1), w_out_t[...])

    first_row = iota((8, LANES), 0) == 0
    waves = []
    for c in range(2):
        tail = decoded[c][:, 128:256]
        shifted = pltpu.roll(tail, 1, 0)
        shifted = cat([jnp.where(first_row, carry[c : c + 1, :], shifted[0:8]), shifted[8:]], 0)
        carry[c : c + 1, :] = tail[TM - 1 : TM, :]
        value = decoded[c][:, 0:128] + jnp.where(offset == 0, 0.0, shifted)
        lines = []
        for q in range(TM // 16):
            line = value[q * 16 : (q + 1) * 16] * here
            lines.append(colsum(line[0:8] + line[8:16]))
        waves.append(cat(lines, 1))
    wave_ref[0:1, :] = jnp.where(side == 0, waves[0], waves[1])
    wave_ref[1:2, :] = jnp.where(side == 0, waves[1], waves[0])

    @pl.when(j == 0)
    def _():
        down_ref[:, 0:128] = cot_ref[0:128, :]
        down_ref[:, 128:256] = grad_skip_ref[0:128, :]

    @pl.when(j == last)
    def _():
        up_ref[0:128, 0:128] = cot_ref[TM - 128 : TM, :]
        up_ref[0:128, 128:256] = grad_skip_ref[TM - 128 : TM, :]
        up_ref[128:136, :] = jnp.zeros((8, 256), F32)
        up_ref[128:129, 0:128] = jnp.where(side == 0, carry[0:1, :], carry[1:2, :])
        up_ref[129:130, 0:128] = jnp.where(side == 0, carry[1:2, :], carry[0:1, :])

    own_norms = cat(norms[0][0] + norms[0][1] + norms[0][0], 1)

    def weight_gradients(rows):
        for n in range(2):
            for c in range(2):
                values = masked[c][n]
                acc_basis[c, :, 256 * n : 256 * (n + 1)] += mm_tn(
                    cat([packed[rows]] * 2, 0), cat([values[rows, 0:256], values[rows, 256:512]], 0)
                )
            yield
        acc_mask[...] += mm_tn(
            three((a_hi[rows], a_lo[rows]), 0), two_of((own_grads[rows, 0:512], own_grads[rows, 512:1024]), 0)
        )
        yield
        acc_out[...] += mm_tn(
            cat([own_norms[rows, 256 * k : 256 * (k + 1)] for k in range(3)], 0), two_of((g_hi[rows], g_lo[rows]), 0)
        )
        yield

    for k in range(TM // T):
        rows = slice(k * T, (k + 1) * T)
        begin = start + k * T
        edge2, ahead2 = boundary(ends, begin)
        plain = edge2 >= begin + T + STEP
        entry = 2 * (j * (TM // T) + k)
        hot_b, hot_a = lane_items(ahead2, items)
        onehot[pl.ds(entry, 1), :] = hot_b
        onehot[pl.ds(entry + 1, 1), :] = hot_a
        row_b2, row_a2 = item_rows(ahead2, items)

        @pl.when(plain)
        def _():
            products = weight_gradients(rows)
            inverse = table_ref[1, pl.ds(row_b2, 1), :]
            lines = [[None] * 8, [None] * 8]
            for c in range(4):
                next(products)
                taps = vec(4, c) + vec(5, c) + vec(6, c)
                level = vec(7, c) + vec(3, c) * taps
                sums = [None] * 8
                for i in range(k * T, (k + 1) * T, ROWS):
                    cut = slice(i, i + ROWS)
                    r, normed, pull = r_ref[cut, column(c)], normed_ref[cut, column(c)], pull_ref[cut, column(c)]
                    depth = depth_refs[i // STEP][i % STEP : i % STEP + ROWS, column(c)] - level
                    pull_r, pull_n = pull * r, pull * normed
                    values = (
                        r, r * normed, pull_r, pull, pull_n, pull_r * depth, pull * depth, pull_n * depth,
                    )
                    sums = [plus(s, fold(value)) for s, value in zip(sums, values)]
                sums = [colsum(s) for s in sums]
                if c < 2:
                    acc_vec[0:1, column(c)] += sums[1]
                    acc_vec[1:2, column(c)] += sums[0]
                gain, flat = vec(9, c), vec(2, c) * taps * inverse
                scales = (gain, gain, flat * gain, flat, flat, inverse * gain, inverse, inverse)
                lines[c >> 1] = [plus(line, s * scale) for line, s, scale in zip(lines[c >> 1], sums, scales)]
            for i in range(8):
                entries[i, pl.ds(entry, 1), :] = lines[0][i] + lines[1][i]

        @pl.when(jnp.logical_not(plain))
        def _():
            products = weight_gradients(rows)
            place = iota((ROWS, LANES), 0) + (begin - k * T - edge2)
            inv_b, inv_a = table_ref[1, pl.ds(row_b2, 1), :], table_ref[1, pl.ds(row_a2, 1), :]
            before, behind = [None] * 8, [None] * 8
            for c in range(4):
                next(products)
                sum_r, sum_rn = None, None
                for i in range(k * T, (k + 1) * T, ROWS):
                    cut = slice(i, i + ROWS)
                    offset = place + i
                    after = offset >= 0
                    taps = jnp.where(after & (offset < STEP), 0.0, vec(4, c)) + vec(5, c)
                    taps = taps + jnp.where((offset < 0) & (offset >= -STEP), 0.0, vec(6, c))
                    r, normed = r_ref[cut, column(c)], normed_ref[cut, column(c)]
                    pull = pull_ref[cut, column(c)] * jnp.where(after, inv_a, inv_b)
                    depth = depth_refs[i // STEP][i % STEP : i % STEP + ROWS, column(c)]
                    flat = pull * (vec(2, c) * taps)
                    cross = pull * (depth - vec(7, c) - vec(3, c) * taps)
                    r_normed = r * normed
                    sum_r, sum_rn = plus(sum_r, fold(r)), plus(sum_rn, fold(r_normed))
                    q = r * vec(9, c)
                    values = (
                        q, q * normed, flat * q, flat, flat * normed, cross * q, cross, cross * normed,
                    )
                    before = [plus(s, fold(jnp.where(after, 0.0, value))) for s, value in zip(before, values)]
                    behind = [plus(s, fold(jnp.where(after, value, 0.0))) for s, value in zip(behind, values)]
                if c < 2:
                    acc_vec[0:1, column(c)] += colsum(sum_rn)
                    acc_vec[1:2, column(c)] += colsum(sum_r)
            for i in range(8):
                entries[i, pl.ds(entry, 1), :] = colsum(before[i])
                entries[i, pl.ds(entry + 1, 1), :] = colsum(behind[i])

    @pl.when(j == last)
    def _():
        hot = onehot[...]
        lines = [colsum(hot * jnp.sum(entries[i], axis=1, keepdims=True)) for i in range(8)]
        msg = cat(lines, 0)
        for i in range(msg_ref.shape[0]):
            msg_ref[i] = msg
        for ref, h in ((keep_ref, half), (give_ref, 1 - half)):
            own = pl.ds(pl.multiple_of(h * 128, 128), 128)
            ref[0:128, :] = acc_out[own, 0:128]
            ref[128:256, :] = acc_out[own, 128:256]
            for k in range(2):
                pair = pl.ds(pl.multiple_of(h * 256 + k * 128, 128), 128)
                ref[256 + 128 * k : 384 + 128 * k, :] = acc_mask[:, pair]
            bias = acc_vec[2:3, pl.ds(pl.multiple_of(h * 256, 256), 256)]
            ref[512:520, :] = cat(
                [
                    bias[:, 0:128], bias[:, 128:256], acc_vec[0:1, own], acc_vec[1:2, own],
                    acc_small[0:3, :], jnp.zeros((1, LANES), F32),
                ], 0,
            )
            for k in range(4):
                cut = column(k)
                ref[520 + 16 * k : 536 + 16 * k, :] = (acc_basis[0, 0:16, cut] + acc_basis[0, 32:48, cut]) + (
                    acc_basis[1, 48:64, cut] + acc_basis[1, 80:96, cut]
                )


def back_kernel(
    len_ref, msg_in_ref, depth_ref, r_a_ref, r_b_ref, low_ref, high_ref, hidden_ref, mix_ref, cot_ref,
    vec_ref, table_in_ref, table_mid_ref, w_out_t, own_ref, core_ref, x_ref, far_ref, got_ref, block_in, skip_in, enc_in,
    grad_mix_ref, send_ref, keep_ref, give_ref, edge_ref, block_ref, skip_ref, enc_ref,
    gathered, table, weights, ring, halo, acc_w, acc_vec,
):
    j = pl.program_id(0)
    last = pl.num_programs(0) - 1
    items = len_ref.shape[0]
    me = lax.axis_index("src")
    half = me & 1
    side = me >> 1
    own_rows = last * T

    def vec(row, c):
        return vec_ref[row : row + 1, column(c)]

    ends = item_ends(len_ref)

    @pl.when(j == 0)
    def _():
        for k, ref in enumerate((own_ref, core_ref, x_ref, far_ref)):
            gathered[half ^ k] = ref[...]
        totals = 0.5 * jnp.sum(msg_in_ref[...], axis=0)
        lane = iota((1, LANES), 1)
        number = jnp.zeros((1, LANES), jnp.int32)
        for k in range(items):
            number = jnp.where(lane == k, len_ref[k], number)
        number = jnp.maximum(number.astype(F32) * HIDDEN, 1.0)
        m1 = totals[0:1] / number
        m2 = totals[1:2] / number
        p1 = (totals[2:3] - m1 * totals[3:4] - m2 * totals[4:5]) / number
        p2 = (totals[5:6] - m1 * totals[6:7] - m2 * totals[7:8]) / number
        padded = table.shape[1]
        for i, value in enumerate((m1, m2, p1, p2)):
            table[i] = to_rows(value, padded)
        acc_w[...] = jnp.zeros_like(acc_w)
        acc_vec[...] = jnp.zeros_like(acc_vec)
        edge_ref[...] = low_ref[128:136, 0:128]
        for k, part in enumerate((low_ref[0:128, :], high_ref[...])):
            halo[k] = mm(three(split(part), 1), w_out_t[...])
        for s in range(4):
            cut = column(s)
            hi, lo = split(gathered[s].T)
            for place in (0, 256):
                place = place + (s >> 1) * 512 + (s & 1) * 128
                weights[place : place + 128, 0:128] = hi
                weights[place : place + 128, 128:256] = lo

    block_ref[...] = got_ref[:, 0:128]
    skip_ref[...] = got_ref[:, 128:256]
    enc_ref[...] = got_ref[:, 256:768]

    base = lax.axis_index("tm") * (2 * own_rows) + half * own_rows
    new, old = j & 1, 1 - (j & 1)

    def chooser(begin, alone, edge, ahead):
        row_b, row_a = item_rows(ahead, items)

        def pick(ref, i):
            value_b = ref[i, pl.ds(row_b, 1), :]
            return value_b, value_b if alone else ref[i, pl.ds(row_a, 1), :]

        def choose(pair, i):
            if alone:
                return pair[0]
            return jnp.where(iota((ROWS, LANES), 0) + (begin - edge) + i >= 0, pair[1], pair[0])

        return pick, choose

    begin = base + j * T - STEP
    edge, ahead = boundary(ends, begin)
    alone = edge >= begin + T

    def filter_rows(alone):
        pick, choose = chooser(begin, alone, edge, ahead)
        means, inverses = pick(table_mid_ref, 0), pick(table_mid_ref, 1)
        firsts, seconds = pick(table, 0), pick(table, 1)
        shifts = tuple(-a * b for a, b in zip(means, inverses))
        firsts = tuple(a * b for a, b in zip(firsts, inverses))
        seconds = tuple(a * b for a, b in zip(seconds, inverses))
        for c in range(4):
            slope, gain = vec(8, c), vec(9, c)
            keep = 1.0 - slope
            halves = [None, None]
            for i in range(0, T, ROWS):
                if i < STEP:
                    r = jnp.where(j == 0, halo[0, i : i + ROWS, column(c)], r_a_ref[i : i + ROWS, column(c)])
                else:
                    cut = slice(i - STEP, i - STEP + ROWS)
                    r = jnp.where(j == last, halo[1, cut, column(c)], r_b_ref[cut, column(c)])
                depth = depth_ref[i : i + ROWS, column(c)]
                s = sigmoid(depth)
                u = depth * (1.0 - s)
                part = keep * s
                mild = slope + part
                inv = choose(inverses, i)
                normed = depth * mild * inv + choose(shifts, i)
                grad_act = r * (gain * inv) - choose(firsts, i) - normed * choose(seconds, i)
                if c < 2:
                    halves[i // STEP] = plus(halves[i // STEP], fold(grad_act * u))
                ring[new, i : i + ROWS, column(c)] = grad_act * (mild + part * u)
            if c < 2:
                in_low = jnp.where(j > 0, 1.0, 0.0)
                in_high = jnp.where(j < last, 1.0, 0.0)
                acc_vec[8:9, column(c)] += in_low * colsum(halves[0]) + in_high * colsum(halves[1])

    pl.when(alone)(lambda: filter_rows(True))
    pl.when(jnp.logical_not(alone))(lambda: filter_rows(False))

    start = base + (j - 1) * T
    edge2, ahead2 = boundary(ends, start)
    plain = edge2 >= start + T + STEP

    def norm_rows(plain):
        pick, choose = chooser(start, plain, edge2, ahead2)
        means, inverses = pick(table_in_ref, 0), pick(table_in_ref, 1)
        firsts, seconds = pick(table, 2), pick(table, 3)
        shifts = tuple(-a * b for a, b in zip(means, inverses))
        firsts = tuple(a * b for a, b in zip(firsts, inverses))
        seconds = tuple(a * b for a, b in zip(seconds, inverses))
        rows = iota((ROWS, LANES), 0) + (start - edge2)
        his, los = [[], [], [], []], [[], [], [], []]
        for c in range(4):
            slope, gain, bias = vec(1, c), vec(2, c), vec(3, c)
            keep = 1.0 - slope
            sums = [None] * 8
            for i in range(0, T, ROWS):
                cut = slice(i, i + ROWS)
                grad_low, grad_high = ring[old, cut, column(c)], ring[new, cut, column(c)]
                if i < STEP:
                    grad_mid = ring[old, i + STEP : i + STEP + ROWS, column(c)]
                else:
                    grad_mid = ring[new, i - STEP : i - STEP + ROWS, column(c)]
                if not plain:
                    offset = rows + i
                    grad_low = jnp.where((offset >= 0) & (offset < STEP), 0.0, grad_low)
                    grad_high = jnp.where((offset < 0) & (offset >= -STEP), 0.0, grad_high)
                grad_norm = vec(5, c) * grad_mid + vec(4, c) * grad_high + vec(6, c) * grad_low
                hidden = hidden_ref[cut, column(c)]
                s = sigmoid(hidden)
                u = hidden * (1.0 - s)
                part = keep * s
                mild = slope + part
                inv = choose(inverses, i)
                normed = hidden * mild * inv + choose(shifts, i)
                grad_act = grad_norm * (gain * inv) - choose(firsts, i) - normed * choose(seconds, i)
                grad_hidden = grad_act * (mild + part * u)
                if c < 2:
                    norm = normed * gain + bias
                    values = (
                        grad_hidden, grad_act * u, grad_norm * normed, grad_norm, norm * grad_high, norm * grad_mid,
                        norm * grad_low, grad_mid,
                    )
                    sums = [plus(s, fold(value)) for s, value in zip(sums, values)]
                hi, lo = split(grad_hidden)
                his[c].append(hi)
                los[c].append(lo)
            if c < 2:
                acc_vec[0:8, column(c)] += cat([colsum(s) for s in sums], 0)
        hi, lo = [cat(p, 0) for p in his], [cat(p, 0) for p in los]
        own = mm(cat(hi[0:2] + lo[0:2], 1), weights[0:512, :])
        back = own + mm(cat(hi[2:4] + lo[2:4], 1), weights[512:1024, :])
        grad_mix = cot_ref[...] + (back[:, 0:128] + back[:, 128:256])
        grad_mix_ref[...] = grad_mix
        send_ref[...] = grad_mix
        mixed = cat(split(mix_ref[...]), 1)
        acc_w[...] += mm_tn(cat([cat(hi[0:2], 1), cat(lo[0:2], 1)], 1), mixed)

    pl.when((j > 0) & plain)(lambda: norm_rows(True))
    pl.when((j > 0) & jnp.logical_not(plain))(lambda: norm_rows(False))

    @pl.when(j == last)
    def _():
        for ref, h in ((keep_ref, half), (give_ref, 1 - half)):
            own = pl.ds(pl.multiple_of(h * 128, 128), 128)
            rest = pl.ds(pl.multiple_of(256 + h * 128, 128), 128)
            ref[0:128, :] = (acc_w[own, 0:128] + (acc_w[own, 128:256] + acc_w[rest, 0:128])).T
            ref[128:144, :] = acc_vec[:, own]


def merge_kernel(len_ref, got_ref, mix_in, mine_ref, other_ref, edge_ref, edge_other_ref, mix_ref, wave_ref):
    me = lax.axis_index("src")
    half = me & 1
    mix_ref[...] = got_ref[...]
    width = mine_ref.shape[1]
    frames = width // STRIDE
    base = lax.axis_index("tm") * (2 * frames)
    ends = item_ends(len_ref)
    lane = iota((2, LANES), 1)
    for part, edge, h in ((mine_ref, edge_ref, half), (other_ref, edge_other_ref, 1 - half)):
        place = base + h * frames
        new = place == 0
        for end in ends:
            new = new | (end == place)
        place = pl.multiple_of(h * width, width)
        wave_ref[:, pl.ds(place, width)] = part[...]
        first = part[:, 0:128] + jnp.where((lane < STRIDE) & jnp.logical_not(new), edge[0:2, :], 0.0)
        wave_ref[:, pl.ds(place, LANES)] = first


def total_of(refs):
    values = [ref[...] for ref in refs]
    while len(values) > 1:
        values = [a + b for a, b in zip(values[0::2], values[1::2])]
    return values[0]


def last_kernel(count, early_ref, early_other_ref, *refs):
    lates = refs[:count]
    (
        w_in, b_in, slope_in, gain_in, beta_in, w_depth, b_depth, slope_mid,
    gain_mid, beta_mid, w_out, b_out, slope_skip, w_mask, b_mask, basis,
    ) = refs[count:]
    late = total_of(lates)
    w_in[...] = late[0:128]
    for ref, row in (
        (b_in, 128), (slope_in, 129), (gain_in, 130), (beta_in, 131), (b_depth, 135), (slope_mid, 136),
    ):
        ref[...] = late[row : row + 1]
    w_depth[...] = late[132:135]
    early = early_ref[...] + early_other_ref[...]
    w_out[:, 0:128] = early[0:128]
    w_out[:, 128:256] = early[128:256]
    w_mask[:, 0:128] = early[256:384]
    w_mask[:, 128:256] = early[384:512]
    b_mask[:, 0:128] = early[512:513]
    b_mask[:, 128:256] = early[513:514]
    gain_mid[...] = early[514:515]
    beta_mid[...] = early[515:516]
    slope_skip[...] = early[516:517]
    b_out[:, 0:128] = early[517:518]
    b_out[:, 128:256] = early[518:519]
    for k in range(4):
        basis[:, column(k)] = early[520 + 16 * k : 536 + 16 * k]


def local(
    mix_in, skip_in, encoded, lengths, w_in, b_in, slope_in, gain_in, beta_in, w_depth, b_depth, slope_mid, gain_mid,
    beta_mid, w_out, b_out, slope_skip, w_mask, b_mask, basis, cot_out, cot_wave,
):
    n_tm, n_src = lax.axis_size("tm"), lax.axis_size("src")
    devices = n_tm * n_src
    frames = mix_in.shape[0]
    own_rows = frames // 2
    items = lengths.shape[0]
    padded = -(-items // 8) * 8
    tiles = own_rows // T
    tiles_m = own_rows // TM
    up = [(i, i + 1) for i in range(n_tm - 1)]
    down = [(j, i) for i, j in up]
    swap = [(i, i ^ 1) for i in range(n_src)]
    cross = [(i, i ^ 2) for i in range(n_src)]

    def half():
        return lax.axis_index("src") & 1

    def struct(*shape):
        return jax.ShapeDtypeStruct(shape, F32)

    def whole(*shape):
        zeros = (0,) * len(shape)
        return pl.BlockSpec(shape, lambda i, n: zeros)

    anywhere = pl.BlockSpec(memory_space=pl.ANY)

    def vmem(*shape):
        return pltpu.VMEM(shape, F32)

    def vmem16(*shape):
        return pltpu.VMEM(shape, BF16)

    def call(kernel, name, grid, in_specs, out_specs, out_shape, scratch, us, **kw):
        return pl.pallas_call(
            kernel,
            grid_spec=pltpu.PrefetchScalarGridSpec(
                num_scalar_prefetch=1, grid=(grid,), in_specs=in_specs, out_specs=out_specs, scratch_shapes=scratch
            ),
            out_shape=out_shape,
            compiler_params=pltpu.CompilerParams(
                vmem_limit_bytes=VMEM, dimension_semantics=("arbitrary",)
            ),
            cost_estimate=pl.CostEstimate(flops=0, bytes_accessed=us * 3_600_000, transcendentals=0),
            name=name,
            **kw,
        )

    msg_shape = (devices, 8, LANES)
    message = struct(*msg_shape)

    def exchange(msg):
        return lax.all_to_all(msg, ("tm", "src"), 0, 0)

    def line(vector):
        return vector.reshape(1, -1)

    def fixed(*shape):
        return pl.BlockSpec(shape, lambda i: (0,) * len(shape))

    n1 = frames // T1
    vectors = (
        line(b_in), line(slope_in), line(gain_in), line(beta_in), w_depth, line(b_depth), line(slope_mid),
        line(gain_mid), line(beta_mid), line(b_mask),
    )
    pack, wide, low, high = pl.pallas_call(
        prep_kernel,
        grid=(1,),
        in_specs=[
            fixed(T, 128), pl.BlockSpec((T, 128), lambda i: (frames // T - 1, 0)), fixed(2, LANES), fixed(128, 128),
            fixed(128, 256), fixed(128, 256), *[fixed(*v.shape) for v in vectors],
        ],
        out_specs=[fixed(PACK_IN, 128), fixed(512, 128), fixed(T + 8, 128), fixed(T, 128)],
        out_shape=[struct(PACK_IN, 128), struct(512, 128), struct(T + 8, 128), struct(T, 128)],
        compiler_params=pltpu.CompilerParams(vmem_limit_bytes=VMEM),
        name="prep",
    )(mix_in, mix_in, cot_wave, w_in, w_out, w_mask, *vectors)
    pack_x = lax.ppermute(pack, "src", cross)
    pack_core = lax.ppermute(pack, "src", swap)
    mix_prev = lax.ppermute(high, "tm", up)
    mix_next = lax.ppermute(low, "tm", down)
    msg1 = call(
        first_kernel, "first", 2,
        [pl.BlockSpec((frames // 2, 128), lambda i, n: (i, 0)), whole(128, 128), whole(1, 128), whole(1, 128)],
        whole(*msg_shape), message,
        [vmem(1, 2 * n1, 128), vmem(1, 2 * n1, 128), vmem(2 * n1, 128), vmem(2 * n1, 128)], 4,
    )(lengths, mix_in, w_in, line(b_in), line(slope_in))
    msg1, pack_x, pack_core, mix_prev, mix_next = lax.optimization_barrier(
        (msg1, pack_x, pack_core, mix_prev, mix_next)
    )
    pack_far = lax.ppermute(pack_x, "src", swap)
    packs = (pack, pack_core, pack_x, pack_far)
    msg1 = exchange(msg1)
    wide_x = lax.ppermute(wide, "src", cross)
    wide_core = lax.ppermute(wide, "src", swap)
    wide_far = lax.ppermute(wide_x, "src", swap)
    wides = (wide, wide_core, wide_x, wide_far)

    entries = -(-2 * (tiles + 1) // 8) * 8
    hidden, depth, msg2, vec, table_in = call(
        depth_kernel, "depth", tiles + 2,
        [
            whole(*msg_shape),
            whole(frames, 128), whole(T, 128), whole(T + 8, 128), *[whole(PACK_IN, 128)] * 4,
        ],
        [
            pl.BlockSpec((T, HIDDEN), lambda i, n: (i, 0)),
            pl.BlockSpec((T, HIDDEN), lambda i, n: (jnp.maximum(i - 1, 0), 0)),
            whole(*msg_shape), whole(NVEC, HIDDEN), whole(2, padded, LANES),
        ],
        [
            struct(own_rows + 2 * T, HIDDEN), struct(own_rows + T, HIDDEN), message, struct(NVEC, HIDDEN),
            struct(2, padded, LANES),
        ],
        [
            vmem(4, PACK_IN, 128), vmem16(512, HIDDEN), vmem(2, T, HIDDEN),
            vmem(4, entries, 128), vmem(4, entries, 128), vmem(entries, 128), vmem(entries, 128),
        ], 8,
    )(lengths, msg1, mix_in, mix_prev, mix_next, *packs)
    msg2 = exchange(msg2)

    def half_rows(width):
        return pl.BlockSpec((TM, width), lambda i, n: (half() * tiles_m + i, 0))

    def rows_m(width):
        return pl.BlockSpec((TM, width), lambda i, n: (i, 0))

    def depth_piece(k):
        return pl.BlockSpec((STEP, HIDDEN), lambda i, n: (TM // STEP * i + 1 + k, 0))

    packed = call(
        cotangent_kernel, "cotangent", tiles_m,
        [
            pl.BlockSpec((2, TM * STRIDE), lambda i, n: (0, half() * tiles_m + i)),
            pl.BlockSpec(
                (2, LANES),
                lambda i, n: (0, jnp.minimum((half() * tiles_m + i + 1) * (TM // 16), (2 * tiles_m) * (TM // 16) - 1)),
            ),
            whole(T + 8, 128), anywhere,
        ],
        rows_m(128), jax.ShapeDtypeStruct((own_rows, 128), BF16), [], 6,
    )(lengths, cot_wave, cot_wave, mix_next, vec)
    pieces = TM // STEP
    (block_out, grad_skip, grad_enc, send, wave_half, r, r_up, r_down, keep, give, msg3, table_mid, w_out_t) = call(
        mask_kernel, "mask", tiles_m,
        [
            whole(*msg_shape), *[depth_piece(k) for k in range(pieces)],
            half_rows(128), half_rows(128), half_rows(HIDDEN), half_rows(128),
            rows_m(128), whole(L, HIDDEN), whole(NVEC, HIDDEN), whole(1, 256), whole(1, 128),
            *[whole(512, 128)] * 4,
        ],
        [
            half_rows(128), half_rows(128), half_rows(HIDDEN), rows_m(768),
            pl.BlockSpec((2, TM * STRIDE), lambda i, n: (0, i)),
            rows_m(HIDDEN), whole(136, 256), whole(128, 256), whole(EARLY, 128), whole(EARLY, 128),
            whole(*msg_shape), whole(2, padded, LANES), whole(768, HIDDEN),
        ],
        [
            struct(frames, 128), struct(frames, 128), struct(frames, HIDDEN), struct(own_rows, 768),
            struct(2, own_rows * STRIDE), struct(own_rows, HIDDEN), struct(136, 256), struct(128, 256),
            struct(EARLY, 128), struct(EARLY, 128), message, struct(2, padded, LANES),
            jax.ShapeDtypeStruct((768, HIDDEN), BF16),
        ],
        [
            vmem(4, 512, 128), vmem16(1536, 256),
            vmem16(512, 1024), vmem16(2, 2, 512, 256), vmem16(2, 768, 256), vmem16(128, 1024), vmem(TM, HIDDEN), vmem(TM, HIDDEN), vmem(8, 128), vmem(256, 256), vmem(128, HIDDEN),
            vmem(2, 128, HIDDEN), vmem(8, HIDDEN), vmem(8, 128),
            vmem(8, 2 * tiles, 128), vmem(2 * tiles, 128),
        ], 28,
    )(
        lengths, msg2, *[depth] * pieces, mix_in, skip_in, encoded, cot_out, packed, basis.T, vec,
        line(b_out), line(slope_skip), *wides,
    )

    both = ("tm", "src")
    later, earlier = [], []
    for i in range(n_tm):
        for s in range(n_src):
            here = i * n_src + s
            there = here + 1 if s % 2 == 0 else (i + 1) * n_src + s - 1
            if s % 2 == 0 or i + 1 < n_tm:
                later.append((here, there))
                earlier.append((there, here))
    hops = [[(i, i ^ (1 << bit)) for i in range(n_tm)] for bit in range(n_tm.bit_length() - 1)]
    early = keep + lax.ppermute(give, "src", swap)
    got_low = lax.ppermute(r_up, both, later)
    got_high = lax.ppermute(r_down, both, earlier)
    msg3 = exchange(msg3)
    early, send, wave_half = lax.optimization_barrier((early, send, wave_half))
    early_other = lax.ppermute(early, "tm", hops[0])
    got = lax.ppermute(send, "src", swap)
    wave_other = lax.ppermute(wave_half, "src", swap)
    msg3, got_low, got_high, early, early_other, got, wave_other = lax.optimization_barrier(
        (msg3, got_low, got_high, early, early_other, got, wave_other)
    )
    early = early + early_other
    early_other = lax.ppermute(early, "tm", hops[-1])

    def rows(width):
        return pl.BlockSpec((T, width), lambda i, n: (i, 0))

    def own_tile(width):
        return pl.BlockSpec((T, width), lambda i, n: (half() * tiles + jnp.maximum(i - 1, 0), 0))

    def other_rows(width):
        return pl.BlockSpec((T, width), lambda i, n: ((1 - half()) * tiles + jnp.minimum(i, tiles - 1), 0))

    grad_mix, mix_send, keep, give, edge, block_out, grad_skip, grad_enc = call(
        back_kernel, "back", tiles + 1,
        [
            whole(*msg_shape), rows(HIDDEN),
            pl.BlockSpec((STEP, HIDDEN), lambda i, n: (jnp.maximum(2 * i - 1, 0), 0)),
            pl.BlockSpec((STEP, HIDDEN), lambda i, n: (jnp.minimum(2 * i, 2 * tiles - 1), 0)),
            whole(136, 256), whole(128, 256),
            pl.BlockSpec((T, HIDDEN), lambda i, n: (jnp.maximum(i, 1), 0)), own_tile(128), own_tile(128),
            whole(NVEC, HIDDEN), whole(2, padded, LANES), whole(2, padded, LANES), whole(768, HIDDEN),
            *[whole(128, 128)] * 4,
            pl.BlockSpec((T, 768), lambda i, n: (jnp.minimum(i, tiles - 1), 0)), anywhere, anywhere, anywhere,
        ],
        [
            own_tile(128), pl.BlockSpec((T, 128), lambda i, n: (jnp.maximum(i - 1, 0), 0)),
            whole(144, 128), whole(144, 128), whole(8, 128), other_rows(128), other_rows(128), other_rows(HIDDEN),
        ],
        [
            struct(frames, 128), struct(own_rows, 128), struct(144, 128), struct(144, 128), struct(8, 128),
            struct(frames, 128), struct(frames, 128), struct(frames, HIDDEN),
        ],
        [
            vmem(4, 128, 128), vmem(4, padded, LANES), vmem16(1024, 256),
            vmem(2, T, HIDDEN), vmem(2, 128, HIDDEN), vmem(512, 256), vmem(16, HIDDEN),
        ], 13,
        input_output_aliases={19: 5, 20: 6, 21: 7},
    )(
        lengths, msg3, depth, r, r, got_low, got_high, hidden, mix_in, cot_out, vec, table_in, table_mid, w_out_t, *packs, got,
        block_out, grad_skip, grad_enc,
    )

    grad_mix, mix_send, keep, give, edge, early_other = lax.optimization_barrier(
        (grad_mix, mix_send, keep, give, edge, early_other)
    )
    late_give = lax.ppermute(give, "src", swap)
    early = early + early_other
    for hop in hops[1:-1]:
        early_other = lax.ppermute(early, "tm", hop)
        if hop is not hops[-2]:
            early = early + early_other
    late_give, early = lax.optimization_barrier((late_give, early))
    late = keep + late_give
    late, edge, mix_send = lax.optimization_barrier((late, edge, mix_send))
    late_other = lax.ppermute(late, "tm", hops[0])
    mix_got = lax.ppermute(mix_send, "src", swap)
    edge_other = lax.ppermute(edge, "src", swap)
    late, late_other, early, mix_got, edge_other = lax.optimization_barrier(
        (late, late_other, early, mix_got, edge_other)
    )
    late = late + late_other
    lates = [late]
    for k in range(1, n_tm // 2):
        lates.append(lax.ppermute(late, "tm", [(i, i ^ (2 * k)) for i in range(n_tm)]))
    wave_width = own_rows * STRIDE
    late, mix_got, edge_other = lax.optimization_barrier((late, mix_got, edge_other))
    grad_mix, wave = call(
        merge_kernel, "merge", 1,
        [
            whole(own_rows, 128), anywhere, whole(2, wave_width), whole(2, wave_width), whole(8, 128), whole(8, 128),
        ],
        [pl.BlockSpec((own_rows, 128), lambda i, n: (1 - half(), 0)), whole(2, 2 * wave_width)],
        [struct(frames, 128), struct(2, 2 * wave_width)], [], 3,
        input_output_aliases={2: 0},
    )(lengths, mix_got, grad_mix, wave_half, wave_other, edge, edge_other)
    *lates, grad_mix, wave = lax.optimization_barrier((*lates, grad_mix, wave))

    parts = (early, early_other, *lates)
    shapes = (
        (128, 128), (1, 128), (1, 128), (1, 128), (1, 128), (3, 128), (1, 128), (1, 128), (1, 128), (1, 128), (128, 256),
        (1, 256), (1, 128), (128, 256), (1, 256), (L, HIDDEN),
    )
    outs = pl.pallas_call(
        functools.partial(last_kernel, len(lates)),
        grid=(1,),
        in_specs=[fixed(*part.shape) for part in parts],
        out_specs=[fixed(*shape) for shape in shapes],
        out_shape=[struct(*shape) for shape in shapes],
        compiler_params=pltpu.CompilerParams(vmem_limit_bytes=VMEM),
        name="last",
    )(*parts)
    outs = [o.reshape(-1) if o.shape[0] == 1 else o for o in outs[:-1]] + [outs[-1].T]
    return (block_out, wave, grad_mix, grad_skip, grad_enc, *outs)


def solution(mesh):
    frames, channels = P("tm", None), P("src")
    in_specs = (
        frames, frames, frames, P(), P(None, "src"), channels, channels, channels, channels, P(None, "src"), channels,
        channels, channels, channels, P("src", None), P(), P(), P(None, "src"), channels, P(), frames, P(None, "tm"),
    )
    out_specs = (
        frames, P(None, "tm"), frames, frames, frames, P(None, "src"), channels, channels, channels, channels,
        P(None, "src"), channels, channels, channels, channels, P("src", None), P(), P(), P(None, "src"), channels,
        P(),
    )
    return jax.shard_map(local, mesh=mesh, in_specs=in_specs, out_specs=out_specs, check_vma=False)
```

```python
import functools

import jax
import jax.numpy as jnp
from jax import lax
from jax.experimental import pallas as pl
from jax.experimental.pallas import tpu as pltpu
from jax.sharding import PartitionSpec as P

L = 16
STRIDE = L // 2
HIDDEN = 512
STEP = 128
EPS = 1e-05
T = 256
T1 = 512
TM = 512
ROWS = 16
LANES = 128
GROUP = 16
F32 = jnp.float32
BF16 = jnp.bfloat16
NVEC = 16
PACK_IN = 128 + NVEC
PACK = PACK_IN + 512
EARLY = 584
VMEM = 64 * 2**20 - 2**15
LOG2E = 1.4426950408889634


def split(x):
    hi = x.astype(BF16)
    return hi, (x - hi.astype(F32)).astype(BF16)


def mm(a, b):
    return lax.dot_general(a, b, (((1,), (0,)), ((), ())), preferred_element_type=F32)


def mm_tn(a, b):
    return lax.dot_general(a, b, (((0,), (0,)), ((), ())), preferred_element_type=F32)


def mm_nt(a, b):
    return lax.dot_general(a, b, (((1,), (1,)), ((), ())), preferred_element_type=F32)


def cat(parts, axis):
    return jnp.concatenate(parts, axis=axis)


def three(x, axis):
    hi, lo = x
    return cat([hi, lo, hi], axis)


def two_of(x, axis):
    hi, lo = x
    return cat([hi, hi, lo], axis)


def iota(shape, axis):
    return lax.broadcasted_iota(jnp.int32, shape, axis)


def sigmoid(x):
    return 1.0 / (1.0 + jnp.exp2(x * -LOG2E))


def colsum(x):
    return jnp.sum(x, axis=0, keepdims=True)


def fold(x):
    total = x[0:8]
    for i in range(8, x.shape[0], 8):
        total = total + x[i : i + 8]
    return total


def plus(a, b):
    return b if a is None else a + b


def column(c):
    return slice(c * LANES, (c + 1) * LANES)


def ones_block(rows):
    return jnp.where(iota((rows, LANES), 1) < 3, 1.0, 0.0).astype(BF16)


def bias_rows(bias, rows):
    hi, lo = split(bias)
    low = (bias - hi.astype(F32) - lo.astype(F32)).astype(BF16)
    place = iota((rows, bias.shape[1]), 0)
    zero = jnp.zeros((rows, bias.shape[1]), F32)
    out = jnp.where(place == 0, hi.astype(F32), zero)
    out = jnp.where(place == 1, lo.astype(F32), out)
    return jnp.where(place == 2, low.astype(F32), out).astype(BF16)


def item_ends(len_ref):
    ends, total = [], jnp.int32(0)
    for k in range(len_ref.shape[0]):
        total = total + len_ref[k]
        ends.append(total)
    return ends


def boundary(ends, start):
    ahead = jnp.where(start - STEP >= 0, 0, -1)
    for end in ends:
        ahead = ahead + (end <= start - STEP).astype(jnp.int32)
    edge = jnp.int32(0)
    for k, end in enumerate(ends):
        edge = jnp.where(ahead == k, end, edge)
    return edge, ahead


def item_rows(ahead, items):
    return jnp.maximum(ahead, 0), jnp.minimum(ahead + 1, items - 1)


def lane_items(ahead, items):
    lane = iota((1, LANES), 1)
    return (lane == ahead).astype(F32), (lane == ahead + 1).astype(F32)


def put_statistics(msg_ref, sums, squares, counts, onehot):
    groups = sums.shape[0]
    count = counts[:, :1]
    safe = jnp.maximum(count, 1.0)
    total = jnp.sum(jnp.sum(sums, axis=0), axis=1, keepdims=True)
    number = count * (groups * LANES)
    mean = total / jnp.maximum(number, 1.0)
    spread = 0.0
    for g in range(groups):
        away = sums[g] / safe - mean
        spread = spread + squares[g] + count * away * away
    spread = jnp.sum(spread, axis=1, keepdims=True)
    item_sum = colsum(onehot * total)
    item_number = colsum(onehot * number)
    item_mean = item_sum / jnp.maximum(item_number, 1.0)
    away = mean - item_mean
    item_spread = colsum(onehot * (spread + number * away * away))
    lines = (item_sum, item_spread, item_number, item_mean)
    if msg_ref.shape[1] == 1:
        msg = lines[0]
        for k, line in enumerate(lines[1:]):
            msg = msg + pltpu.roll(line, GROUP * (k + 1), 1)
    else:
        msg = cat([*lines, jnp.zeros((4, LANES), F32)], 0)
    for i in range(msg_ref.shape[0]):
        msg_ref[i] = msg


def to_rows(row, items_padded):
    wide = jnp.broadcast_to(row, (items_padded, LANES))
    own = iota((items_padded, LANES), 0) == iota((items_padded, LANES), 1)
    column = jnp.sum(jnp.where(own, wide, 0.0), axis=1, keepdims=True)
    return jnp.broadcast_to(column, (items_padded, LANES))


def merge_statistics(msg_ref, table_ref):
    msg = msg_ref[...]
    if msg_ref.shape[1] == 1:
        totals = jnp.sum(msg, axis=0)
        first = iota((1, LANES), 1) < GROUP
        item_sum = jnp.where(first, totals, 0.0)
        number = jnp.where(first, pltpu.roll(totals, LANES - 2 * GROUP, 1), 0.0)
        mean = item_sum / jnp.maximum(number, 1.0)
        away = msg - pltpu.roll(mean, 3 * GROUP, 1)[None]
        around = jnp.sum(pltpu.roll(msg, GROUP, 2) * away * away, axis=0)
        squares = pltpu.roll(totals, LANES - GROUP, 1) + pltpu.roll(around, LANES - 3 * GROUP, 1)
        squares = jnp.where(first, squares, 0.0)
    else:
        item_sum = jnp.sum(msg[:, 0:1, :], axis=0)
        number = jnp.sum(msg[:, 2:3, :], axis=0)
        mean = item_sum / jnp.maximum(number, 1.0)
        away = msg[:, 3:4, :] - mean[None]
        squares = jnp.sum(msg[:, 1:2, :] + msg[:, 2:3, :] * away * away, axis=0)
    inverse = lax.rsqrt(squares / jnp.maximum(number, 1.0) + EPS)
    padded = table_ref.shape[1]
    table_ref[0] = to_rows(mean, padded)
    table_ref[1] = to_rows(inverse, padded)


def put_entry(refs, groups, entry, sums, squares, number, hot):
    sums_ref, squares_ref, counts_ref, onehot_ref = refs
    row = pl.ds(entry, 1)
    for g in range(groups):
        sums_ref[g, row, :] = sums[g]
        squares_ref[g, row, :] = squares[g]
    counts_ref[row, :] = jnp.full((1, LANES), number, F32)
    onehot_ref[row, :] = hot


def general_entries(refs, acts, after, before, n_after, n_before, entry, ahead):
    hot_b, hot_a = lane_items(ahead, 0)
    for part, keep, number, hot in ((0, before, n_before, hot_b), (1, after, n_after, hot_a)):
        sums, squares = [], []
        for act in acts:
            total = colsum(jnp.where(keep, act, 0.0))
            away = act - total / jnp.maximum(number, 1.0)
            sums.append(total)
            squares.append(colsum(jnp.where(keep, away * away, 0.0)))
        put_entry(refs, len(acts), 2 * entry + part, sums, squares, number, hot)


def prep_kernel(
    top_ref, bottom_ref, cot_ref, w_in_ref, w_out_ref, w_mask_ref, b_in, slope_in, gain_in, beta_in, w_depth, b_depth,
    slope_mid, gain_mid, beta_mid, b_mask, pack_ref, wide_ref, low_ref, high_ref,
):
    pack_ref[0:128, :] = w_in_ref[...]
    vectors = (b_in, slope_in, gain_in, beta_in, w_depth, b_depth, slope_mid, gain_mid, beta_mid)
    bias = b_mask[...]
    pack_ref[128:144, :] = cat(
        [ref[...] for ref in vectors] + [bias[:, 0:128], bias[:, 128:256], jnp.zeros((3, LANES), F32)], 0
    )
    for k in range(2):
        wide_ref[128 * k : 128 * (k + 1), :] = w_out_ref[:, column(k)]
        wide_ref[128 * (k + 2) : 128 * (k + 3), :] = w_mask_ref[:, column(k)]
    low_ref[0:T, :] = top_ref[...]
    low_ref[T : T + 8, :] = cat([cot_ref[...], jnp.zeros((6, LANES), F32)], 0)
    high_ref[...] = bottom_ref[...]


def first_kernel(len_ref, mix_ref, w_in_ref, b_in, slope_in, msg_ref, sums, squares, counts, onehot):
    step = pl.program_id(0)
    last = pl.num_programs(0) - 1
    tiles = mix_ref.shape[0] // T1
    ends = item_ends(len_ref)
    weights = two_of(split(w_in_ref[...]), 0)
    slope = slope_in[...]
    keep = 1.0 - slope
    bias = b_in[...]
    refs = (sums, squares, counts, onehot)
    for t in range(tiles):
        j = step * tiles + t
        start = lax.axis_index("tm") * ((last + 1) * tiles * T1) + j * T1
        edge, ahead = boundary(ends, start)
        hidden = mm(three(split(mix_ref[t * T1 : (t + 1) * T1, :]), 1), weights)
        pieces, total = [], None
        for i in range(0, T1, ROWS):
            x = hidden[i : i + ROWS] + bias
            act = x * (slope + keep * sigmoid(x))
            pieces.append(act)
            total = plus(total, fold(act))
        total = colsum(total)
        mean = total / T1
        square = None
        for act in pieces:
            away = act - mean
            square = plus(square, fold(away * away))
        put_entry(refs, 1, 2 * j, [total], [colsum(square)], jnp.float32(T1), lane_items(ahead, 0)[0])
        nothing = jnp.zeros((1, LANES), F32)
        put_entry(refs, 1, 2 * j + 1, [nothing], [nothing], jnp.float32(0.0), nothing)

        @pl.when(edge < start + T1)
        def _():
            offset = iota((T1, LANES), 0) + (start - edge)
            n_before = jnp.clip(edge - start, 0, T1).astype(F32)
            act = cat(pieces, 0)
            general_entries(refs, [act], offset >= 0, offset < 0, T1 - n_before, n_before, j, ahead)

    @pl.when(step == last)
    def _():
        put_statistics(msg_ref, sums[...], squares[...], counts[...], onehot[...])


def depth_kernel(
    len_ref, msg_in_ref, mix_ref, prev_ref, next_ref, own_ref, core_ref, x_ref, far_ref,
    hidden_ref, depth_ref, msg_ref, vec_ref, table_ref,
    gathered, weights, ring, sums, squares, counts, onehot,
):
    m = pl.program_id(0)
    last = pl.num_programs(0) - 1
    items = len_ref.shape[0]
    me = lax.axis_index("src")
    half = me & 1
    own_rows = (last - 1) * T

    @pl.when(m == 0)
    def _():
        for k, ref in enumerate((own_ref, core_ref, x_ref, far_ref)):
            gathered[half ^ k] = ref[...]
        merge_statistics(msg_in_ref, table_ref)
        for ref in (sums, squares, counts, onehot):
            ref[...] = jnp.zeros_like(ref)
        for s in range(4):
            cut = column(s)
            weights[0:384, cut] = two_of(split(gathered[s, 0:128, :]), 0)
            weights[384:512, cut] = bias_rows(gathered[s, 128:129, :], 128)
            vec_ref[:, cut] = gathered[s, 128 : 128 + NVEC, :]

    def vec(row, c):
        return vec_ref[row : row + 1, column(c)]

    ends = item_ends(len_ref)
    base = lax.axis_index("tm") * (2 * own_rows) + half * own_rows
    start = base + (m - 1) * T
    edge, ahead = boundary(ends, start)
    alone = edge >= start + T
    block = half * (own_rows // T) + m - 1
    top = 2 * (own_rows // T)
    new, old = m & 1, 1 - (m & 1)

    def norm_rows(alone):
        place = pl.multiple_of(jnp.clip(block, 0, top - 1) * T, T)
        mix = mix_ref[pl.ds(place, T), :]
        mix = jnp.where(block < 0, prev_ref[...], jnp.where(block >= top, next_ref[0:T, :], mix))
        mixed = split(mix)
        hidden = mm(cat([mixed[0], mixed[1], mixed[0], ones_block(T)], 1), weights[...])
        hidden_ref[...] = hidden
        row_b, row_a = item_rows(ahead, items)
        rows = iota((ROWS, LANES), 0) + (start - edge)
        for c in range(4):
            slope = vec(1, c)
            keep = 1.0 - slope
            scale_b = table_ref[1, pl.ds(row_b, 1), :] * vec(2, c)
            shift_b = vec(3, c) - table_ref[0, pl.ds(row_b, 1), :] * scale_b
            scale_a = table_ref[1, pl.ds(row_a, 1), :] * vec(2, c)
            shift_a = vec(3, c) - table_ref[0, pl.ds(row_a, 1), :] * scale_a
            for i in range(0, T, ROWS):
                x = hidden[i : i + ROWS, column(c)]
                act = x * (slope + keep * sigmoid(x))
                if alone:
                    value = act * scale_b + shift_b
                else:
                    after = rows + i >= 0
                    value = act * jnp.where(after, scale_a, scale_b) + jnp.where(after, shift_a, shift_b)
                ring[new, i : i + ROWS, column(c)] = value

    pl.when(alone)(lambda: norm_rows(True))
    pl.when(jnp.logical_not(alone))(lambda: norm_rows(False))

    begin = start - STEP
    edge2, ahead2 = boundary(ends, begin)
    plain = edge2 >= begin + T + STEP
    refs = (sums, squares, counts, onehot)

    def filtered(c, i, lower_weight, upper_weight):
        lower = ring[old, i : i + ROWS, column(c)]
        upper = ring[new, i : i + ROWS, column(c)]
        if i < STEP:
            middle = ring[old, i + STEP : i + STEP + ROWS, column(c)]
        else:
            middle = ring[new, i - STEP : i - STEP + ROWS, column(c)]
        return lower_weight * lower + vec(5, c) * middle + upper_weight * upper + vec(7, c)

    @pl.when((m > 0) & plain)
    def _():
        in_low = jnp.where(m > 1, 1.0, 0.0)
        in_high = jnp.where(m < last, 1.0, 0.0)
        number = STEP * (in_low + in_high)
        all_sums, all_squares = [], []
        for c in range(4):
            slope = vec(8, c)
            keep = 1.0 - slope
            acts, halves = [], [None, None]
            for i in range(0, T, ROWS):
                depth = filtered(c, i, vec(4, c), vec(6, c))
                depth_ref[i : i + ROWS, column(c)] = depth
                act = depth * (slope + keep * sigmoid(depth))
                acts.append(act)
                halves[i // STEP] = plus(halves[i // STEP], fold(act))
            total = in_low * colsum(halves[0]) + in_high * colsum(halves[1])
            mean = total / number
            halves = [None, None]
            for i, act in enumerate(acts):
                away = act - mean
                halves[i * ROWS // STEP] = plus(halves[i * ROWS // STEP], fold(away * away))
            all_sums.append(total)
            all_squares.append(in_low * colsum(halves[0]) + in_high * colsum(halves[1]))
        put_entry(refs, 4, 2 * (m - 1), all_sums, all_squares, number, lane_items(ahead2, 0)[0])

    @pl.when((m > 0) & jnp.logical_not(plain))
    def _():
        low = jnp.where(m == 1, STEP, 0)
        high = jnp.where(m == last, STEP, T)
        rows = iota((ROWS, LANES), 0) + (begin - edge2)
        acts = []
        for c in range(4):
            slope = vec(8, c)
            pieces = []
            for i in range(0, T, ROWS):
                offset = rows + i
                lower_weight = jnp.where((offset >= 0) & (offset < STEP), 0.0, vec(4, c))
                upper_weight = jnp.where((offset < 0) & (offset >= -STEP), 0.0, vec(6, c))
                depth = filtered(c, i, lower_weight, upper_weight)
                depth_ref[i : i + ROWS, column(c)] = depth
                pieces.append(depth * (slope + (1.0 - slope) * sigmoid(depth)))
            acts.append(cat(pieces, 0))
        row = iota((T, LANES), 0)
        own = (row >= low) & (row < high)
        offset = row + (begin - edge2)
        n_before = jnp.clip(edge2 - begin, low, high) - low
        n_after = (high - low - n_before).astype(F32)
        general_entries(
            refs, acts, own & (offset >= 0), own & (offset < 0), n_after, n_before.astype(F32), m - 1, ahead2
        )

    @pl.when(m == last)
    def _():
        put_statistics(msg_ref, sums[...], squares[...], counts[...], onehot[...])


def cotangent_kernel(len_ref, wave_cot_ref, wave_next_ref, edge_next_ref, after_ref, packed_ref):
    j = pl.program_id(0)
    last = pl.num_programs(0) - 1
    me = lax.axis_index("src")
    half = me & 1
    side = me >> 1
    own_rows = (last + 1) * TM
    start = lax.axis_index("tm") * (2 * own_rows) + half * own_rows + j * TM
    edge, _ = boundary(item_ends(len_ref), start)
    offset = iota((TM, LANES), 0) + (start - edge)
    selects_hi, selects_lo = [], []
    for c in range(2):
        row = iota((2 * LANES, LANES), 0)
        col = iota((2 * LANES, LANES), 1) - 48 * c
        place = (row & 7) + ((row >> 7) << 3)
        selects_hi.append(((col == place) | (col == place + 16)).astype(F32).astype(BF16))
        selects_lo.append((col == place + 32).astype(F32).astype(BF16))

    lane_frame = iota((16, LANES), 1) >> 3
    frame = iota((16, LANES), 0)
    here = jnp.where(lane_frame == frame, 1.0, 0.0)
    coming = jnp.where(lane_frame == ((frame + 1) & 15), 1.0, 0.0)
    final_row = frame == 15
    packed = None
    waves = [wave_cot_ref[0:1, :], wave_cot_ref[1:2, :]]
    finals = [
        jnp.where((half == 1) & (j == last), edge_next_ref[T + c : T + c + 1, :], wave_next_ref[c : c + 1, :])
        for c in range(2)
    ]
    for c in range(2):
        wave = jnp.where(side == 0, waves[c], waves[1 - c])
        final = jnp.where(side == 0, finals[c], finals[1 - c])
        for part, select in zip(split(cat([wave, final], 1)), (selects_hi, selects_lo)):
            part = part.astype(F32)
            lines = [part[:, column(q)] for q in range(TM // 16 + 1)]
            pieces = []
            for q in range(TM // 16):
                following = jnp.where(final_row, lines[q + 1], lines[q]) * coming
                pieces.append(cat([lines[q] * here, following], 1).astype(BF16))
            packed = plus(packed, mm(cat(pieces, 0), select[c]))
    lane = iota((1, LANES), 1)
    lane = jnp.where(lane < 48, lane, lane - 48)
    packed_ref[...] = jnp.where((offset == -1) & ((lane & 15) >= 8), 0.0, packed).astype(BF16)


def mask_kernel(
    len_ref, msg_in_ref, *refs,
):
    depth_refs = refs[: TM // STEP]
    (
        mix_ref, skip_ref, enc_ref, cot_ref, packed_ref, basis_ref, vec_ref,
        b_out_ref, slope_skip_ref, own_ref, core_ref, x_ref, far_ref,
        block_ref, grad_skip_ref, grad_enc_ref, send_ref, wave_ref, r_ref, up_ref, down_ref, keep_ref, give_ref,
        msg_ref, table_ref, w_out_t,
        gathered, w_out, w_mask, w_mask_t, decode, basis_back, normed_ref,
        pull_ref, carry, acc_out, acc_mask, acc_basis, acc_vec,
        acc_small, entries, onehot,
    ) = refs[TM // STEP :]
    j = pl.program_id(0)
    last = pl.num_programs(0) - 1
    items = len_ref.shape[0]
    me = lax.axis_index("src")
    half = me & 1
    side = me >> 1
    own_rows = (last + 1) * TM

    def vec(row, c):
        return vec_ref[row : row + 1, column(c)]

    @pl.when(j == 0)
    def _():
        for k, ref in enumerate((own_ref, core_ref, x_ref, far_ref)):
            gathered[half ^ k] = ref[...]
        merge_statistics(msg_in_ref, table_ref)
        for ref in (acc_out, acc_mask, acc_basis, acc_vec, acc_small, carry, entries):
            ref[...] = jnp.zeros_like(ref)
        basis = split(basis_ref[...])
        b_hi, b_lo = basis
        col = iota((L, 2 * LANES), 1)
        row = iota((L, 2 * LANES), 0)
        spread = ((col & 7) == (row & 7)) & ((col >> 7) == (row >> 3))
        spread = spread.astype(F32).astype(BF16)
        wide = (mm_tn(b_hi, spread).astype(BF16), mm_tn(b_lo, spread).astype(BF16))
        for n in range(2):
            decode[n] = two_of([part[n * 256 : (n + 1) * 256] for part in wide], 0)
        for c in range(2):
            row = iota((LANES, L), 0) - 48 * c
            col = iota((LANES, L), 1)
            with_hi = ((row == col) | (row == col + 32)).astype(F32).astype(BF16)
            with_lo = (row == col + 16).astype(F32).astype(BF16)
            back = mm(with_hi, b_hi) + mm(with_lo, b_lo)
            basis_back[:, c * HIDDEN : (c + 1) * HIDDEN] = back.astype(BF16)
        for s in range(4):
            cut = column(s)
            for k in range(2):
                part = gathered[s, column(k), :]
                hi, lo = split(part)
                for place, value in ((0, hi), (256, hi), (512, lo)):
                    place = place + (s >> 1) * 768 + (s & 1) * 128
                    w_out[place : place + 128, column(k)] = value
                hi, lo = split(part.T)
                for place, value in ((0, hi), (256, hi), (512, lo)):
                    w_out_t[place + k * 128 : place + (k + 1) * 128, cut] = value
                part = gathered[s, column(2 + k), :]
                wide = slice(s * 256 + k * LANES, s * 256 + (k + 1) * LANES)
                w_mask[0:384, wide] = two_of(split(part * -LOG2E), 0)
                w_mask[384:512, wide] = bias_rows(vec_ref[11 + k : 12 + k, cut] * -LOG2E, 128)
                hi, lo = split(part.T)
                for place in (0, 256):
                    w_mask_t[s >> 1, s & 1, place + k * 128 : place + (k + 1) * 128, 0:128] = hi
                    w_mask_t[s >> 1, s & 1, place + k * 128 : place + (k + 1) * 128, 128:256] = lo

    ends = item_ends(len_ref)
    start = lax.axis_index("tm") * (2 * own_rows) + half * own_rows + j * TM
    edge, ahead = boundary(ends, start)
    row_b, row_a = item_rows(ahead, items)
    offset = iota((TM, LANES), 0) + (start - edge)

    lane_frame = iota((16, LANES), 1) >> 3
    here = jnp.where(lane_frame == iota((16, LANES), 0), 1.0, 0.0)
    packed = packed_ref[...]

    chunks = [[slice(c * HIDDEN + n * 256, c * HIDDEN + (n + 1) * 256) for c in range(2)] for n in range(2)]
    all_grads = [[None, None], [None, None]]
    after = offset >= 0
    inv_b, inv_a = table_ref[1, pl.ds(row_b, 1), :], table_ref[1, pl.ds(row_a, 1), :]
    shift_b, shift_a = -inv_b * table_ref[0, pl.ds(row_b, 1), :], -inv_a * table_ref[0, pl.ds(row_a, 1), :]
    inv = jnp.where(after, inv_a, inv_b)
    shift = jnp.where(after, shift_a, shift_b)
    norms = [[], []], [[], []]
    for c in range(4):
        slope = vec(8, c)
        keep = 1.0 - slope
        his, los = [], []
        for i in range(0, TM, ROWS):
            rows = slice(i, i + ROWS)
            depth = depth_refs[i // STEP][i % STEP : i % STEP + ROWS, column(c)]
            s = sigmoid(depth)
            part = keep * s
            mild = slope + part
            normed = depth * mild * inv[rows] + shift[rows]
            normed_ref[rows, column(c)] = normed
            pull_ref[rows, column(c)] = mild + part * (depth * (1.0 - s))
            hi, lo = split(normed * vec(9, c) + vec(10, c))
            his.append(hi)
            los.append(lo)
        norms[c >> 1][0].append(cat(his, 0))
        norms[c >> 1][1].append(cat(los, 0))
        all_grads[c >> 1][c & 1] = mm(packed, basis_back[:, chunks[c >> 1][c & 1]])
    branch = [
        mm(cat(his + los + his, 1), w_out[768 * k : 768 * (k + 1), :]) for k, (his, los) in enumerate(norms)
    ]
    branch = branch[0] + branch[1]
    slope_skip = slope_skip_ref[...]
    keep = 1.0 - slope_skip
    totals, skips, actives = [], [], []
    for i in range(0, TM, ROWS):
        rows = slice(i, i + ROWS)
        block = mix_ref[rows, :] + (branch[rows, 0:128] + b_out_ref[:, 0:128])
        block_ref[rows, :] = block
        send_ref[rows, 0:128] = block
        total = skip_ref[rows, :] + (branch[rows, 128:256] + b_out_ref[:, 128:256])
        s = sigmoid(total)
        part = keep * s
        mild = slope_skip + part
        rest = total * (1.0 - s)
        totals.append(rest)
        skips.append(mild + part * rest)
        actives.append(split(total * mild))
    a_hi, a_lo = cat([a for a, _ in actives], 0), cat([a for _, a in actives], 0)
    query = cat([a_hi, a_lo, a_hi, ones_block(TM)], 1)

    decoded = [None, None]
    back = [None, None]
    masked, grads_hi, grads_lo = [[], []], [], []
    all_logits = [[mm(query, w_mask[:, chunk]) for chunk in chunks[0]], [None, None]]

    def logits_of(c):
        all_logits[1][c] = mm(query, w_mask[:, chunks[1][c]])

    def decode_of(n, c):
        hi, lo = all_blocks[n][c]
        decoded[c] = plus(decoded[c], mm(cat(hi + lo + hi, 1), decode[n]))

    def back_of(n, c):
        hi, lo = all_blocks[n][2 + c]
        back[c] = plus(back[c], mm(cat(hi + lo, 1), w_mask_t[c, n]))

    all_blocks = [[[[], []] for _ in range(4)] for _ in range(2)]
    for n in range(2):
        if n == 0:
            waiting = [functools.partial(logits_of, c) for c in range(2)]
        else:
            waiting = [functools.partial(f, 0, c) for f in (back_of, decode_of) for c in range(2)]
        every = 2 * (TM // ROWS) // len(waiting)
        logits, grads = all_logits[n], all_grads[n]
        blocks = all_blocks[n]
        for b in range(2):
            col = column(2 * n + b)
            bias_sum = None
            pieces = [[[], []] for _ in range(4)]
            for k, i in enumerate(range(0, TM, ROWS)):
                if (b * (TM // ROWS) + k) % every == 0 and waiting:
                    waiting.pop(0)()
                rows = slice(i, i + ROWS)
                enc = enc_ref[rows, col]
                grad_enc = None
                for c in range(2):
                    mask = 1.0 / (1.0 + jnp.exp2(logits[c][rows, column(b)]))
                    grad = grads[c][rows, column(b)]
                    grad_enc = plus(grad_enc, grad * mask)
                    value = mask * enc
                    for h, part in enumerate(split(value)):
                        pieces[c][h].append(part)
                    grad_logits = grad * value * (1.0 - mask)
                    if c == 0:
                        bias_sum = plus(bias_sum, fold(grad_logits))
                    for h, part in enumerate(split(grad_logits)):
                        pieces[2 + c][h].append(part)
                grad_enc_ref[rows, col] = grad_enc
                send_ref[rows, 256 + (2 * n + b) * 128 : 256 + (2 * n + b + 1) * 128] = grad_enc
            acc_vec[2:3, (2 * n + b) * 128 : (2 * n + b + 1) * 128] += colsum(bias_sum)
            for block, piece in zip(blocks, pieces):
                for h in range(2):
                    block[h].append(cat(piece[h], 0))
        for c in range(2):
            masked[c].append(cat(blocks[c][0] + blocks[c][1], 1))
        grads_hi = grads_hi + blocks[2][0]
        grads_lo = grads_lo + blocks[2][1]
    for c in range(2):
        back_of(1, c)
    for c in range(2):
        decode_of(1, c)
    back = back[0] + back[1]
    own_grads = cat(grads_hi + grads_lo, 1)

    pieces, along, cot_sum, skip_sum = [], None, None, None
    for k, i in enumerate(range(0, TM, ROWS)):
        rows = slice(i, i + ROWS)
        grad_active = back[rows, 0:128] + back[rows, 128:256]
        grad_skip = grad_active * skips[k]
        along = plus(along, fold(grad_active * totals[k]))
        grad_skip_ref[rows, :] = grad_skip
        send_ref[rows, 128:256] = grad_skip
        cot = cot_ref[rows, :]
        cot_sum = plus(cot_sum, fold(cot))
        skip_sum = plus(skip_sum, fold(grad_skip))
        pieces.append(split(cat([cot, grad_skip], 1)))
    acc_small[0:1, :] += colsum(along)
    acc_small[1:2, :] += colsum(cot_sum)
    acc_small[2:3, :] += colsum(skip_sum)
    g_hi, g_lo = cat([p for p, _ in pieces], 0), cat([p for _, p in pieces], 0)
    r_ref[...] = mm(three((g_hi, g_lo), 1), w_out_t[...])

    first_row = iota((8, LANES), 0) == 0
    waves = []
    for c in range(2):
        tail = decoded[c][:, 128:256]
        shifted = pltpu.roll(tail, 1, 0)
        shifted = cat([jnp.where(first_row, carry[c : c + 1, :], shifted[0:8]), shifted[8:]], 0)
        carry[c : c + 1, :] = tail[TM - 1 : TM, :]
        value = decoded[c][:, 0:128] + jnp.where(offset == 0, 0.0, shifted)
        lines = []
        for q in range(TM // 16):
            line = value[q * 16 : (q + 1) * 16] * here
            lines.append(colsum(line[0:8] + line[8:16]))
        waves.append(cat(lines, 1))
    wave_ref[0:1, :] = jnp.where(side == 0, waves[0], waves[1])
    wave_ref[1:2, :] = jnp.where(side == 0, waves[1], waves[0])

    @pl.when(j == 0)
    def _():
        down_ref[:, 0:128] = cot_ref[0:128, :]
        down_ref[:, 128:256] = grad_skip_ref[0:128, :]

    @pl.when(j == last)
    def _():
        up_ref[0:128, 0:128] = cot_ref[TM - 128 : TM, :]
        up_ref[0:128, 128:256] = grad_skip_ref[TM - 128 : TM, :]
        up_ref[128:136, :] = jnp.zeros((8, 256), F32)
        up_ref[128:129, 0:128] = jnp.where(side == 0, carry[0:1, :], carry[1:2, :])
        up_ref[129:130, 0:128] = jnp.where(side == 0, carry[1:2, :], carry[0:1, :])

    own_norms = cat(norms[0][0] + norms[0][1] + norms[0][0], 1)

    def weight_gradients(rows):
        for n in range(2):
            for c in range(2):
                values = masked[c][n]
                acc_basis[c, :, 256 * n : 256 * (n + 1)] += mm_tn(
                    cat([packed[rows]] * 2, 0), cat([values[rows, 0:256], values[rows, 256:512]], 0)
                )
            yield
        acc_mask[...] += mm_tn(
            three((a_hi[rows], a_lo[rows]), 0), two_of((own_grads[rows, 0:512], own_grads[rows, 512:1024]), 0)
        )
        yield
        acc_out[...] += mm_tn(
            cat([own_norms[rows, 256 * k : 256 * (k + 1)] for k in range(3)], 0), two_of((g_hi[rows], g_lo[rows]), 0)
        )
        yield

    for k in range(TM // T):
        rows = slice(k * T, (k + 1) * T)
        begin = start + k * T
        edge2, ahead2 = boundary(ends, begin)
        plain = edge2 >= begin + T + STEP
        entry = 2 * (j * (TM // T) + k)
        hot_b, hot_a = lane_items(ahead2, items)
        onehot[pl.ds(entry, 1), :] = hot_b
        onehot[pl.ds(entry + 1, 1), :] = hot_a
        row_b2, row_a2 = item_rows(ahead2, items)

        @pl.when(plain)
        def _():
            products = weight_gradients(rows)
            inverse = table_ref[1, pl.ds(row_b2, 1), :]
            lines = [[None] * 8, [None] * 8]
            for c in range(4):
                next(products)
                taps = vec(4, c) + vec(5, c) + vec(6, c)
                level = vec(7, c) + vec(3, c) * taps
                sums = [None] * 8
                for i in range(k * T, (k + 1) * T, ROWS):
                    cut = slice(i, i + ROWS)
                    r, normed, pull = r_ref[cut, column(c)], normed_ref[cut, column(c)], pull_ref[cut, column(c)]
                    depth = depth_refs[i // STEP][i % STEP : i % STEP + ROWS, column(c)] - level
                    pull_r, pull_n = pull * r, pull * normed
                    values = (
                        r, r * normed, pull_r, pull, pull_n, pull_r * depth, pull * depth, pull_n * depth,
                    )
                    sums = [plus(s, fold(value)) for s, value in zip(sums, values)]
                sums = [colsum(s) for s in sums]
                if c < 2:
                    acc_vec[0:1, column(c)] += sums[1]
                    acc_vec[1:2, column(c)] += sums[0]
                gain, flat = vec(9, c), vec(2, c) * taps * inverse
                scales = (gain, gain, flat * gain, flat, flat, inverse * gain, inverse, inverse)
                lines[c >> 1] = [plus(line, s * scale) for line, s, scale in zip(lines[c >> 1], sums, scales)]
            for i in range(8):
                entries[i, pl.ds(entry, 1), :] = lines[0][i] + lines[1][i]

        @pl.when(jnp.logical_not(plain))
        def _():
            products = weight_gradients(rows)
            place = iota((ROWS, LANES), 0) + (begin - k * T - edge2)
            inv_b, inv_a = table_ref[1, pl.ds(row_b2, 1), :], table_ref[1, pl.ds(row_a2, 1), :]
            before, behind = [None] * 8, [None] * 8
            for c in range(4):
                next(products)
                sum_r, sum_rn = None, None
                for i in range(k * T, (k + 1) * T, ROWS):
                    cut = slice(i, i + ROWS)
                    offset = place + i
                    after = offset >= 0
                    taps = jnp.where(after & (offset < STEP), 0.0, vec(4, c)) + vec(5, c)
                    taps = taps + jnp.where((offset < 0) & (offset >= -STEP), 0.0, vec(6, c))
                    r, normed = r_ref[cut, column(c)], normed_ref[cut, column(c)]
                    pull = pull_ref[cut, column(c)] * jnp.where(after, inv_a, inv_b)
                    depth = depth_refs[i // STEP][i % STEP : i % STEP + ROWS, column(c)]
                    flat = pull * (vec(2, c) * taps)
                    cross = pull * (depth - vec(7, c) - vec(3, c) * taps)
                    r_normed = r * normed
                    sum_r, sum_rn = plus(sum_r, fold(r)), plus(sum_rn, fold(r_normed))
                    q = r * vec(9, c)
                    values = (
                        q, q * normed, flat * q, flat, flat * normed, cross * q, cross, cross * normed,
                    )
                    before = [plus(s, fold(jnp.where(after, 0.0, value))) for s, value in zip(before, values)]
                    behind = [plus(s, fold(jnp.where(after, value, 0.0))) for s, value in zip(behind, values)]
                if c < 2:
                    acc_vec[0:1, column(c)] += colsum(sum_rn)
                    acc_vec[1:2, column(c)] += colsum(sum_r)
            for i in range(8):
                entries[i, pl.ds(entry, 1), :] = colsum(before[i])
                entries[i, pl.ds(entry + 1, 1), :] = colsum(behind[i])

    @pl.when(j == last)
    def _():
        hot = onehot[...]
        lines = [colsum(hot * jnp.sum(entries[i], axis=1, keepdims=True)) for i in range(8)]
        msg = cat(lines, 0)
        for i in range(msg_ref.shape[0]):
            msg_ref[i] = msg
        for ref, h in ((keep_ref, half), (give_ref, 1 - half)):
            own = pl.ds(pl.multiple_of(h * 128, 128), 128)
            ref[0:128, :] = acc_out[own, 0:128]
            ref[128:256, :] = acc_out[own, 128:256]
            for k in range(2):
                pair = pl.ds(pl.multiple_of(h * 256 + k * 128, 128), 128)
                ref[256 + 128 * k : 384 + 128 * k, :] = acc_mask[:, pair]
            bias = acc_vec[2:3, pl.ds(pl.multiple_of(h * 256, 256), 256)]
            ref[512:520, :] = cat(
                [
                    bias[:, 0:128], bias[:, 128:256], acc_vec[0:1, own], acc_vec[1:2, own],
                    acc_small[0:3, :], jnp.zeros((1, LANES), F32),
                ], 0,
            )
            for k in range(4):
                cut = column(k)
                ref[520 + 16 * k : 536 + 16 * k, :] = (acc_basis[0, 0:16, cut] + acc_basis[0, 32:48, cut]) + (
                    acc_basis[1, 48:64, cut] + acc_basis[1, 80:96, cut]
                )


def back_kernel(
    len_ref, msg_in_ref, depth_ref, r_a_ref, r_b_ref, low_ref, high_ref, hidden_ref, mix_ref, cot_ref,
    vec_ref, table_in_ref, table_mid_ref, w_out_t, own_ref, core_ref, x_ref, far_ref, got_ref, block_in, skip_in, enc_in,
    grad_mix_ref, send_ref, keep_ref, give_ref, edge_ref, block_ref, skip_ref, enc_ref,
    gathered, table, weights, ring, halo, acc_w, acc_vec,
):
    j = pl.program_id(0)
    last = pl.num_programs(0) - 1
    items = len_ref.shape[0]
    me = lax.axis_index("src")
    half = me & 1
    side = me >> 1
    own_rows = last * T

    def vec(row, c):
        return vec_ref[row : row + 1, column(c)]

    ends = item_ends(len_ref)

    @pl.when(j == 0)
    def _():
        for k, ref in enumerate((own_ref, core_ref, x_ref, far_ref)):
            gathered[half ^ k] = ref[...]
        totals = 0.5 * jnp.sum(msg_in_ref[...], axis=0)
        lane = iota((1, LANES), 1)
        number = jnp.zeros((1, LANES), jnp.int32)
        for k in range(items):
            number = jnp.where(lane == k, len_ref[k], number)
        number = jnp.maximum(number.astype(F32) * HIDDEN, 1.0)
        m1 = totals[0:1] / number
        m2 = totals[1:2] / number
        p1 = (totals[2:3] - m1 * totals[3:4] - m2 * totals[4:5]) / number
        p2 = (totals[5:6] - m1 * totals[6:7] - m2 * totals[7:8]) / number
        padded = table.shape[1]
        for i, value in enumerate((m1, m2, p1, p2)):
            table[i] = to_rows(value, padded)
        acc_w[...] = jnp.zeros_like(acc_w)
        acc_vec[...] = jnp.zeros_like(acc_vec)
        edge_ref[...] = low_ref[128:136, 0:128]
        for k, part in enumerate((low_ref[0:128, :], high_ref[...])):
            halo[k] = mm(three(split(part), 1), w_out_t[...])
        for s in range(4):
            cut = column(s)
            hi, lo = split(gathered[s].T)
            for place in (0, 256):
                place = place + (s >> 1) * 512 + (s & 1) * 128
                weights[place : place + 128, 0:128] = hi
                weights[place : place + 128, 128:256] = lo

    block_ref[...] = got_ref[:, 0:128]
    skip_ref[...] = got_ref[:, 128:256]
    enc_ref[...] = got_ref[:, 256:768]

    base = lax.axis_index("tm") * (2 * own_rows) + half * own_rows
    new, old = j & 1, 1 - (j & 1)

    def chooser(begin, alone, edge, ahead):
        row_b, row_a = item_rows(ahead, items)

        def pick(ref, i):
            value_b = ref[i, pl.ds(row_b, 1), :]
            return value_b, value_b if alone else ref[i, pl.ds(row_a, 1), :]

        def choose(pair, i):
            if alone:
                return pair[0]
            return jnp.where(iota((ROWS, LANES), 0) + (begin - edge) + i >= 0, pair[1], pair[0])

        return pick, choose

    begin = base + j * T - STEP
    edge, ahead = boundary(ends, begin)
    alone = edge >= begin + T

    def filter_rows(alone):
        pick, choose = chooser(begin, alone, edge, ahead)
        means, inverses = pick(table_mid_ref, 0), pick(table_mid_ref, 1)
        firsts, seconds = pick(table, 0), pick(table, 1)
        shifts = tuple(-a * b for a, b in zip(means, inverses))
        firsts = tuple(a * b for a, b in zip(firsts, inverses))
        seconds = tuple(a * b for a, b in zip(seconds, inverses))
        for c in range(4):
            slope, gain = vec(8, c), vec(9, c)
            keep = 1.0 - slope
            halves = [None, None]
            for i in range(0, T, ROWS):
                if i < STEP:
                    r = jnp.where(j == 0, halo[0, i : i + ROWS, column(c)], r_a_ref[i : i + ROWS, column(c)])
                else:
                    cut = slice(i - STEP, i - STEP + ROWS)
                    r = jnp.where(j == last, halo[1, cut, column(c)], r_b_ref[cut, column(c)])
                depth = depth_ref[i : i + ROWS, column(c)]
                s = sigmoid(depth)
                u = depth * (1.0 - s)
                part = keep * s
                mild = slope + part
                inv = choose(inverses, i)
                normed = depth * mild * inv + choose(shifts, i)
                grad_act = r * (gain * inv) - choose(firsts, i) - normed * choose(seconds, i)
                if c < 2:
                    halves[i // STEP] = plus(halves[i // STEP], fold(grad_act * u))
                ring[new, i : i + ROWS, column(c)] = grad_act * (mild + part * u)
            if c < 2:
                in_low = jnp.where(j > 0, 1.0, 0.0)
                in_high = jnp.where(j < last, 1.0, 0.0)
                acc_vec[8:9, column(c)] += in_low * colsum(halves[0]) + in_high * colsum(halves[1])

    pl.when(alone)(lambda: filter_rows(True))
    pl.when(jnp.logical_not(alone))(lambda: filter_rows(False))

    start = base + (j - 1) * T
    edge2, ahead2 = boundary(ends, start)
    plain = edge2 >= start + T + STEP

    def norm_rows(plain):
        pick, choose = chooser(start, plain, edge2, ahead2)
        means, inverses = pick(table_in_ref, 0), pick(table_in_ref, 1)
        firsts, seconds = pick(table, 2), pick(table, 3)
        shifts = tuple(-a * b for a, b in zip(means, inverses))
        firsts = tuple(a * b for a, b in zip(firsts, inverses))
        seconds = tuple(a * b for a, b in zip(seconds, inverses))
        rows = iota((ROWS, LANES), 0) + (start - edge2)
        his, los = [[], [], [], []], [[], [], [], []]
        for c in range(4):
            slope, gain, bias = vec(1, c), vec(2, c), vec(3, c)
            keep = 1.0 - slope
            sums = [None] * 8
            for i in range(0, T, ROWS):
                cut = slice(i, i + ROWS)
                grad_low, grad_high = ring[old, cut, column(c)], ring[new, cut, column(c)]
                if i < STEP:
                    grad_mid = ring[old, i + STEP : i + STEP + ROWS, column(c)]
                else:
                    grad_mid = ring[new, i - STEP : i - STEP + ROWS, column(c)]
                if not plain:
                    offset = rows + i
                    grad_low = jnp.where((offset >= 0) & (offset < STEP), 0.0, grad_low)
                    grad_high = jnp.where((offset < 0) & (offset >= -STEP), 0.0, grad_high)
                grad_norm = vec(5, c) * grad_mid + vec(4, c) * grad_high + vec(6, c) * grad_low
                hidden = hidden_ref[cut, column(c)]
                s = sigmoid(hidden)
                u = hidden * (1.0 - s)
                part = keep * s
                mild = slope + part
                inv = choose(inverses, i)
                normed = hidden * mild * inv + choose(shifts, i)
                grad_act = grad_norm * (gain * inv) - choose(firsts, i) - normed * choose(seconds, i)
                grad_hidden = grad_act * (mild + part * u)
                if c < 2:
                    norm = normed * gain + bias
                    values = (
                        grad_hidden, grad_act * u, grad_norm * normed, grad_norm, norm * grad_high, norm * grad_mid,
                        norm * grad_low, grad_mid,
                    )
                    sums = [plus(s, fold(value)) for s, value in zip(sums, values)]
                hi, lo = split(grad_hidden)
                his[c].append(hi)
                los[c].append(lo)
            if c < 2:
                acc_vec[0:8, column(c)] += cat([colsum(s) for s in sums], 0)
        hi, lo = [cat(p, 0) for p in his], [cat(p, 0) for p in los]
        own = mm(cat(hi[0:2] + lo[0:2], 1), weights[0:512, :])
        back = own + mm(cat(hi[2:4] + lo[2:4], 1), weights[512:1024, :])
        grad_mix = cot_ref[...] + (back[:, 0:128] + back[:, 128:256])
        grad_mix_ref[...] = grad_mix
        send_ref[...] = grad_mix
        mixed = cat(split(mix_ref[...]), 1)
        acc_w[...] += mm_tn(cat([cat(hi[0:2], 1), cat(lo[0:2], 1)], 1), mixed)

    pl.when((j > 0) & plain)(lambda: norm_rows(True))
    pl.when((j > 0) & jnp.logical_not(plain))(lambda: norm_rows(False))

    @pl.when(j == last)
    def _():
        for ref, h in ((keep_ref, half), (give_ref, 1 - half)):
            own = pl.ds(pl.multiple_of(h * 128, 128), 128)
            rest = pl.ds(pl.multiple_of(256 + h * 128, 128), 128)
            ref[0:128, :] = (acc_w[own, 0:128] + (acc_w[own, 128:256] + acc_w[rest, 0:128])).T
            ref[128:144, :] = acc_vec[:, own]


def merge_kernel(len_ref, got_ref, mix_in, mine_ref, other_ref, edge_ref, edge_other_ref, mix_ref, wave_ref):
    me = lax.axis_index("src")
    half = me & 1
    mix_ref[...] = got_ref[...]
    width = mine_ref.shape[1]
    frames = width // STRIDE
    base = lax.axis_index("tm") * (2 * frames)
    ends = item_ends(len_ref)
    lane = iota((2, LANES), 1)
    for part, edge, h in ((mine_ref, edge_ref, half), (other_ref, edge_other_ref, 1 - half)):
        place = base + h * frames
        new = place == 0
        for end in ends:
            new = new | (end == place)
        place = pl.multiple_of(h * width, width)
        wave_ref[:, pl.ds(place, width)] = part[...]
        first = part[:, 0:128] + jnp.where((lane < STRIDE) & jnp.logical_not(new), edge[0:2, :], 0.0)
        wave_ref[:, pl.ds(place, LANES)] = first


def total_of(refs):
    values = [ref[...] for ref in refs]
    while len(values) > 1:
        values = [a + b for a, b in zip(values[0::2], values[1::2])]
    return values[0]


def last_kernel(count, early_ref, early_other_ref, *refs):
    lates = refs[:count]
    (
        w_in, b_in, slope_in, gain_in, beta_in, w_depth, b_depth, slope_mid,
    gain_mid, beta_mid, w_out, b_out, slope_skip, w_mask, b_mask, basis,
    ) = refs[count:]
    late = total_of(lates)
    w_in[...] = late[0:128]
    for ref, row in (
        (b_in, 128), (slope_in, 129), (gain_in, 130), (beta_in, 131), (b_depth, 135), (slope_mid, 136),
    ):
        ref[...] = late[row : row + 1]
    w_depth[...] = late[132:135]
    early = early_ref[...] + early_other_ref[...]
    w_out[:, 0:128] = early[0:128]
    w_out[:, 128:256] = early[128:256]
    w_mask[:, 0:128] = early[256:384]
    w_mask[:, 128:256] = early[384:512]
    b_mask[:, 0:128] = early[512:513]
    b_mask[:, 128:256] = early[513:514]
    gain_mid[...] = early[514:515]
    beta_mid[...] = early[515:516]
    slope_skip[...] = early[516:517]
    b_out[:, 0:128] = early[517:518]
    b_out[:, 128:256] = early[518:519]
    for k in range(4):
        basis[:, column(k)] = early[520 + 16 * k : 536 + 16 * k]


def local(
    mix_in, skip_in, encoded, lengths, w_in, b_in, slope_in, gain_in, beta_in, w_depth, b_depth, slope_mid, gain_mid,
    beta_mid, w_out, b_out, slope_skip, w_mask, b_mask, basis, cot_out, cot_wave,
):
    n_tm, n_src = lax.axis_size("tm"), lax.axis_size("src")
    devices = n_tm * n_src
    frames = mix_in.shape[0]
    own_rows = frames // 2
    items = lengths.shape[0]
    padded = -(-items // 8) * 8
    tiles = own_rows // T
    tiles_m = own_rows // TM
    up = [(i, i + 1) for i in range(n_tm - 1)]
    down = [(j, i) for i, j in up]
    swap = [(i, i ^ 1) for i in range(n_src)]
    cross = [(i, i ^ 2) for i in range(n_src)]

    def half():
        return lax.axis_index("src") & 1

    def struct(*shape):
        return jax.ShapeDtypeStruct(shape, F32)

    def whole(*shape):
        zeros = (0,) * len(shape)
        return pl.BlockSpec(shape, lambda i, n: zeros)

    anywhere = pl.BlockSpec(memory_space=pl.ANY)

    def vmem(*shape):
        return pltpu.VMEM(shape, F32)

    def vmem16(*shape):
        return pltpu.VMEM(shape, BF16)

    def call(kernel, name, grid, in_specs, out_specs, out_shape, scratch, us, **kw):
        return pl.pallas_call(
            kernel,
            grid_spec=pltpu.PrefetchScalarGridSpec(
                num_scalar_prefetch=1, grid=(grid,), in_specs=in_specs, out_specs=out_specs, scratch_shapes=scratch
            ),
            out_shape=out_shape,
            compiler_params=pltpu.CompilerParams(
                vmem_limit_bytes=VMEM, dimension_semantics=("arbitrary",)
            ),
            cost_estimate=pl.CostEstimate(flops=0, bytes_accessed=us * 3_600_000, transcendentals=0),
            name=name,
            **kw,
        )

    msg_shape = (devices, 8, LANES)
    message = struct(*msg_shape)
    stat_shape = (devices, 1, LANES) if items <= GROUP else msg_shape
    statistic = struct(*stat_shape)

    def exchange(msg):
        return lax.all_to_all(msg, ("tm", "src"), 0, 0)

    def line(vector):
        return vector.reshape(1, -1)

    def fixed(*shape):
        return pl.BlockSpec(shape, lambda i: (0,) * len(shape))

    n1 = frames // T1
    vectors = (
        line(b_in), line(slope_in), line(gain_in), line(beta_in), w_depth, line(b_depth), line(slope_mid),
        line(gain_mid), line(beta_mid), line(b_mask),
    )
    pack, wide, low, high = pl.pallas_call(
        prep_kernel,
        grid=(1,),
        in_specs=[
            fixed(T, 128), pl.BlockSpec((T, 128), lambda i: (frames // T - 1, 0)), fixed(2, LANES), fixed(128, 128),
            fixed(128, 256), fixed(128, 256), *[fixed(*v.shape) for v in vectors],
        ],
        out_specs=[fixed(PACK_IN, 128), fixed(512, 128), fixed(T + 8, 128), fixed(T, 128)],
        out_shape=[struct(PACK_IN, 128), struct(512, 128), struct(T + 8, 128), struct(T, 128)],
        compiler_params=pltpu.CompilerParams(vmem_limit_bytes=VMEM),
        name="prep",
    )(mix_in, mix_in, cot_wave, w_in, w_out, w_mask, *vectors)
    pack_x = lax.ppermute(pack, "src", cross)
    pack_core = lax.ppermute(pack, "src", swap)
    mix_prev = lax.ppermute(high, "tm", up)
    mix_next = lax.ppermute(low, "tm", down)
    msg1 = call(
        first_kernel, "first", 2,
        [pl.BlockSpec((frames // 2, 128), lambda i, n: (i, 0)), whole(128, 128), whole(1, 128), whole(1, 128)],
        whole(*msg_shape), message,
        [vmem(1, 2 * n1, 128), vmem(1, 2 * n1, 128), vmem(2 * n1, 128), vmem(2 * n1, 128)], 4,
    )(lengths, mix_in, w_in, line(b_in), line(slope_in))
    msg1, pack_x, pack_core, mix_prev, mix_next = lax.optimization_barrier(
        (msg1, pack_x, pack_core, mix_prev, mix_next)
    )
    pack_far = lax.ppermute(pack_x, "src", swap)
    packs = (pack, pack_core, pack_x, pack_far)
    msg1 = exchange(msg1)
    wide_x = lax.ppermute(wide, "src", cross)
    wide_core = lax.ppermute(wide, "src", swap)
    wide_far = lax.ppermute(wide_x, "src", swap)
    wides = (wide, wide_core, wide_x, wide_far)

    entries = -(-2 * (tiles + 1) // 8) * 8
    hidden, depth, msg2, vec, table_in = call(
        depth_kernel, "depth", tiles + 2,
        [
            whole(*msg_shape),
            whole(frames, 128), whole(T, 128), whole(T + 8, 128), *[whole(PACK_IN, 128)] * 4,
        ],
        [
            pl.BlockSpec((T, HIDDEN), lambda i, n: (i, 0)),
            pl.BlockSpec((T, HIDDEN), lambda i, n: (jnp.maximum(i - 1, 0), 0)),
            whole(*stat_shape), whole(NVEC, HIDDEN), whole(2, padded, LANES),
        ],
        [
            struct(own_rows + 2 * T, HIDDEN), struct(own_rows + T, HIDDEN), statistic, struct(NVEC, HIDDEN),
            struct(2, padded, LANES),
        ],
        [
            vmem(4, PACK_IN, 128), vmem16(512, HIDDEN), vmem(2, T, HIDDEN),
            vmem(4, entries, 128), vmem(4, entries, 128), vmem(entries, 128), vmem(entries, 128),
        ], 8,
    )(lengths, msg1, mix_in, mix_prev, mix_next, *packs)
    msg2 = exchange(msg2)

    def half_rows(width):
        return pl.BlockSpec((TM, width), lambda i, n: (half() * tiles_m + i, 0))

    def rows_m(width):
        return pl.BlockSpec((TM, width), lambda i, n: (i, 0))

    def depth_piece(k):
        return pl.BlockSpec((STEP, HIDDEN), lambda i, n: (TM // STEP * i + 1 + k, 0))

    packed = call(
        cotangent_kernel, "cotangent", tiles_m,
        [
            pl.BlockSpec((2, TM * STRIDE), lambda i, n: (0, half() * tiles_m + i)),
            pl.BlockSpec(
                (2, LANES),
                lambda i, n: (0, jnp.minimum((half() * tiles_m + i + 1) * (TM // 16), (2 * tiles_m) * (TM // 16) - 1)),
            ),
            whole(T + 8, 128), anywhere,
        ],
        rows_m(128), jax.ShapeDtypeStruct((own_rows, 128), BF16), [], 6,
    )(lengths, cot_wave, cot_wave, mix_next, vec)
    pieces = TM // STEP
    (block_out, grad_skip, grad_enc, send, wave_half, r, r_up, r_down, keep, give, msg3, table_mid, w_out_t) = call(
        mask_kernel, "mask", tiles_m,
        [
            whole(*stat_shape), *[depth_piece(k) for k in range(pieces)],
            half_rows(128), half_rows(128), half_rows(HIDDEN), half_rows(128),
            rows_m(128), whole(L, HIDDEN), whole(NVEC, HIDDEN), whole(1, 256), whole(1, 128),
            *[whole(512, 128)] * 4,
        ],
        [
            half_rows(128), half_rows(128), half_rows(HIDDEN), rows_m(768),
            pl.BlockSpec((2, TM * STRIDE), lambda i, n: (0, i)),
            rows_m(HIDDEN), whole(136, 256), whole(128, 256), whole(EARLY, 128), whole(EARLY, 128),
            whole(*msg_shape), whole(2, padded, LANES), whole(768, HIDDEN),
        ],
        [
            struct(frames, 128), struct(frames, 128), struct(frames, HIDDEN), struct(own_rows, 768),
            struct(2, own_rows * STRIDE), struct(own_rows, HIDDEN), struct(136, 256), struct(128, 256),
            struct(EARLY, 128), struct(EARLY, 128), message, struct(2, padded, LANES),
            jax.ShapeDtypeStruct((768, HIDDEN), BF16),
        ],
        [
            vmem(4, 512, 128), vmem16(1536, 256),
            vmem16(512, 1024), vmem16(2, 2, 512, 256), vmem16(2, 768, 256), vmem16(128, 1024), vmem(TM, HIDDEN), vmem(TM, HIDDEN), vmem(8, 128), vmem(256, 256), vmem(128, HIDDEN),
            vmem(2, 128, HIDDEN), vmem(8, HIDDEN), vmem(8, 128),
            vmem(8, 2 * tiles, 128), vmem(2 * tiles, 128),
        ], 28,
    )(
        lengths, msg2, *[depth] * pieces, mix_in, skip_in, encoded, cot_out, packed, basis.T, vec,
        line(b_out), line(slope_skip), *wides,
    )

    both = ("tm", "src")
    later, earlier = [], []
    for i in range(n_tm):
        for s in range(n_src):
            here = i * n_src + s
            there = here + 1 if s % 2 == 0 else (i + 1) * n_src + s - 1
            if s % 2 == 0 or i + 1 < n_tm:
                later.append((here, there))
                earlier.append((there, here))
    hops = [[(i, i ^ (1 << bit)) for i in range(n_tm)] for bit in range(n_tm.bit_length() - 1)]
    early = keep + lax.ppermute(give, "src", swap)
    got_low = lax.ppermute(r_up, both, later)
    got_high = lax.ppermute(r_down, both, earlier)
    msg3 = exchange(msg3)
    early, send = lax.optimization_barrier((early, send))
    early_other = lax.ppermute(early, "tm", hops[0])
    got = lax.ppermute(send, "src", swap)
    msg3, got_low, got_high, early, early_other, got, wave_half = lax.optimization_barrier(
        (msg3, got_low, got_high, early, early_other, got, wave_half)
    )
    wave_other = lax.ppermute(wave_half, "src", swap)
    early = early + early_other
    early_other = lax.ppermute(early, "tm", hops[-1])

    def rows(width):
        return pl.BlockSpec((T, width), lambda i, n: (i, 0))

    def own_tile(width):
        return pl.BlockSpec((T, width), lambda i, n: (half() * tiles + jnp.maximum(i - 1, 0), 0))

    def other_rows(width):
        return pl.BlockSpec((T, width), lambda i, n: ((1 - half()) * tiles + jnp.minimum(i, tiles - 1), 0))

    grad_mix, mix_send, keep, give, edge, block_out, grad_skip, grad_enc = call(
        back_kernel, "back", tiles + 1,
        [
            whole(*msg_shape), rows(HIDDEN),
            pl.BlockSpec((STEP, HIDDEN), lambda i, n: (jnp.maximum(2 * i - 1, 0), 0)),
            pl.BlockSpec((STEP, HIDDEN), lambda i, n: (jnp.minimum(2 * i, 2 * tiles - 1), 0)),
            whole(136, 256), whole(128, 256),
            pl.BlockSpec((T, HIDDEN), lambda i, n: (jnp.maximum(i, 1), 0)), own_tile(128), own_tile(128),
            whole(NVEC, HIDDEN), whole(2, padded, LANES), whole(2, padded, LANES), whole(768, HIDDEN),
            *[whole(128, 128)] * 4,
            pl.BlockSpec((T, 768), lambda i, n: (jnp.minimum(i, tiles - 1), 0)), anywhere, anywhere, anywhere,
        ],
        [
            own_tile(128), pl.BlockSpec((T, 128), lambda i, n: (jnp.maximum(i - 1, 0), 0)),
            whole(144, 128), whole(144, 128), whole(8, 128), other_rows(128), other_rows(128), other_rows(HIDDEN),
        ],
        [
            struct(frames, 128), struct(own_rows, 128), struct(144, 128), struct(144, 128), struct(8, 128),
            struct(frames, 128), struct(frames, 128), struct(frames, HIDDEN),
        ],
        [
            vmem(4, 128, 128), vmem(4, padded, LANES), vmem16(1024, 256),
            vmem(2, T, HIDDEN), vmem(2, 128, HIDDEN), vmem(512, 256), vmem(16, HIDDEN),
        ], 13,
        input_output_aliases={19: 5, 20: 6, 21: 7},
    )(
        lengths, msg3, depth, r, r, got_low, got_high, hidden, mix_in, cot_out, vec, table_in, table_mid, w_out_t, *packs, got,
        block_out, grad_skip, grad_enc,
    )

    grad_mix, mix_send, keep, give, edge, early_other, wave_other = lax.optimization_barrier(
        (grad_mix, mix_send, keep, give, edge, early_other, wave_other)
    )
    late_give = lax.ppermute(give, "src", swap)
    early = early + early_other
    for hop in hops[1:-1]:
        early_other = lax.ppermute(early, "tm", hop)
        if hop is not hops[-2]:
            early = early + early_other
    late_give, early = lax.optimization_barrier((late_give, early))
    late = keep + late_give
    late, edge, mix_send = lax.optimization_barrier((late, edge, mix_send))
    late_other = lax.ppermute(late, "tm", hops[0])
    mix_got = lax.ppermute(mix_send, "src", swap)
    edge_other = lax.ppermute(edge, "src", swap)
    late, late_other, early, mix_got, edge_other = lax.optimization_barrier(
        (late, late_other, early, mix_got, edge_other)
    )
    late = late + late_other
    lates = [late]
    for k in range(1, n_tm // 2):
        lates.append(lax.ppermute(late, "tm", [(i, i ^ (2 * k)) for i in range(n_tm)]))
    wave_width = own_rows * STRIDE
    late, mix_got, edge_other = lax.optimization_barrier((late, mix_got, edge_other))
    grad_mix, wave = call(
        merge_kernel, "merge", 1,
        [
            whole(own_rows, 128), anywhere, whole(2, wave_width), whole(2, wave_width), whole(8, 128), whole(8, 128),
        ],
        [pl.BlockSpec((own_rows, 128), lambda i, n: (1 - half(), 0)), whole(2, 2 * wave_width)],
        [struct(frames, 128), struct(2, 2 * wave_width)], [], 3,
        input_output_aliases={2: 0},
    )(lengths, mix_got, grad_mix, wave_half, wave_other, edge, edge_other)
    *lates, grad_mix, wave = lax.optimization_barrier((*lates, grad_mix, wave))

    parts = (early, early_other, *lates)
    shapes = (
        (128, 128), (1, 128), (1, 128), (1, 128), (1, 128), (3, 128), (1, 128), (1, 128), (1, 128), (1, 128), (128, 256),
        (1, 256), (1, 128), (128, 256), (1, 256), (L, HIDDEN),
    )
    outs = pl.pallas_call(
        functools.partial(last_kernel, len(lates)),
        grid=(1,),
        in_specs=[fixed(*part.shape) for part in parts],
        out_specs=[fixed(*shape) for shape in shapes],
        out_shape=[struct(*shape) for shape in shapes],
        compiler_params=pltpu.CompilerParams(vmem_limit_bytes=VMEM),
        name="last",
    )(*parts)
    outs = [o.reshape(-1) if o.shape[0] == 1 else o for o in outs[:-1]] + [outs[-1].T]
    return (block_out, wave, grad_mix, grad_skip, grad_enc, *outs)


def solution(mesh):
    frames, channels = P("tm", None), P("src")
    in_specs = (
        frames, frames, frames, P(), P(None, "src"), channels, channels, channels, channels, P(None, "src"), channels,
        channels, channels, channels, P("src", None), P(), P(), P(None, "src"), channels, P(), frames, P(None, "tm"),
    )
    out_specs = (
        frames, P(None, "tm"), frames, frames, frames, P(None, "src"), channels, channels, channels, channels,
        P(None, "src"), channels, channels, channels, channels, P("src", None), P(), P(), P(None, "src"), channels,
        P(),
    )
    return jax.shard_map(local, mesh=mesh, in_specs=in_specs, out_specs=out_specs, check_vma=False)
```

```python
import functools

import jax
import jax.numpy as jnp
from jax import lax
from jax.experimental import pallas as pl
from jax.experimental.pallas import tpu as pltpu
from jax.sharding import PartitionSpec as P

L = 16
STRIDE = L // 2
HIDDEN = 512
STEP = 128
EPS = 1e-05
T = 256
T1 = 512
TM = 512
ROWS = 16
LANES = 128
GROUP = 16
F32 = jnp.float32
BF16 = jnp.bfloat16
NVEC = 16
PACK_IN = 128 + NVEC
PACK = PACK_IN + 512
EARLY = 584
VMEM = 64 * 2**20 - 2**15
LOG2E = 1.4426950408889634


def split(x):
    hi = x.astype(BF16)
    return hi, (x - hi.astype(F32)).astype(BF16)


def mm(a, b):
    return lax.dot_general(a, b, (((1,), (0,)), ((), ())), preferred_element_type=F32)


def mm_tn(a, b):
    return lax.dot_general(a, b, (((0,), (0,)), ((), ())), preferred_element_type=F32)


def mm_nt(a, b):
    return lax.dot_general(a, b, (((1,), (1,)), ((), ())), preferred_element_type=F32)


def cat(parts, axis):
    return jnp.concatenate(parts, axis=axis)


def three(x, axis):
    hi, lo = x
    return cat([hi, lo, hi], axis)


def two_of(x, axis):
    hi, lo = x
    return cat([hi, hi, lo], axis)


def iota(shape, axis):
    return lax.broadcasted_iota(jnp.int32, shape, axis)


def sigmoid(x):
    return 1.0 / (1.0 + jnp.exp2(x * -LOG2E))


def colsum(x):
    return jnp.sum(x, axis=0, keepdims=True)


def fold(x):
    total = x[0:8]
    for i in range(8, x.shape[0], 8):
        total = total + x[i : i + 8]
    return total


def plus(a, b):
    return b if a is None else a + b


def column(c):
    return slice(c * LANES, (c + 1) * LANES)


def ones_block(rows):
    return jnp.where(iota((rows, LANES), 1) < 3, 1.0, 0.0).astype(BF16)


def bias_rows(bias, rows):
    hi, lo = split(bias)
    low = (bias - hi.astype(F32) - lo.astype(F32)).astype(BF16)
    place = iota((rows, bias.shape[1]), 0)
    zero = jnp.zeros((rows, bias.shape[1]), F32)
    out = jnp.where(place == 0, hi.astype(F32), zero)
    out = jnp.where(place == 1, lo.astype(F32), out)
    return jnp.where(place == 2, low.astype(F32), out).astype(BF16)


def item_ends(len_ref):
    ends, total = [], jnp.int32(0)
    for k in range(len_ref.shape[0]):
        total = total + len_ref[k]
        ends.append(total)
    return ends


def boundary(ends, start):
    ahead = jnp.where(start - STEP >= 0, 0, -1)
    for end in ends:
        ahead = ahead + (end <= start - STEP).astype(jnp.int32)
    edge = jnp.int32(0)
    for k, end in enumerate(ends):
        edge = jnp.where(ahead == k, end, edge)
    return edge, ahead


def item_rows(ahead, items):
    return jnp.maximum(ahead, 0), jnp.minimum(ahead + 1, items - 1)


def lane_items(ahead, items):
    lane = iota((1, LANES), 1)
    return (lane == ahead).astype(F32), (lane == ahead + 1).astype(F32)


def put_statistics(msg_ref, sums, squares, counts, onehot):
    groups = sums.shape[0]
    count = counts[:, :1]
    safe = jnp.maximum(count, 1.0)
    total = jnp.sum(jnp.sum(sums, axis=0), axis=1, keepdims=True)
    number = count * (groups * LANES)
    mean = total / jnp.maximum(number, 1.0)
    spread = 0.0
    for g in range(groups):
        away = sums[g] / safe - mean
        spread = spread + squares[g] + count * away * away
    spread = jnp.sum(spread, axis=1, keepdims=True)
    item_sum = colsum(onehot * total)
    item_number = colsum(onehot * number)
    item_mean = item_sum / jnp.maximum(item_number, 1.0)
    away = mean - item_mean
    item_spread = colsum(onehot * (spread + number * away * away))
    lines = (item_sum, item_spread, item_number, item_mean)
    if msg_ref.shape[1] == 1:
        msg = lines[0]
        for k, line in enumerate(lines[1:]):
            msg = msg + pltpu.roll(line, GROUP * (k + 1), 1)
    else:
        msg = cat([*lines, jnp.zeros((4, LANES), F32)], 0)
    for i in range(msg_ref.shape[0]):
        msg_ref[i] = msg


def to_rows(row, items_padded):
    wide = jnp.broadcast_to(row, (items_padded, LANES))
    own = iota((items_padded, LANES), 0) == iota((items_padded, LANES), 1)
    column = jnp.sum(jnp.where(own, wide, 0.0), axis=1, keepdims=True)
    return jnp.broadcast_to(column, (items_padded, LANES))


def merge_statistics(msg_ref, table_ref):
    msg = msg_ref[...]
    if msg_ref.shape[1] == 1:
        totals = jnp.sum(msg, axis=0)
        first = iota((1, LANES), 1) < GROUP
        item_sum = jnp.where(first, totals, 0.0)
        number = jnp.where(first, pltpu.roll(totals, LANES - 2 * GROUP, 1), 0.0)
        mean = item_sum / jnp.maximum(number, 1.0)
        away = msg - pltpu.roll(mean, 3 * GROUP, 1)[None]
        around = jnp.sum(pltpu.roll(msg, GROUP, 2) * away * away, axis=0)
        squares = pltpu.roll(totals, LANES - GROUP, 1) + pltpu.roll(around, LANES - 3 * GROUP, 1)
        squares = jnp.where(first, squares, 0.0)
    else:
        item_sum = jnp.sum(msg[:, 0:1, :], axis=0)
        number = jnp.sum(msg[:, 2:3, :], axis=0)
        mean = item_sum / jnp.maximum(number, 1.0)
        away = msg[:, 3:4, :] - mean[None]
        squares = jnp.sum(msg[:, 1:2, :] + msg[:, 2:3, :] * away * away, axis=0)
    inverse = lax.rsqrt(squares / jnp.maximum(number, 1.0) + EPS)
    padded = table_ref.shape[1]
    table_ref[0] = to_rows(mean, padded)
    table_ref[1] = to_rows(inverse, padded)


def put_entry(refs, groups, entry, sums, squares, number, hot):
    sums_ref, squares_ref, counts_ref, onehot_ref = refs
    row = pl.ds(entry, 1)
    for g in range(groups):
        sums_ref[g, row, :] = sums[g]
        squares_ref[g, row, :] = squares[g]
    counts_ref[row, :] = jnp.full((1, LANES), number, F32)
    onehot_ref[row, :] = hot


def general_entries(refs, acts, after, before, n_after, n_before, entry, ahead):
    hot_b, hot_a = lane_items(ahead, 0)
    for part, keep, number, hot in ((0, before, n_before, hot_b), (1, after, n_after, hot_a)):
        sums, squares = [], []
        for act in acts:
            total = colsum(jnp.where(keep, act, 0.0))
            away = act - total / jnp.maximum(number, 1.0)
            sums.append(total)
            squares.append(colsum(jnp.where(keep, away * away, 0.0)))
        put_entry(refs, len(acts), 2 * entry + part, sums, squares, number, hot)


def prep_kernel(
    top_ref, bottom_ref, cot_ref, w_in_ref, w_out_ref, w_mask_ref, b_in, slope_in, gain_in, beta_in, w_depth, b_depth,
    slope_mid, gain_mid, beta_mid, b_mask, pack_ref, wide_ref, low_ref, high_ref,
):
    pack_ref[0:128, :] = w_in_ref[...]
    vectors = (b_in, slope_in, gain_in, beta_in, w_depth, b_depth, slope_mid, gain_mid, beta_mid)
    bias = b_mask[...]
    pack_ref[128:144, :] = cat(
        [ref[...] for ref in vectors] + [bias[:, 0:128], bias[:, 128:256], jnp.zeros((3, LANES), F32)], 0
    )
    for k in range(2):
        wide_ref[128 * k : 128 * (k + 1), :] = w_out_ref[:, column(k)]
        wide_ref[128 * (k + 2) : 128 * (k + 3), :] = w_mask_ref[:, column(k)]
    low_ref[0:T, :] = top_ref[...]
    low_ref[T : T + 8, :] = cat([cot_ref[...], jnp.zeros((6, LANES), F32)], 0)
    high_ref[...] = bottom_ref[...]


def first_kernel(len_ref, mix_ref, w_in_ref, b_in, slope_in, msg_ref, sums, squares, counts, onehot):
    step = pl.program_id(0)
    last = pl.num_programs(0) - 1
    tiles = mix_ref.shape[0] // T1
    ends = item_ends(len_ref)
    weights = two_of(split(w_in_ref[...]), 0)
    slope = slope_in[...]
    keep = 1.0 - slope
    bias = b_in[...]
    refs = (sums, squares, counts, onehot)
    for t in range(tiles):
        j = step * tiles + t
        start = lax.axis_index("tm") * ((last + 1) * tiles * T1) + j * T1
        edge, ahead = boundary(ends, start)
        hidden = mm(three(split(mix_ref[t * T1 : (t + 1) * T1, :]), 1), weights)
        pieces, total = [], None
        for i in range(0, T1, ROWS):
            x = hidden[i : i + ROWS] + bias
            act = x * (slope + keep * sigmoid(x))
            pieces.append(act)
            total = plus(total, fold(act))
        total = colsum(total)
        mean = total / T1
        square = None
        for act in pieces:
            away = act - mean
            square = plus(square, fold(away * away))
        put_entry(refs, 1, 2 * j, [total], [colsum(square)], jnp.float32(T1), lane_items(ahead, 0)[0])
        nothing = jnp.zeros((1, LANES), F32)
        put_entry(refs, 1, 2 * j + 1, [nothing], [nothing], jnp.float32(0.0), nothing)

        @pl.when(edge < start + T1)
        def _():
            offset = iota((T1, LANES), 0) + (start - edge)
            n_before = jnp.clip(edge - start, 0, T1).astype(F32)
            act = cat(pieces, 0)
            general_entries(refs, [act], offset >= 0, offset < 0, T1 - n_before, n_before, j, ahead)

    @pl.when(step == last)
    def _():
        put_statistics(msg_ref, sums[...], squares[...], counts[...], onehot[...])


def depth_kernel(
    len_ref, msg_in_ref, mix_ref, prev_ref, next_ref, own_ref, core_ref, x_ref, far_ref,
    hidden_ref, depth_ref, msg_ref, vec_ref, table_ref,
    gathered, weights, ring, sums, squares, counts, onehot,
):
    m = pl.program_id(0)
    last = pl.num_programs(0) - 1
    items = len_ref.shape[0]
    me = lax.axis_index("src")
    half = me & 1
    own_rows = (last - 1) * T

    @pl.when(m == 0)
    def _():
        for k, ref in enumerate((own_ref, core_ref, x_ref, far_ref)):
            gathered[half ^ k] = ref[...]
        merge_statistics(msg_in_ref, table_ref)
        for ref in (sums, squares, counts, onehot):
            ref[...] = jnp.zeros_like(ref)
        for s in range(4):
            cut = column(s)
            weights[0:384, cut] = two_of(split(gathered[s, 0:128, :]), 0)
            weights[384:512, cut] = bias_rows(gathered[s, 128:129, :], 128)
            vec_ref[:, cut] = gathered[s, 128 : 128 + NVEC, :]

    def vec(row, c):
        return vec_ref[row : row + 1, column(c)]

    ends = item_ends(len_ref)
    base = lax.axis_index("tm") * (2 * own_rows) + half * own_rows
    start = base + (m - 1) * T
    edge, ahead = boundary(ends, start)
    alone = edge >= start + T
    block = half * (own_rows // T) + m - 1
    top = 2 * (own_rows // T)
    new, old = m & 1, 1 - (m & 1)

    def norm_rows(alone):
        place = pl.multiple_of(jnp.clip(block, 0, top - 1) * T, T)
        mix = mix_ref[pl.ds(place, T), :]
        mix = jnp.where(block < 0, prev_ref[...], jnp.where(block >= top, next_ref[0:T, :], mix))
        mixed = split(mix)
        hidden = mm(cat([mixed[0], mixed[1], mixed[0], ones_block(T)], 1), weights[...])
        hidden_ref[...] = hidden
        row_b, row_a = item_rows(ahead, items)
        rows = iota((ROWS, LANES), 0) + (start - edge)
        for c in range(4):
            slope = vec(1, c)
            keep = 1.0 - slope
            scale_b = table_ref[1, pl.ds(row_b, 1), :] * vec(2, c)
            shift_b = vec(3, c) - table_ref[0, pl.ds(row_b, 1), :] * scale_b
            scale_a = table_ref[1, pl.ds(row_a, 1), :] * vec(2, c)
            shift_a = vec(3, c) - table_ref[0, pl.ds(row_a, 1), :] * scale_a
            for i in range(0, T, ROWS):
                x = hidden[i : i + ROWS, column(c)]
                act = x * (slope + keep * sigmoid(x))
                if alone:
                    value = act * scale_b + shift_b
                else:
                    after = rows + i >= 0
                    value = act * jnp.where(after, scale_a, scale_b) + jnp.where(after, shift_a, shift_b)
                ring[new, i : i + ROWS, column(c)] = value

    pl.when(alone)(lambda: norm_rows(True))
    pl.when(jnp.logical_not(alone))(lambda: norm_rows(False))

    begin = start - STEP
    edge2, ahead2 = boundary(ends, begin)
    plain = edge2 >= begin + T + STEP
    refs = (sums, squares, counts, onehot)

    def filtered(c, i, lower_weight, upper_weight):
        lower = ring[old, i : i + ROWS, column(c)]
        upper = ring[new, i : i + ROWS, column(c)]
        if i < STEP:
            middle = ring[old, i + STEP : i + STEP + ROWS, column(c)]
        else:
            middle = ring[new, i - STEP : i - STEP + ROWS, column(c)]
        return lower_weight * lower + vec(5, c) * middle + upper_weight * upper + vec(7, c)

    @pl.when((m > 0) & plain)
    def _():
        in_low = jnp.where(m > 1, 1.0, 0.0)
        in_high = jnp.where(m < last, 1.0, 0.0)
        number = STEP * (in_low + in_high)
        all_sums, all_squares = [], []
        for c in range(4):
            slope = vec(8, c)
            keep = 1.0 - slope
            acts, halves = [], [None, None]
            for i in range(0, T, ROWS):
                depth = filtered(c, i, vec(4, c), vec(6, c))
                depth_ref[i : i + ROWS, column(c)] = depth
                act = depth * (slope + keep * sigmoid(depth))
                acts.append(act)
                halves[i // STEP] = plus(halves[i // STEP], fold(act))
            total = in_low * colsum(halves[0]) + in_high * colsum(halves[1])
            mean = total / number
            halves = [None, None]
            for i, act in enumerate(acts):
                away = act - mean
                halves[i * ROWS // STEP] = plus(halves[i * ROWS // STEP], fold(away * away))
            all_sums.append(total)
            all_squares.append(in_low * colsum(halves[0]) + in_high * colsum(halves[1]))
        put_entry(refs, 4, 2 * (m - 1), all_sums, all_squares, number, lane_items(ahead2, 0)[0])

    @pl.when((m > 0) & jnp.logical_not(plain))
    def _():
        low = jnp.where(m == 1, STEP, 0)
        high = jnp.where(m == last, STEP, T)
        rows = iota((ROWS, LANES), 0) + (begin - edge2)
        acts = []
        for c in range(4):
            slope = vec(8, c)
            pieces = []
            for i in range(0, T, ROWS):
                offset = rows + i
                lower_weight = jnp.where((offset >= 0) & (offset < STEP), 0.0, vec(4, c))
                upper_weight = jnp.where((offset < 0) & (offset >= -STEP), 0.0, vec(6, c))
                depth = filtered(c, i, lower_weight, upper_weight)
                depth_ref[i : i + ROWS, column(c)] = depth
                pieces.append(depth * (slope + (1.0 - slope) * sigmoid(depth)))
            acts.append(cat(pieces, 0))
        row = iota((T, LANES), 0)
        own = (row >= low) & (row < high)
        offset = row + (begin - edge2)
        n_before = jnp.clip(edge2 - begin, low, high) - low
        n_after = (high - low - n_before).astype(F32)
        general_entries(
            refs, acts, own & (offset >= 0), own & (offset < 0), n_after, n_before.astype(F32), m - 1, ahead2
        )

    @pl.when(m == last)
    def _():
        put_statistics(msg_ref, sums[...], squares[...], counts[...], onehot[...])


def cotangent_kernel(len_ref, wave_cot_ref, wave_next_ref, edge_next_ref, after_ref, packed_ref):
    j = pl.program_id(0)
    last = pl.num_programs(0) - 1
    me = lax.axis_index("src")
    half = me & 1
    side = me >> 1
    own_rows = (last + 1) * TM
    start = lax.axis_index("tm") * (2 * own_rows) + half * own_rows + j * TM
    edge, _ = boundary(item_ends(len_ref), start)
    offset = iota((TM, LANES), 0) + (start - edge)
    selects_hi, selects_lo = [], []
    for c in range(2):
        row = iota((2 * LANES, LANES), 0)
        col = iota((2 * LANES, LANES), 1) - 48 * c
        place = (row & 7) + ((row >> 7) << 3)
        selects_hi.append(((col == place) | (col == place + 16)).astype(F32).astype(BF16))
        selects_lo.append((col == place + 32).astype(F32).astype(BF16))

    lane_frame = iota((16, LANES), 1) >> 3
    frame = iota((16, LANES), 0)
    here = jnp.where(lane_frame == frame, 1.0, 0.0)
    coming = jnp.where(lane_frame == ((frame + 1) & 15), 1.0, 0.0)
    final_row = frame == 15
    packed = None
    waves = [wave_cot_ref[0:1, :], wave_cot_ref[1:2, :]]
    finals = [
        jnp.where((half == 1) & (j == last), edge_next_ref[T + c : T + c + 1, :], wave_next_ref[c : c + 1, :])
        for c in range(2)
    ]
    for c in range(2):
        wave = jnp.where(side == 0, waves[c], waves[1 - c])
        final = jnp.where(side == 0, finals[c], finals[1 - c])
        for part, select in zip(split(cat([wave, final], 1)), (selects_hi, selects_lo)):
            part = part.astype(F32)
            lines = [part[:, column(q)] for q in range(TM // 16 + 1)]
            pieces = []
            for q in range(TM // 16):
                following = jnp.where(final_row, lines[q + 1], lines[q]) * coming
                pieces.append(cat([lines[q] * here, following], 1).astype(BF16))
            packed = plus(packed, mm(cat(pieces, 0), select[c]))
    lane = iota((1, LANES), 1)
    lane = jnp.where(lane < 48, lane, lane - 48)
    packed_ref[...] = jnp.where((offset == -1) & ((lane & 15) >= 8), 0.0, packed).astype(BF16)


def mask_kernel(
    len_ref, msg_in_ref, *refs,
):
    depth_refs = refs[: TM // STEP]
    (
        mix_ref, skip_ref, enc_ref, cot_ref, packed_ref, basis_ref, vec_ref,
        b_out_ref, slope_skip_ref, own_ref, core_ref, x_ref, far_ref,
        block_ref, grad_skip_ref, grad_enc_ref, send_ref, wave_ref, r_ref, up_ref, down_ref, keep_ref, give_ref,
        msg_ref, table_ref, w_out_t,
        gathered, w_out, w_mask, w_mask_t, decode, basis_back, normed_ref,
        pull_ref, carry, acc_out, acc_mask, acc_basis, acc_vec,
        acc_small, entries, onehot,
    ) = refs[TM // STEP :]
    j = pl.program_id(0)
    last = pl.num_programs(0) - 1
    items = len_ref.shape[0]
    me = lax.axis_index("src")
    half = me & 1
    side = me >> 1
    own_rows = (last + 1) * TM

    def vec(row, c):
        return vec_ref[row : row + 1, column(c)]

    @pl.when(j == 0)
    def _():
        for k, ref in enumerate((own_ref, core_ref, x_ref, far_ref)):
            gathered[half ^ k] = ref[...]
        merge_statistics(msg_in_ref, table_ref)
        for ref in (acc_out, acc_mask, acc_basis, acc_vec, acc_small, carry, entries):
            ref[...] = jnp.zeros_like(ref)
        basis = split(basis_ref[...])
        b_hi, b_lo = basis
        col = iota((L, 2 * LANES), 1)
        row = iota((L, 2 * LANES), 0)
        spread = ((col & 7) == (row & 7)) & ((col >> 7) == (row >> 3))
        spread = spread.astype(F32).astype(BF16)
        wide = (mm_tn(b_hi, spread).astype(BF16), mm_tn(b_lo, spread).astype(BF16))
        for n in range(2):
            decode[n] = two_of([part[n * 256 : (n + 1) * 256] for part in wide], 0)
        for c in range(2):
            row = iota((LANES, L), 0) - 48 * c
            col = iota((LANES, L), 1)
            with_hi = ((row == col) | (row == col + 32)).astype(F32).astype(BF16)
            with_lo = (row == col + 16).astype(F32).astype(BF16)
            back = mm(with_hi, b_hi) + mm(with_lo, b_lo)
            basis_back[:, c * HIDDEN : (c + 1) * HIDDEN] = back.astype(BF16)
        for s in range(4):
            cut = column(s)
            for k in range(2):
                part = gathered[s, column(k), :]
                hi, lo = split(part)
                for place, value in ((0, hi), (256, hi), (512, lo)):
                    place = place + (s >> 1) * 768 + (s & 1) * 128
                    w_out[place : place + 128, column(k)] = value
                hi, lo = split(part.T)
                for place, value in ((0, hi), (256, hi), (512, lo)):
                    w_out_t[place + k * 128 : place + (k + 1) * 128, cut] = value
                part = gathered[s, column(2 + k), :]
                wide = slice(s * 256 + k * LANES, s * 256 + (k + 1) * LANES)
                w_mask[0:384, wide] = two_of(split(part * -LOG2E), 0)
                w_mask[384:512, wide] = bias_rows(vec_ref[11 + k : 12 + k, cut] * -LOG2E, 128)
                hi, lo = split(part.T)
                for place in (0, 256):
                    w_mask_t[s >> 1, s & 1, place + k * 128 : place + (k + 1) * 128, 0:128] = hi
                    w_mask_t[s >> 1, s & 1, place + k * 128 : place + (k + 1) * 128, 128:256] = lo

    ends = item_ends(len_ref)
    start = lax.axis_index("tm") * (2 * own_rows) + half * own_rows + j * TM
    edge, ahead = boundary(ends, start)
    row_b, row_a = item_rows(ahead, items)
    offset = iota((TM, LANES), 0) + (start - edge)

    lane_frame = iota((16, LANES), 1) >> 3
    here = jnp.where(lane_frame == iota((16, LANES), 0), 1.0, 0.0)
    packed = packed_ref[...]

    chunks = [[slice(c * HIDDEN + n * 256, c * HIDDEN + (n + 1) * 256) for c in range(2)] for n in range(2)]
    all_grads = [[None, None], [None, None]]
    after = offset >= 0
    inv_b, inv_a = table_ref[1, pl.ds(row_b, 1), :], table_ref[1, pl.ds(row_a, 1), :]
    shift_b, shift_a = -inv_b * table_ref[0, pl.ds(row_b, 1), :], -inv_a * table_ref[0, pl.ds(row_a, 1), :]
    inv = jnp.where(after, inv_a, inv_b)
    shift = jnp.where(after, shift_a, shift_b)
    norms = [[], []], [[], []]
    for c in range(4):
        slope = vec(8, c)
        keep = 1.0 - slope
        his, los = [], []
        for i in range(0, TM, ROWS):
            rows = slice(i, i + ROWS)
            depth = depth_refs[i // STEP][i % STEP : i % STEP + ROWS, column(c)]
            s = sigmoid(depth)
            part = keep * s
            mild = slope + part
            normed = depth * mild * inv[rows] + shift[rows]
            normed_ref[rows, column(c)] = normed
            pull_ref[rows, column(c)] = mild + part * (depth * (1.0 - s))
            hi, lo = split(normed * vec(9, c) + vec(10, c))
            his.append(hi)
            los.append(lo)
        norms[c >> 1][0].append(cat(his, 0))
        norms[c >> 1][1].append(cat(los, 0))
        all_grads[c >> 1][c & 1] = mm(packed, basis_back[:, chunks[c >> 1][c & 1]])
    branch = [
        mm(cat(his + los + his, 1), w_out[768 * k : 768 * (k + 1), :]) for k, (his, los) in enumerate(norms)
    ]
    branch = branch[0] + branch[1]
    slope_skip = slope_skip_ref[...]
    keep = 1.0 - slope_skip
    totals, skips, actives = [], [], []
    for i in range(0, TM, ROWS):
        rows = slice(i, i + ROWS)
        block = mix_ref[rows, :] + (branch[rows, 0:128] + b_out_ref[:, 0:128])
        block_ref[rows, :] = block
        send_ref[rows, 0:128] = block
        total = skip_ref[rows, :] + (branch[rows, 128:256] + b_out_ref[:, 128:256])
        s = sigmoid(total)
        part = keep * s
        mild = slope_skip + part
        rest = total * (1.0 - s)
        totals.append(rest)
        skips.append(mild + part * rest)
        actives.append(split(total * mild))
    a_hi, a_lo = cat([a for a, _ in actives], 0), cat([a for _, a in actives], 0)
    query = cat([a_hi, a_lo, a_hi, ones_block(TM)], 1)

    decoded = [None, None]
    back = [None, None]
    masked, grads_hi, grads_lo = [[], []], [], []
    all_logits = [[mm(query, w_mask[:, chunk]) for chunk in chunks[0]], [None, None]]

    def logits_of(c):
        all_logits[1][c] = mm(query, w_mask[:, chunks[1][c]])

    def decode_of(n, c):
        hi, lo = all_blocks[n][c]
        decoded[c] = plus(decoded[c], mm(cat(hi + lo + hi, 1), decode[n]))

    def back_of(n, c):
        hi, lo = all_blocks[n][2 + c]
        back[c] = plus(back[c], mm(cat(hi + lo, 1), w_mask_t[c, n]))

    all_blocks = [[[[], []] for _ in range(4)] for _ in range(2)]
    for n in range(2):
        if n == 0:
            waiting = [functools.partial(logits_of, c) for c in range(2)]
        else:
            waiting = [functools.partial(f, 0, c) for f in (back_of, decode_of) for c in range(2)]
        every = 2 * (TM // ROWS) // len(waiting)
        logits, grads = all_logits[n], all_grads[n]
        blocks = all_blocks[n]
        for b in range(2):
            col = column(2 * n + b)
            bias_sum = None
            pieces = [[[], []] for _ in range(4)]
            for k, i in enumerate(range(0, TM, ROWS)):
                if (b * (TM // ROWS) + k) % every == 0 and waiting:
                    waiting.pop(0)()
                rows = slice(i, i + ROWS)
                enc = enc_ref[rows, col]
                grad_enc = None
                for c in range(2):
                    mask = 1.0 / (1.0 + jnp.exp2(logits[c][rows, column(b)]))
                    grad = grads[c][rows, column(b)]
                    grad_enc = plus(grad_enc, grad * mask)
                    value = mask * enc
                    for h, part in enumerate(split(value)):
                        pieces[c][h].append(part)
                    grad_logits = grad * value * (1.0 - mask)
                    if c == 0:
                        bias_sum = plus(bias_sum, fold(grad_logits))
                    for h, part in enumerate(split(grad_logits)):
                        pieces[2 + c][h].append(part)
                grad_enc_ref[rows, col] = grad_enc
                send_ref[rows, 256 + (2 * n + b) * 128 : 256 + (2 * n + b + 1) * 128] = grad_enc
            acc_vec[2:3, (2 * n + b) * 128 : (2 * n + b + 1) * 128] += colsum(bias_sum)
            for block, piece in zip(blocks, pieces):
                for h in range(2):
                    block[h].append(cat(piece[h], 0))
        for c in range(2):
            masked[c].append(cat(blocks[c][0] + blocks[c][1], 1))
        grads_hi = grads_hi + blocks[2][0]
        grads_lo = grads_lo + blocks[2][1]
    for c in range(2):
        back_of(1, c)
    for c in range(2):
        decode_of(1, c)
    back = back[0] + back[1]
    own_grads = cat(grads_hi + grads_lo, 1)

    pieces, along, cot_sum, skip_sum = [], None, None, None
    for k, i in enumerate(range(0, TM, ROWS)):
        rows = slice(i, i + ROWS)
        grad_active = back[rows, 0:128] + back[rows, 128:256]
        grad_skip = grad_active * skips[k]
        along = plus(along, fold(grad_active * totals[k]))
        grad_skip_ref[rows, :] = grad_skip
        send_ref[rows, 128:256] = grad_skip
        cot = cot_ref[rows, :]
        cot_sum = plus(cot_sum, fold(cot))
        skip_sum = plus(skip_sum, fold(grad_skip))
        pieces.append(split(cat([cot, grad_skip], 1)))
    acc_small[0:1, :] += colsum(along)
    acc_small[1:2, :] += colsum(cot_sum)
    acc_small[2:3, :] += colsum(skip_sum)
    g_hi, g_lo = cat([p for p, _ in pieces], 0), cat([p for _, p in pieces], 0)
    r_ref[...] = mm(three((g_hi, g_lo), 1), w_out_t[...])

    first_row = iota((8, LANES), 0) == 0
    waves = []
    for c in range(2):
        tail = decoded[c][:, 128:256]
        shifted = pltpu.roll(tail, 1, 0)
        shifted = cat([jnp.where(first_row, carry[c : c + 1, :], shifted[0:8]), shifted[8:]], 0)
        carry[c : c + 1, :] = tail[TM - 1 : TM, :]
        value = decoded[c][:, 0:128] + jnp.where(offset == 0, 0.0, shifted)
        lines = []
        for q in range(TM // 16):
            line = value[q * 16 : (q + 1) * 16] * here
            lines.append(colsum(line[0:8] + line[8:16]))
        waves.append(cat(lines, 1))
    wave_ref[0:1, :] = jnp.where(side == 0, waves[0], waves[1])
    wave_ref[1:2, :] = jnp.where(side == 0, waves[1], waves[0])

    @pl.when(j == 0)
    def _():
        down_ref[:, 0:128] = cot_ref[0:128, :]
        down_ref[:, 128:256] = grad_skip_ref[0:128, :]

    @pl.when(j == last)
    def _():
        up_ref[0:128, 0:128] = cot_ref[TM - 128 : TM, :]
        up_ref[0:128, 128:256] = grad_skip_ref[TM - 128 : TM, :]
        up_ref[128:136, :] = jnp.zeros((8, 256), F32)
        up_ref[128:129, 0:128] = jnp.where(side == 0, carry[0:1, :], carry[1:2, :])
        up_ref[129:130, 0:128] = jnp.where(side == 0, carry[1:2, :], carry[0:1, :])

    own_norms = cat(norms[0][0] + norms[0][1] + norms[0][0], 1)

    def weight_gradients(rows):
        for n in range(2):
            for c in range(2):
                values = masked[c][n]
                acc_basis[c, :, 256 * n : 256 * (n + 1)] += mm_tn(
                    cat([packed[rows]] * 2, 0), cat([values[rows, 0:256], values[rows, 256:512]], 0)
                )
            yield
        acc_mask[...] += mm_tn(
            three((a_hi[rows], a_lo[rows]), 0), two_of((own_grads[rows, 0:512], own_grads[rows, 512:1024]), 0)
        )
        yield
        acc_out[...] += mm_tn(
            cat([own_norms[rows, 256 * k : 256 * (k + 1)] for k in range(3)], 0), two_of((g_hi[rows], g_lo[rows]), 0)
        )
        yield

    for k in range(TM // T):
        rows = slice(k * T, (k + 1) * T)
        begin = start + k * T
        edge2, ahead2 = boundary(ends, begin)
        plain = edge2 >= begin + T + STEP
        entry = 2 * (j * (TM // T) + k)
        hot_b, hot_a = lane_items(ahead2, items)
        onehot[pl.ds(entry, 1), :] = hot_b
        onehot[pl.ds(entry + 1, 1), :] = hot_a
        row_b2, row_a2 = item_rows(ahead2, items)

        @pl.when(plain)
        def _():
            products = weight_gradients(rows)
            inverse = table_ref[1, pl.ds(row_b2, 1), :]
            lines = [[None] * 8, [None] * 8]
            for c in range(4):
                next(products)
                taps = vec(4, c) + vec(5, c) + vec(6, c)
                level = vec(7, c) + vec(3, c) * taps
                sums = [None] * 8
                for i in range(k * T, (k + 1) * T, ROWS):
                    cut = slice(i, i + ROWS)
                    r, normed, pull = r_ref[cut, column(c)], normed_ref[cut, column(c)], pull_ref[cut, column(c)]
                    depth = depth_refs[i // STEP][i % STEP : i % STEP + ROWS, column(c)] - level
                    pull_r, pull_n = pull * r, pull * normed
                    values = (
                        r, r * normed, pull_r, pull, pull_n, pull_r * depth, pull * depth, pull_n * depth,
                    )
                    sums = [plus(s, fold(value)) for s, value in zip(sums, values)]
                sums = [colsum(s) for s in sums]
                if c < 2:
                    acc_vec[0:1, column(c)] += sums[1]
                    acc_vec[1:2, column(c)] += sums[0]
                gain, flat = vec(9, c), vec(2, c) * taps * inverse
                scales = (gain, gain, flat * gain, flat, flat, inverse * gain, inverse, inverse)
                lines[c >> 1] = [plus(line, s * scale) for line, s, scale in zip(lines[c >> 1], sums, scales)]
            for i in range(8):
                entries[i, pl.ds(entry, 1), :] = lines[0][i] + lines[1][i]

        @pl.when(jnp.logical_not(plain))
        def _():
            products = weight_gradients(rows)
            place = iota((ROWS, LANES), 0) + (begin - k * T - edge2)
            inv_b, inv_a = table_ref[1, pl.ds(row_b2, 1), :], table_ref[1, pl.ds(row_a2, 1), :]
            before, behind = [None] * 8, [None] * 8
            for c in range(4):
                next(products)
                sum_r, sum_rn = None, None
                for i in range(k * T, (k + 1) * T, ROWS):
                    cut = slice(i, i + ROWS)
                    offset = place + i
                    after = offset >= 0
                    taps = jnp.where(after & (offset < STEP), 0.0, vec(4, c)) + vec(5, c)
                    taps = taps + jnp.where((offset < 0) & (offset >= -STEP), 0.0, vec(6, c))
                    r, normed = r_ref[cut, column(c)], normed_ref[cut, column(c)]
                    pull = pull_ref[cut, column(c)] * jnp.where(after, inv_a, inv_b)
                    depth = depth_refs[i // STEP][i % STEP : i % STEP + ROWS, column(c)]
                    flat = pull * (vec(2, c) * taps)
                    cross = pull * (depth - vec(7, c) - vec(3, c) * taps)
                    r_normed = r * normed
                    sum_r, sum_rn = plus(sum_r, fold(r)), plus(sum_rn, fold(r_normed))
                    q = r * vec(9, c)
                    values = (
                        q, q * normed, flat * q, flat, flat * normed, cross * q, cross, cross * normed,
                    )
                    before = [plus(s, fold(jnp.where(after, 0.0, value))) for s, value in zip(before, values)]
                    behind = [plus(s, fold(jnp.where(after, value, 0.0))) for s, value in zip(behind, values)]
                if c < 2:
                    acc_vec[0:1, column(c)] += colsum(sum_rn)
                    acc_vec[1:2, column(c)] += colsum(sum_r)
            for i in range(8):
                entries[i, pl.ds(entry, 1), :] = colsum(before[i])
                entries[i, pl.ds(entry + 1, 1), :] = colsum(behind[i])

    @pl.when(j == last)
    def _():
        hot = onehot[...]
        lines = [colsum(hot * jnp.sum(entries[i], axis=1, keepdims=True)) for i in range(8)]
        msg = cat(lines, 0)
        for i in range(msg_ref.shape[0]):
            msg_ref[i] = msg
        for ref, h in ((keep_ref, half), (give_ref, 1 - half)):
            own = pl.ds(pl.multiple_of(h * 128, 128), 128)
            ref[0:128, :] = acc_out[own, 0:128]
            ref[128:256, :] = acc_out[own, 128:256]
            for k in range(2):
                pair = pl.ds(pl.multiple_of(h * 256 + k * 128, 128), 128)
                ref[256 + 128 * k : 384 + 128 * k, :] = acc_mask[:, pair]
            bias = acc_vec[2:3, pl.ds(pl.multiple_of(h * 256, 256), 256)]
            ref[512:520, :] = cat(
                [
                    bias[:, 0:128], bias[:, 128:256], acc_vec[0:1, own], acc_vec[1:2, own],
                    acc_small[0:3, :], jnp.zeros((1, LANES), F32),
                ], 0,
            )
            for k in range(4):
                cut = column(k)
                ref[520 + 16 * k : 536 + 16 * k, :] = (acc_basis[0, 0:16, cut] + acc_basis[0, 32:48, cut]) + (
                    acc_basis[1, 48:64, cut] + acc_basis[1, 80:96, cut]
                )


def back_kernel(
    len_ref, msg_in_ref, depth_ref, r_a_ref, r_b_ref, low_ref, high_ref, hidden_ref, mix_ref, cot_ref,
    vec_ref, table_in_ref, table_mid_ref, w_out_t, own_ref, core_ref, x_ref, far_ref, got_ref, block_in, skip_in, enc_in,
    grad_mix_ref, send_ref, keep_ref, give_ref, edge_ref, block_ref, skip_ref, enc_ref,
    gathered, table, weights, ring, halo, acc_w, acc_vec,
):
    j = pl.program_id(0)
    last = pl.num_programs(0) - 1
    items = len_ref.shape[0]
    me = lax.axis_index("src")
    half = me & 1
    side = me >> 1
    own_rows = last * T

    def vec(row, c):
        return vec_ref[row : row + 1, column(c)]

    ends = item_ends(len_ref)

    @pl.when(j == 0)
    def _():
        for k, ref in enumerate((own_ref, core_ref, x_ref, far_ref)):
            gathered[half ^ k] = ref[...]
        totals = 0.5 * jnp.sum(msg_in_ref[...], axis=0)
        lane = iota((1, LANES), 1)
        number = jnp.zeros((1, LANES), jnp.int32)
        for k in range(items):
            number = jnp.where(lane == k, len_ref[k], number)
        number = jnp.maximum(number.astype(F32) * HIDDEN, 1.0)
        m1 = totals[0:1] / number
        m2 = totals[1:2] / number
        p1 = (totals[2:3] - m1 * totals[3:4] - m2 * totals[4:5]) / number
        p2 = (totals[5:6] - m1 * totals[6:7] - m2 * totals[7:8]) / number
        padded = table.shape[1]
        for i, value in enumerate((m1, m2, p1, p2)):
            table[i] = to_rows(value, padded)
        acc_w[...] = jnp.zeros_like(acc_w)
        acc_vec[...] = jnp.zeros_like(acc_vec)
        edge_ref[...] = low_ref[128:136, 0:128]
        for k, part in enumerate((low_ref[0:128, :], high_ref[...])):
            halo[k] = mm(three(split(part), 1), w_out_t[...])
        for s in range(4):
            cut = column(s)
            hi, lo = split(gathered[s].T)
            for place in (0, 256):
                place = place + (s >> 1) * 512 + (s & 1) * 128
                weights[place : place + 128, 0:128] = hi
                weights[place : place + 128, 128:256] = lo

    block_ref[...] = got_ref[:, 0:128]
    skip_ref[...] = got_ref[:, 128:256]
    enc_ref[...] = got_ref[:, 256:768]

    base = lax.axis_index("tm") * (2 * own_rows) + half * own_rows
    new, old = j & 1, 1 - (j & 1)

    def chooser(begin, alone, edge, ahead):
        row_b, row_a = item_rows(ahead, items)

        def pick(ref, i):
            value_b = ref[i, pl.ds(row_b, 1), :]
            return value_b, value_b if alone else ref[i, pl.ds(row_a, 1), :]

        def choose(pair, i):
            if alone:
                return pair[0]
            return jnp.where(iota((ROWS, LANES), 0) + (begin - edge) + i >= 0, pair[1], pair[0])

        return pick, choose

    begin = base + j * T - STEP
    edge, ahead = boundary(ends, begin)
    alone = edge >= begin + T

    def filter_rows(alone):
        pick, choose = chooser(begin, alone, edge, ahead)
        means, inverses = pick(table_mid_ref, 0), pick(table_mid_ref, 1)
        firsts, seconds = pick(table, 0), pick(table, 1)
        shifts = tuple(-a * b for a, b in zip(means, inverses))
        firsts = tuple(a * b for a, b in zip(firsts, inverses))
        seconds = tuple(a * b for a, b in zip(seconds, inverses))
        for c in range(4):
            slope, gain = vec(8, c), vec(9, c)
            keep = 1.0 - slope
            halves = [None, None]
            for i in range(0, T, ROWS):
                if i < STEP:
                    r = jnp.where(j == 0, halo[0, i : i + ROWS, column(c)], r_a_ref[i : i + ROWS, column(c)])
                else:
                    cut = slice(i - STEP, i - STEP + ROWS)
                    r = jnp.where(j == last, halo[1, cut, column(c)], r_b_ref[cut, column(c)])
                depth = depth_ref[i : i + ROWS, column(c)]
                s = sigmoid(depth)
                u = depth * (1.0 - s)
                part = keep * s
                mild = slope + part
                inv = choose(inverses, i)
                normed = depth * mild * inv + choose(shifts, i)
                grad_act = r * (gain * inv) - choose(firsts, i) - normed * choose(seconds, i)
                if c < 2:
                    halves[i // STEP] = plus(halves[i // STEP], fold(grad_act * u))
                ring[new, i : i + ROWS, column(c)] = grad_act * (mild + part * u)
            if c < 2:
                in_low = jnp.where(j > 0, 1.0, 0.0)
                in_high = jnp.where(j < last, 1.0, 0.0)
                acc_vec[8:9, column(c)] += in_low * colsum(halves[0]) + in_high * colsum(halves[1])

    pl.when(alone)(lambda: filter_rows(True))
    pl.when(jnp.logical_not(alone))(lambda: filter_rows(False))

    start = base + (j - 1) * T
    edge2, ahead2 = boundary(ends, start)
    plain = edge2 >= start + T + STEP

    def norm_rows(plain):
        pick, choose = chooser(start, plain, edge2, ahead2)
        means, inverses = pick(table_in_ref, 0), pick(table_in_ref, 1)
        firsts, seconds = pick(table, 2), pick(table, 3)
        shifts = tuple(-a * b for a, b in zip(means, inverses))
        firsts = tuple(a * b for a, b in zip(firsts, inverses))
        seconds = tuple(a * b for a, b in zip(seconds, inverses))
        rows = iota((ROWS, LANES), 0) + (start - edge2)
        his, los = [[], [], [], []], [[], [], [], []]
        for c in range(4):
            slope, gain, bias = vec(1, c), vec(2, c), vec(3, c)
            keep = 1.0 - slope
            sums = [None] * 8
            for i in range(0, T, ROWS):
                cut = slice(i, i + ROWS)
                grad_low, grad_high = ring[old, cut, column(c)], ring[new, cut, column(c)]
                if i < STEP:
                    grad_mid = ring[old, i + STEP : i + STEP + ROWS, column(c)]
                else:
                    grad_mid = ring[new, i - STEP : i - STEP + ROWS, column(c)]
                if not plain:
                    offset = rows + i
                    grad_low = jnp.where((offset >= 0) & (offset < STEP), 0.0, grad_low)
                    grad_high = jnp.where((offset < 0) & (offset >= -STEP), 0.0, grad_high)
                grad_norm = vec(5, c) * grad_mid + vec(4, c) * grad_high + vec(6, c) * grad_low
                hidden = hidden_ref[cut, column(c)]
                s = sigmoid(hidden)
                u = hidden * (1.0 - s)
                part = keep * s
                mild = slope + part
                inv = choose(inverses, i)
                normed = hidden * mild * inv + choose(shifts, i)
                grad_act = grad_norm * (gain * inv) - choose(firsts, i) - normed * choose(seconds, i)
                grad_hidden = grad_act * (mild + part * u)
                if c < 2:
                    norm = normed * gain + bias
                    values = (
                        grad_hidden, grad_act * u, grad_norm * normed, grad_norm, norm * grad_high, norm * grad_mid,
                        norm * grad_low, grad_mid,
                    )
                    sums = [plus(s, fold(value)) for s, value in zip(sums, values)]
                hi, lo = split(grad_hidden)
                his[c].append(hi)
                los[c].append(lo)
            if c < 2:
                acc_vec[0:8, column(c)] += cat([colsum(s) for s in sums], 0)
        hi, lo = [cat(p, 0) for p in his], [cat(p, 0) for p in los]
        own = mm(cat(hi[0:2] + lo[0:2], 1), weights[0:512, :])
        back = own + mm(cat(hi[2:4] + lo[2:4], 1), weights[512:1024, :])
        grad_mix = cot_ref[...] + (back[:, 0:128] + back[:, 128:256])
        grad_mix_ref[...] = grad_mix
        send_ref[...] = grad_mix
        mixed = cat(split(mix_ref[...]), 1)
        acc_w[...] += mm_tn(cat([cat(hi[0:2], 1), cat(lo[0:2], 1)], 1), mixed)

    pl.when((j > 0) & plain)(lambda: norm_rows(True))
    pl.when((j > 0) & jnp.logical_not(plain))(lambda: norm_rows(False))

    @pl.when(j == last)
    def _():
        for ref, h in ((keep_ref, half), (give_ref, 1 - half)):
            own = pl.ds(pl.multiple_of(h * 128, 128), 128)
            rest = pl.ds(pl.multiple_of(256 + h * 128, 128), 128)
            ref[0:128, :] = (acc_w[own, 0:128] + (acc_w[own, 128:256] + acc_w[rest, 0:128])).T
            ref[128:144, :] = acc_vec[:, own]


def merge_kernel(len_ref, got_ref, mix_in, mine_ref, other_ref, edge_ref, edge_other_ref, mix_ref, wave_ref):
    me = lax.axis_index("src")
    half = me & 1
    mix_ref[...] = got_ref[...]
    width = mine_ref.shape[1]
    frames = width // STRIDE
    base = lax.axis_index("tm") * (2 * frames)
    ends = item_ends(len_ref)
    lane = iota((2, LANES), 1)
    for part, edge, h in ((mine_ref, edge_ref, half), (other_ref, edge_other_ref, 1 - half)):
        place = base + h * frames
        new = place == 0
        for end in ends:
            new = new | (end == place)
        place = pl.multiple_of(h * width, width)
        wave_ref[:, pl.ds(place, width)] = part[...]
        first = part[:, 0:128] + jnp.where((lane < STRIDE) & jnp.logical_not(new), edge[0:2, :], 0.0)
        wave_ref[:, pl.ds(place, LANES)] = first


def total_of(refs):
    values = [ref[...] for ref in refs]
    while len(values) > 1:
        values = [a + b for a, b in zip(values[0::2], values[1::2])]
    return values[0]


def last_kernel(count, early_ref, early_other_ref, *refs):
    lates = refs[:count]
    (
        w_in, b_in, slope_in, gain_in, beta_in, w_depth, b_depth, slope_mid,
    gain_mid, beta_mid, w_out, b_out, slope_skip, w_mask, b_mask, basis,
    ) = refs[count:]
    late = total_of(lates)
    w_in[...] = late[0:128]
    for ref, row in (
        (b_in, 128), (slope_in, 129), (gain_in, 130), (beta_in, 131), (b_depth, 135), (slope_mid, 136),
    ):
        ref[...] = late[row : row + 1]
    w_depth[...] = late[132:135]
    early = early_ref[...] + early_other_ref[...]
    w_out[:, 0:128] = early[0:128]
    w_out[:, 128:256] = early[128:256]
    w_mask[:, 0:128] = early[256:384]
    w_mask[:, 128:256] = early[384:512]
    b_mask[:, 0:128] = early[512:513]
    b_mask[:, 128:256] = early[513:514]
    gain_mid[...] = early[514:515]
    beta_mid[...] = early[515:516]
    slope_skip[...] = early[516:517]
    b_out[:, 0:128] = early[517:518]
    b_out[:, 128:256] = early[518:519]
    for k in range(4):
        basis[:, column(k)] = early[520 + 16 * k : 536 + 16 * k]


def local(
    mix_in, skip_in, encoded, lengths, w_in, b_in, slope_in, gain_in, beta_in, w_depth, b_depth, slope_mid, gain_mid,
    beta_mid, w_out, b_out, slope_skip, w_mask, b_mask, basis, cot_out, cot_wave,
):
    n_tm, n_src = lax.axis_size("tm"), lax.axis_size("src")
    devices = n_tm * n_src
    frames = mix_in.shape[0]
    own_rows = frames // 2
    items = lengths.shape[0]
    padded = -(-items // 8) * 8
    tiles = own_rows // T
    tiles_m = own_rows // TM
    up = [(i, i + 1) for i in range(n_tm - 1)]
    down = [(j, i) for i, j in up]
    swap = [(i, i ^ 1) for i in range(n_src)]
    cross = [(i, i ^ 2) for i in range(n_src)]

    def half():
        return lax.axis_index("src") & 1

    def struct(*shape):
        return jax.ShapeDtypeStruct(shape, F32)

    def whole(*shape):
        zeros = (0,) * len(shape)
        return pl.BlockSpec(shape, lambda i, n: zeros)

    anywhere = pl.BlockSpec(memory_space=pl.ANY)

    def vmem(*shape):
        return pltpu.VMEM(shape, F32)

    def vmem16(*shape):
        return pltpu.VMEM(shape, BF16)

    def call(kernel, name, grid, in_specs, out_specs, out_shape, scratch, us, **kw):
        return pl.pallas_call(
            kernel,
            grid_spec=pltpu.PrefetchScalarGridSpec(
                num_scalar_prefetch=1, grid=(grid,), in_specs=in_specs, out_specs=out_specs, scratch_shapes=scratch
            ),
            out_shape=out_shape,
            compiler_params=pltpu.CompilerParams(
                vmem_limit_bytes=VMEM, dimension_semantics=("arbitrary",)
            ),
            cost_estimate=pl.CostEstimate(flops=0, bytes_accessed=us * 3_600_000, transcendentals=0),
            name=name,
            **kw,
        )

    msg_shape = (devices, 8, LANES)
    message = struct(*msg_shape)
    stat_shape = (devices, 1, LANES) if items <= GROUP else msg_shape
    statistic = struct(*stat_shape)

    def exchange(msg):
        return lax.all_to_all(msg, ("tm", "src"), 0, 0)

    def line(vector):
        return vector.reshape(1, -1)

    def fixed(*shape):
        return pl.BlockSpec(shape, lambda i: (0,) * len(shape))

    n1 = frames // T1
    vectors = (
        line(b_in), line(slope_in), line(gain_in), line(beta_in), w_depth, line(b_depth), line(slope_mid),
        line(gain_mid), line(beta_mid), line(b_mask),
    )
    pack, wide, low, high = pl.pallas_call(
        prep_kernel,
        grid=(1,),
        in_specs=[
            fixed(T, 128), pl.BlockSpec((T, 128), lambda i: (frames // T - 1, 0)), fixed(2, LANES), fixed(128, 128),
            fixed(128, 256), fixed(128, 256), *[fixed(*v.shape) for v in vectors],
        ],
        out_specs=[fixed(PACK_IN, 128), fixed(512, 128), fixed(T + 8, 128), fixed(T, 128)],
        out_shape=[struct(PACK_IN, 128), struct(512, 128), struct(T + 8, 128), struct(T, 128)],
        compiler_params=pltpu.CompilerParams(vmem_limit_bytes=VMEM),
        name="prep",
    )(mix_in, mix_in, cot_wave, w_in, w_out, w_mask, *vectors)
    pack_x = lax.ppermute(pack, "src", cross)
    pack_core = lax.ppermute(pack, "src", swap)
    mix_prev = lax.ppermute(high, "tm", up)
    mix_next = lax.ppermute(low, "tm", down)
    msg1 = call(
        first_kernel, "first", 2,
        [pl.BlockSpec((frames // 2, 128), lambda i, n: (i, 0)), whole(128, 128), whole(1, 128), whole(1, 128)],
        whole(*msg_shape), message,
        [vmem(1, 2 * n1, 128), vmem(1, 2 * n1, 128), vmem(2 * n1, 128), vmem(2 * n1, 128)], 4,
    )(lengths, mix_in, w_in, line(b_in), line(slope_in))
    msg1, pack_x, pack_core, mix_prev, mix_next = lax.optimization_barrier(
        (msg1, pack_x, pack_core, mix_prev, mix_next)
    )
    pack_far = lax.ppermute(pack_x, "src", swap)
    packs = (pack, pack_core, pack_x, pack_far)
    msg1 = exchange(msg1)
    wide_x = lax.ppermute(wide, "src", cross)
    wide_core = lax.ppermute(wide, "src", swap)
    wide_far = lax.ppermute(wide_x, "src", swap)
    wides = (wide, wide_core, wide_x, wide_far)

    entries = -(-2 * (tiles + 1) // 8) * 8
    hidden, depth, msg2, vec, table_in = call(
        depth_kernel, "depth", tiles + 2,
        [
            whole(*msg_shape),
            whole(frames, 128), whole(T, 128), whole(T + 8, 128), *[whole(PACK_IN, 128)] * 4,
        ],
        [
            pl.BlockSpec((T, HIDDEN), lambda i, n: (i, 0)),
            pl.BlockSpec((T, HIDDEN), lambda i, n: (jnp.maximum(i - 1, 0), 0)),
            whole(*stat_shape), whole(NVEC, HIDDEN), whole(2, padded, LANES),
        ],
        [
            struct(own_rows + 2 * T, HIDDEN), struct(own_rows + T, HIDDEN), statistic, struct(NVEC, HIDDEN),
            struct(2, padded, LANES),
        ],
        [
            vmem(4, PACK_IN, 128), vmem16(512, HIDDEN), vmem(2, T, HIDDEN),
            vmem(4, entries, 128), vmem(4, entries, 128), vmem(entries, 128), vmem(entries, 128),
        ], 8,
    )(lengths, msg1, mix_in, mix_prev, mix_next, *packs)
    msg2 = exchange(msg2)

    def half_rows(width):
        return pl.BlockSpec((TM, width), lambda i, n: (half() * tiles_m + i, 0))

    def rows_m(width):
        return pl.BlockSpec((TM, width), lambda i, n: (i, 0))

    def depth_piece(k):
        return pl.BlockSpec((STEP, HIDDEN), lambda i, n: (TM // STEP * i + 1 + k, 0))

    packed = call(
        cotangent_kernel, "cotangent", tiles_m,
        [
            pl.BlockSpec((2, TM * STRIDE), lambda i, n: (0, half() * tiles_m + i)),
            pl.BlockSpec(
                (2, LANES),
                lambda i, n: (0, jnp.minimum((half() * tiles_m + i + 1) * (TM // 16), (2 * tiles_m) * (TM // 16) - 1)),
            ),
            whole(T + 8, 128), anywhere,
        ],
        rows_m(128), jax.ShapeDtypeStruct((own_rows, 128), BF16), [], 6,
    )(lengths, cot_wave, cot_wave, mix_next, vec)
    pieces = TM // STEP
    (block_out, grad_skip, grad_enc, send, wave_half, r, r_up, r_down, keep, give, msg3, table_mid, w_out_t) = call(
        mask_kernel, "mask", tiles_m,
        [
            whole(*stat_shape), *[depth_piece(k) for k in range(pieces)],
            half_rows(128), half_rows(128), half_rows(HIDDEN), half_rows(128),
            rows_m(128), whole(L, HIDDEN), whole(NVEC, HIDDEN), whole(1, 256), whole(1, 128),
            *[whole(512, 128)] * 4,
        ],
        [
            half_rows(128), half_rows(128), half_rows(HIDDEN), rows_m(768),
            pl.BlockSpec((2, TM * STRIDE), lambda i, n: (0, i)),
            rows_m(HIDDEN), whole(136, 256), whole(128, 256), whole(EARLY, 128), whole(EARLY, 128),
            whole(*msg_shape), whole(2, padded, LANES), whole(768, HIDDEN),
        ],
        [
            struct(frames, 128), struct(frames, 128), struct(frames, HIDDEN), struct(own_rows, 768),
            struct(2, own_rows * STRIDE), struct(own_rows, HIDDEN), struct(136, 256), struct(128, 256),
            struct(EARLY, 128), struct(EARLY, 128), message, struct(2, padded, LANES),
            jax.ShapeDtypeStruct((768, HIDDEN), BF16),
        ],
        [
            vmem(4, 512, 128), vmem16(1536, 256),
            vmem16(512, 1024), vmem16(2, 2, 512, 256), vmem16(2, 768, 256), vmem16(128, 1024), vmem(TM, HIDDEN), vmem(TM, HIDDEN), vmem(8, 128), vmem(256, 256), vmem(128, HIDDEN),
            vmem(2, 128, HIDDEN), vmem(8, HIDDEN), vmem(8, 128),
            vmem(8, 2 * tiles, 128), vmem(2 * tiles, 128),
        ], 28,
    )(
        lengths, msg2, *[depth] * pieces, mix_in, skip_in, encoded, cot_out, packed, basis.T, vec,
        line(b_out), line(slope_skip), *wides,
    )

    both = ("tm", "src")
    later, earlier = [], []
    for i in range(n_tm):
        for s in range(n_src):
            here = i * n_src + s
            there = here + 1 if s % 2 == 0 else (i + 1) * n_src + s - 1
            if s % 2 == 0 or i + 1 < n_tm:
                later.append((here, there))
                earlier.append((there, here))
    hops = [[(i, i ^ (1 << bit)) for i in range(n_tm)] for bit in range(n_tm.bit_length() - 1)]
    early = keep + lax.ppermute(give, "src", swap)
    got_low = lax.ppermute(r_up, both, later)
    got_high = lax.ppermute(r_down, both, earlier)
    msg3 = exchange(msg3)
    early, send = lax.optimization_barrier((early, send))
    got = lax.ppermute(send, "src", swap)
    msg3, got_low, got_high, early, got, wave_half = lax.optimization_barrier(
        (msg3, got_low, got_high, early, got, wave_half)
    )
    wave_other = lax.ppermute(wave_half, "src", swap)
    early_other = lax.ppermute(early, "tm", hops[-1])

    def rows(width):
        return pl.BlockSpec((T, width), lambda i, n: (i, 0))

    def own_tile(width):
        return pl.BlockSpec((T, width), lambda i, n: (half() * tiles + jnp.maximum(i - 1, 0), 0))

    def other_rows(width):
        return pl.BlockSpec((T, width), lambda i, n: ((1 - half()) * tiles + jnp.minimum(i, tiles - 1), 0))

    grad_mix, mix_send, keep, give, edge, block_out, grad_skip, grad_enc = call(
        back_kernel, "back", tiles + 1,
        [
            whole(*msg_shape), rows(HIDDEN),
            pl.BlockSpec((STEP, HIDDEN), lambda i, n: (jnp.maximum(2 * i - 1, 0), 0)),
            pl.BlockSpec((STEP, HIDDEN), lambda i, n: (jnp.minimum(2 * i, 2 * tiles - 1), 0)),
            whole(136, 256), whole(128, 256),
            pl.BlockSpec((T, HIDDEN), lambda i, n: (jnp.maximum(i, 1), 0)), own_tile(128), own_tile(128),
            whole(NVEC, HIDDEN), whole(2, padded, LANES), whole(2, padded, LANES), whole(768, HIDDEN),
            *[whole(128, 128)] * 4,
            pl.BlockSpec((T, 768), lambda i, n: (jnp.minimum(i, tiles - 1), 0)), anywhere, anywhere, anywhere,
        ],
        [
            own_tile(128), pl.BlockSpec((T, 128), lambda i, n: (jnp.maximum(i - 1, 0), 0)),
            whole(144, 128), whole(144, 128), whole(8, 128), other_rows(128), other_rows(128), other_rows(HIDDEN),
        ],
        [
            struct(frames, 128), struct(own_rows, 128), struct(144, 128), struct(144, 128), struct(8, 128),
            struct(frames, 128), struct(frames, 128), struct(frames, HIDDEN),
        ],
        [
            vmem(4, 128, 128), vmem(4, padded, LANES), vmem16(1024, 256),
            vmem(2, T, HIDDEN), vmem(2, 128, HIDDEN), vmem(512, 256), vmem(16, HIDDEN),
        ], 13,
        input_output_aliases={19: 5, 20: 6, 21: 7},
    )(
        lengths, msg3, depth, r, r, got_low, got_high, hidden, mix_in, cot_out, vec, table_in, table_mid, w_out_t, *packs, got,
        block_out, grad_skip, grad_enc,
    )

    grad_mix, mix_send, keep, give, edge, early_other, wave_other = lax.optimization_barrier(
        (grad_mix, mix_send, keep, give, edge, early_other, wave_other)
    )
    late_give = lax.ppermute(give, "src", swap)
    early = early + early_other
    early_other = lax.ppermute(early, "tm", hops[0])
    late_give, early = lax.optimization_barrier((late_give, early))
    late = keep + late_give
    late, edge, mix_send = lax.optimization_barrier((late, edge, mix_send))
    lates = [late] + [lax.ppermute(late, "tm", [(i, i ^ (2 * k)) for i in range(n_tm)]) for k in range(1, n_tm // 2)]
    mix_got = lax.ppermute(mix_send, "src", swap)
    edge_other = lax.ppermute(edge, "src", swap)
    wave_width = own_rows * STRIDE
    grad_mix, wave = call(
        merge_kernel, "merge", 1,
        [
            whole(own_rows, 128), anywhere, whole(2, wave_width), whole(2, wave_width), whole(8, 128), whole(8, 128),
        ],
        [pl.BlockSpec((own_rows, 128), lambda i, n: (1 - half(), 0)), whole(2, 2 * wave_width)],
        [struct(frames, 128), struct(2, 2 * wave_width)], [], 3,
        input_output_aliases={2: 0},
    )(lengths, mix_got, grad_mix, wave_half, wave_other, edge, edge_other)
    *lates, grad_mix, wave = lax.optimization_barrier((*lates, grad_mix, wave))
    while len(lates) > 1:
        lates = [a + b for a, b in zip(lates[0::2], lates[1::2])]
    late = lates[0]
    late_other = lax.ppermute(late, "tm", hops[0])
    late, early, early_other = lax.optimization_barrier((late, early, early_other))
    for hop in hops[1:-1]:
        early = early + early_other
        early_other = lax.ppermute(early, "tm", hop)

    lates = [late, late_other]
    parts = (early, early_other, *lates)
    shapes = (
        (128, 128), (1, 128), (1, 128), (1, 128), (1, 128), (3, 128), (1, 128), (1, 128), (1, 128), (1, 128), (128, 256),
        (1, 256), (1, 128), (128, 256), (1, 256), (L, HIDDEN),
    )
    outs = pl.pallas_call(
        functools.partial(last_kernel, len(lates)),
        grid=(1,),
        in_specs=[fixed(*part.shape) for part in parts],
        out_specs=[fixed(*shape) for shape in shapes],
        out_shape=[struct(*shape) for shape in shapes],
        compiler_params=pltpu.CompilerParams(vmem_limit_bytes=VMEM),
        name="last",
    )(*parts)
    outs = [o.reshape(-1) if o.shape[0] == 1 else o for o in outs[:-1]] + [outs[-1].T]
    return (block_out, wave, grad_mix, grad_skip, grad_enc, *outs)


def solution(mesh):
    frames, channels = P("tm", None), P("src")
    in_specs = (
        frames, frames, frames, P(), P(None, "src"), channels, channels, channels, channels, P(None, "src"), channels,
        channels, channels, channels, P("src", None), P(), P(), P(None, "src"), channels, P(), frames, P(None, "tm"),
    )
    out_specs = (
        frames, P(None, "tm"), frames, frames, frames, P(None, "src"), channels, channels, channels, channels,
        P(None, "src"), channels, channels, channels, channels, P("src", None), P(), P(), P(None, "src"), channels,
        P(),
    )
    return jax.shard_map(local, mesh=mesh, in_specs=in_specs, out_specs=out_specs, check_vma=False)
```
